32 devices in a mesh: dp: 8 (over z, core), tensor: 4 (over y, x).
Axes of the slice: x: 2, y: 2, z: 4, core: 2. Of those that a mesh axis runs over, the one named last changes fastest.
Arguments:
- hidden: bfloat16 [32768, 1536], P(('dp', 'tensor')), may hold values from -6 to 6
- norm_gain: float32 [1536], replicated, may hold values from 0.5 to 1.5
- head_weight: bfloat16 [1536, 2, 3072], P('dp', None, 'tensor'), may hold values from -0.15625 to 0.15625
- step_weight: bfloat16 [1536, 48], P('dp', 'tensor'), may hold values from -0.15625 to 0.15625
- map_weight: bfloat16 [1536, 256], P(('dp', 'tensor')), may hold values from -0.15625 to 0.15625
- conv_weight: float32 [4, 3328], replicated, may hold values from -3 to 3
- conv_bias: float32 [3328], replicated, may hold values from -0.5 to 0.5
- step_bias: float32 [48], replicated, may hold values from -6 to -3
- decay_log: float32 [48], replicated, may hold values from -2 to 1
- skip_gain: float32 [48], replicated, may hold values from 0.5 to 1.5
- gate_gain: float32 [3072], replicated, may hold values from 0.5 to 1.5
- out_weight: bfloat16 [1536, 3072], P('dp', 'tensor'), may hold values from -0.109375 to 0.109375
- cotangent: bfloat16 [32768, 1536], P(('dp', 'tensor')), may hold values from -6 to 6
Outputs:
- block_out: bfloat16 [32768, 1536], P(('dp', 'tensor'))
- grad_hidden: float32 [32768, 1536], P(('dp', 'tensor'))
- grad_norm_gain: float32 [1536], replicated
- grad_head_weight: float32 [1536, 2, 3072], P('dp', None, 'tensor')
- grad_step_weight: float32 [1536, 48], P('dp', 'tensor')
- grad_map_weight: float32 [1536, 256], P(('dp', 'tensor'))
- grad_conv_weight: float32 [4, 3328], replicated
- grad_conv_bias: float32 [3328], replicated
- grad_step_bias: float32 [48], replicated
- grad_decay_log: float32 [48], replicated
- grad_skip_gain: float32 [48], replicated
- grad_gate_gain: float32 [3072], replicated
- grad_out_weight: float32 [1536, 3072], P('dp', 'tensor')
The draws below stay inside these ranges and needn't reach their ends.
All inputs are finite; a program needn't handle non-finite values.
Results may differ from the reference program's by a relative error of at most 0.014.
Values may be sent and summed in bfloat16 or wider, within the bound.
No kernel may reach another device: no remote copies, remote signals or barrier semaphores. Data moves between devices by JAX's collectives and lax.ppermute only.
A program may use at most 384 MiB of HBM per device.

```python
import jax
import jax.numpy as jnp
from jax import lax

D = 1536
H = 48
HEAD = 64
NS = 128
KW = 4
BLOCK = 256
LEN = 2048
DI = 3072
TOKENS = 32768


def shard_levels(key, dims, split, least, top_value):
    loudness, own = 1.0, jax.random.fold_in(key, 6)
    for dim, blocks in split:
        heights = jnp.exp(jax.random.uniform(jax.random.fold_in(own, dim), (blocks,), jnp.float32, least / len(split), top_value / len(split)))
        loudness = loudness * jnp.repeat(heights, dims[dim] // blocks).reshape([-1 if axis == dim else 1 for axis in range(len(dims))])
    return loudness


def normal_values(rng, dims, deviation, bound, cuts=(), kind=jnp.bfloat16):
    factor_of = shard_levels(rng, dims, cuts, -0.22, 0.18) if cuts else 1.0
    values = jax.random.normal(rng, dims, jnp.float32) * deviation * factor_of
    return jnp.minimum(jnp.maximum(values, -bound), bound).astype(kind)


def setup_inputs(seed: int = 0) -> dict:
    key_list = jax.random.split(jax.random.key(seed), 14)
    return {
        "hidden": normal_values(key_list[0], (TOKENS, D), 1.0, 6.0, ((0, 32),)),
        "norm_gain": jnp.clip(1.0 + 0.1 * jax.random.normal(key_list[1], (D,), jnp.float32), 0.5, 1.5),
        "head_weight": normal_values(key_list[2], (D, 2, DI), D ** -0.5, 0.15625, ((0, 8), (2, 4))),
        "step_weight": normal_values(key_list[3], (D, H), D ** -0.5, 0.15625, ((0, 8), (1, 4))),
        "map_weight": normal_values(key_list[4], (D, 2 * NS), D ** -0.5, 0.15625, ((0, 32),)),
        "conv_weight": normal_values(key_list[5], (KW, DI + 2 * NS), KW ** -0.5, 3.0, (), jnp.float32),
        "conv_bias": jnp.clip(jax.random.uniform(key_list[6], (DI + 2 * NS,), jnp.float32, -0.5, 0.5), -0.5, 0.5),
        "step_bias": jnp.clip(jax.random.uniform(key_list[7], (H,), jnp.float32, -6.0, -3.0), -6.0, -3.0),
        "decay_log": jnp.clip(jax.random.uniform(key_list[8], (H,), jnp.float32, -2.0, 1.0), -2.0, 1.0),
        "skip_gain": jnp.clip(jax.random.uniform(key_list[9], (H,), jnp.float32, 0.5, 1.5), 0.5, 1.5),
        "gate_gain": jnp.clip(1.0 + 0.1 * jax.random.normal(key_list[10], (DI,), jnp.float32), 0.5, 1.5),
        "out_weight": normal_values(key_list[11], (D, DI), DI ** -0.5, 0.109375, ((0, 8), (1, 4))),
        "cotangent": normal_values(key_list[12], (TOKENS, D), 1.0, 6.0, ((0, 32),)),
    }


EPSILON = 1e-05
PRECISE = lax.Precision.HIGHEST

@jax.custom_vjp
def low(v):
    return lax.optimization_barrier(v.astype(jnp.bfloat16)).astype(jnp.float32)

@jax.custom_vjp
def low_back(v):
    return v

def low_keep(v):
    return (low(v), None)

def low_pass(kept, grad):
    return (grad,)

def back_keep(v):
    return (v, None)

def back_low(kept, grad):
    return (low(grad),)
low.defvjp(low_keep, low_pass)
low_back.defvjp(back_keep, back_low)

def conv_silu(before, weight, bias):
    channels = before.shape[1]
    seqs = before.shape[0] // LEN
    shaped = before.reshape(seqs, LEN, channels)
    padded = jnp.pad(shaped, ((0, 0), (KW - 1, 0), (0, 0)))
    total = bias + weight[0] * padded[:, 0:LEN]
    for shift_by in range(1, KW):
        total = total + weight[shift_by] * padded[:, shift_by:shift_by + LEN]
    return jax.nn.silu(total).reshape(seqs * LEN, channels)

def ssd(values, delta, in_map, out_map, rate, skip):
    seqs, length, heads, width = values.shape
    blocks = length // BLOCK

    def to_blocks(array):
        shaped = array.reshape((seqs, blocks, BLOCK) + array.shape[2:])
        return jnp.moveaxis(shaped, 1, 0)
    causal = jnp.arange(BLOCK)[:, None] >= jnp.arange(BLOCK)[None, :]

    def step(state, block):
        block_x, block_dt, block_b, block_c = block
        decay_sum = jnp.cumsum(block_dt * rate, axis=1)
        scores = jnp.einsum('sqn,skn->sqk', block_c, block_b, precision=PRECISE)
        spread_log = decay_sum[:, :, None, :] - decay_sum[:, None, :, :]
        weights = jnp.exp(jnp.where(causal[None, :, :, None], spread_log, -1e+30))
        weights = weights * scores[:, :, :, None] * block_dt[:, None, :, :]
        within = jnp.einsum('sqkh,skhp->sqhp', weights, block_x, precision=PRECISE)
        across = jnp.exp(decay_sum)[:, :, :, None] * jnp.einsum('sqn,shpn->sqhp', block_c, state, precision=PRECISE)
        to_end = jnp.exp(decay_sum[:, -1:, :] - decay_sum) * block_dt
        carried = jnp.exp(decay_sum[:, -1, :])[:, :, None, None] * state
        state = carried + jnp.einsum('skh,skhp,skn->shpn', to_end, block_x, block_b, precision=PRECISE)
        return (state, within + across + skip[None, None, :, None] * block_x)
    initial = jnp.zeros((seqs, heads, width, in_map.shape[-1]), jnp.float32)
    _, outputs = lax.scan(jax.checkpoint(step), initial, (to_blocks(values), to_blocks(delta), to_blocks(in_map), to_blocks(out_map)))
    return jnp.moveaxis(outputs, 0, 1).reshape(seqs, length, heads, width)

def mixer_tail(mixed, step_raw, gate, step_bias, decay_log, skip_gain):
    rows_all, inner = gate.shape
    heads = inner // HEAD
    seqs = rows_all // LEN
    block_x = mixed[:, :inner].reshape(seqs, LEN, heads, HEAD)
    in_map = mixed[:, inner:inner + NS].reshape(seqs, LEN, NS)
    out_map = mixed[:, inner + NS:].reshape(seqs, LEN, NS)
    delta = jax.nn.softplus(step_raw + step_bias).reshape(seqs, LEN, heads)
    result = ssd(block_x, delta, in_map, out_map, -jnp.exp(decay_log), skip_gain)
    return result.reshape(rows_all, inner) * jax.nn.silu(gate)

def forward(params, rows):
    norm_gain, head_weight, step_weight, map_weight, conv_weight, conv_bias, step_bias, decay_log, skip_gain, gate_gain, out_weight = params
    normed = low(rows * lax.rsqrt(lax.optimization_barrier(jnp.mean(rows * rows, axis=-1, keepdims=True)) + EPSILON) * norm_gain)
    columns = jnp.concatenate([head_weight.reshape(D, 2 * DI), step_weight, map_weight], axis=1)
    projected = low_back(jnp.dot(normed, columns, precision=PRECISE))
    gate = projected[:, :DI]
    before = jnp.concatenate([projected[:, DI:2 * DI], projected[:, 2 * DI + H:]], axis=1)
    mixed = low(conv_silu(before, conv_weight, conv_bias))
    gated = mixer_tail(mixed, projected[:, 2 * DI:2 * DI + H], gate, step_bias, decay_log, skip_gain)
    scaled = low(gated * lax.rsqrt(lax.optimization_barrier(jnp.mean(gated * gated, axis=-1, keepdims=True)) + EPSILON) * gate_gain)
    return rows + jnp.dot(scaled, out_weight.T, precision=PRECISE)

def reference(hidden, norm_gain, head_weight, step_weight, map_weight, conv_weight, conv_bias, step_bias, decay_log, skip_gain, gate_gain, out_weight, cotangent):
    params = tuple((weight_in.astype(jnp.float32) for weight_in in (norm_gain, head_weight, step_weight, map_weight, conv_weight, conv_bias, step_bias, decay_log, skip_gain, gate_gain, out_weight)))

    def one_sequence(totals, block):
        rows, grad_rows = block
        result, pull = jax.vjp(forward, params, rows)
        grads, grad_in = pull(grad_rows)
        return (jax.tree.map(jnp.add, totals, grads), (result.astype(jnp.bfloat16), grad_in))
    zero_grads = jax.tree.map(jnp.zeros_like, params)
    sequences = hidden.astype(jnp.float32).reshape(-1, LEN, D)
    grads_given = cotangent.astype(jnp.float32).reshape(-1, LEN, D)
    totals, (results, grad_rows_all) = lax.scan(one_sequence, zero_grads, (sequences, grads_given))
    grad_norm, grad_head, grad_step, grad_map, grad_conv, grad_cbias, grad_sbias, grad_decay, grad_skip, grad_gate, grad_out = totals
    return (results.reshape(-1, D), grad_rows_all.reshape(-1, D), grad_norm, grad_head, grad_step, grad_map, grad_conv, grad_cbias, grad_sbias, grad_decay, grad_skip, grad_gate, grad_out)
```

```python
import functools
import math

import jax
import jax.numpy as jnp
from jax import lax
from jax.experimental import pallas as pl
from jax.experimental.pallas import tpu as pltpu
from jax.sharding import PartitionSpec as P

D = 1536
H = 48
HEAD = 64
NS = 128
KW = 4
LEN = 2048
DI = 3072
EPSILON = 1e-05

CHUNK = 128
HALO = 16
LANES = 128
LOG2E = math.log2(math.e)
NEG = -1e30
VMEM = 58 * 2**20
F32 = jnp.float32
BF16 = jnp.bfloat16
PRECISE = lax.Precision.HIGHEST
NT = (((1,), (1,)), ((), ()))
TN = (((0,), (0,)), ((), ()))


def dot(a, b, dims=(((1,), (0,)), ((), ())), precision=None):
    return lax.dot_general(a, b, dims, precision=precision, preferred_element_type=F32)


def iota(shape, axis):
    return lax.broadcasted_iota(jnp.int32, shape, axis)


def first_half(shape):
    return iota(shape, len(shape) - 1) < HEAD


def mix(columns, head, rows=CHUNK):
    shape = (rows, LANES)
    left = jnp.broadcast_to(columns[:, head : head + 1], shape)
    right = jnp.broadcast_to(columns[:, head + 1 : head + 2], shape)
    return jnp.where(first_half(shape), left, right)


def mix_row(row, head):
    shape = (1, LANES)
    left = jnp.broadcast_to(row[:, head : head + 1], shape)
    right = jnp.broadcast_to(row[:, head + 1 : head + 2], shape)
    return jnp.where(first_half(shape), left, right)


def halves(block):
    left = first_half(block.shape)
    zero = jnp.zeros_like(block)
    return jnp.where(left, block, zero), jnp.where(left, zero, block)


def shifted(block):
    return [pltpu.roll(block, KW - 1 - tap, 0)[HALO:] if tap < KW - 1 else block[HALO:] for tap in range(KW)]


def conv_total(taps, weight, bias):
    total = bias + weight[KW - 1 : KW] * taps[KW - 1]
    for tap in range(KW - 1):
        total = total + weight[tap : tap + 1] * taps[tap]
    return total


def conv_pull(grad, after, weight):
    rows = grad.shape[0]
    ext = jnp.concatenate([grad, after], axis=0)
    out = weight[KW - 1 : KW] * grad
    for ahead in range(1, KW):
        out = out + weight[KW - 1 - ahead : KW - ahead] * pltpu.roll(ext, rows + 8 - ahead, 0)[:rows]
    return out


def fold(block):
    total = block[0:8]
    for at in range(8, block.shape[0], 8):
        total = total + block[at : at + 8]
    return total


def col_sum(block):
    return jnp.sum(block, axis=0, keepdims=True)


def prep_kernel(heads, n_ref, wm_ref, ws_ref, cw_ref, cb_ref, sb_ref, dl_ref, pre_ref, bc_ref, v_ref, c2_ref, cd_ref, c2t_ref, cdt_ref, wf_ref, ei_ref, tot_ref, c2_s, cd_s):
    rows = bc_ref.shape[0]
    groups = c2_ref.shape[0]
    count = rows // CHUNK
    pre_ref[...] = dot(n_ref[...], wm_ref[...]).astype(BF16)
    for at in range(count):
        for pair in range(2):
            cols = slice(pair * LANES, (pair + 1) * LANES)
            block = pre_ref[at * CHUNK : at * CHUNK + CHUNK + HALO, cols].astype(F32)
            total = conv_total(shifted(block), cw_ref[:, cols], cb_ref[:, cols])
            bc_ref[at * CHUNK : (at + 1) * CHUNK, cols] = (total * jax.nn.sigmoid(total)).astype(BF16)
    rate = -jnp.exp(dl_ref[...]) * LOG2E
    lower = (iota((CHUNK, CHUNK), 0) >= iota((CHUNK, CHUNK), 1)).astype(F32)
    raw = dot(n_ref[HALO:], ws_ref[...])
    totals = []
    for at in range(count):
        here = slice(at * CHUNK, (at + 1) * CHUNK)
        v = raw[here] + sb_ref[...]
        delta = jnp.maximum(v, 0.0) + jnp.log1p(jnp.exp(-jnp.abs(v)))
        log_delta = jnp.where(v < -15.0, v, jnp.log(jnp.maximum(delta, 1e-30)))
        c2 = dot(lower, delta * rate, precision=PRECISE)
        cd = c2 - log_delta * LOG2E
        c2_s[here] = c2
        cd_s[here] = cd
        totals.append(c2[CHUNK - 1 : CHUNK])
        v_t, c2_t, cd_t = v.T, c2.T, cd.T
        for g in range(groups):
            own = slice(g * heads, (g + 1) * heads)
            c2_ref[g, here] = c2[:, own]
            cd_ref[g, here] = cd[:, own]
            v_ref[g, :, here] = v_t[own]
            c2t_ref[g, :, here] = c2_t[own]
            cdt_ref[g, :, here] = cd_t[own]
    before = jnp.zeros_like(totals[0])
    for at in range(count):
        here = slice(at * CHUNK, (at + 1) * CHUNK)
        to_here = jnp.exp2(before + c2_s[here])
        before = before + totals[at]
        for g in range(groups):
            ei_ref[g, here] = to_here[:, g * heads : (g + 1) * heads]
    tot_ref[...] = before
    after = jnp.zeros_like(totals[0])
    for at in range(count - 1, -1, -1):
        here = slice(at * CHUNK, (at + 1) * CHUNK)
        after = after + totals[at]
        to_end = jnp.exp2(after - cd_s[here])
        for g in range(groups):
            wf_ref[g, here] = to_end[:, g * heads : (g + 1) * heads]


def prep(normed, map_w, step_w, conv_w, conv_b, step_b, decay_log, groups, heads):
    rows = normed.shape[0] - HALO
    cols = jax.ShapeDtypeStruct((groups, rows, heads), F32)
    flat = jax.ShapeDtypeStruct((groups, heads, rows), F32)
    return pl.pallas_call(
        functools.partial(prep_kernel, heads),
        out_shape=(
            jax.ShapeDtypeStruct((rows + HALO, 2 * NS), BF16),
            jax.ShapeDtypeStruct((rows, 2 * NS), BF16),
            flat,
            cols,
            cols,
            flat,
            flat,
            cols,
            cols,
            jax.ShapeDtypeStruct((1, LANES), F32),
        ),
        scratch_shapes=[pltpu.VMEM((rows, LANES), F32), pltpu.VMEM((rows, LANES), F32)],
        compiler_params=pltpu.CompilerParams(vmem_limit_bytes=VMEM),
        name="prep",
    )(normed, map_w, step_w, conv_w, conv_b, step_b, decay_log)


def proj_kernel(tile, n_ref, w_ref, cw_ref, cb_ref, bc_ref, wf_ref, pre_ref, x_ref, s_ref, xw_s):
    rows, inner = x_ref.shape
    for at in range(0, inner, tile):
        cols = slice(at, at + tile)
        pre_ref[:, cols] = dot(n_ref[...], w_ref[0, :, cols]).astype(BF16)

        def chunk(k, carry, at=at):
            start = pl.multiple_of(k * CHUNK, CHUNK)
            weights = wf_ref[0, pl.ds(start, CHUNK)]
            for q in range(at // LANES, (at + tile) // LANES):
                lanes = slice(q * LANES, (q + 1) * LANES)
                block = pre_ref[pl.ds(start, CHUNK + HALO), lanes].astype(F32)
                total = conv_total(shifted(block), cw_ref[:, lanes], cb_ref[:, lanes])
                x = (total * jax.nn.sigmoid(total)).astype(BF16)
                x_ref[pl.ds(start, CHUNK), lanes] = x
                xw_s[pl.ds(start, CHUNK), lanes] = (x.astype(F32) * mix(weights, 2 * q)).astype(BF16)
            return carry

        lax.fori_loop(0, rows // CHUNK, chunk, 0)
    s_ref[...] = dot(bc_ref[:, :NS], xw_s[...], TN)


def project(normed, weight, conv_w, conv_b, bc, wf):
    ext = normed.shape[0]
    rows = ext - HALO
    groups, _, inner = weight.shape
    heads = inner // HEAD
    tile = 256 if inner % 256 == 0 else LANES
    return pl.pallas_call(
        functools.partial(proj_kernel, tile),
        grid=(groups,),
        in_specs=[
            pl.BlockSpec((ext, D), lambda g: (0, 0)),
            pl.BlockSpec((1, D, inner), lambda g: (g, 0, 0)),
            pl.BlockSpec((KW, inner), lambda g: (0, g)),
            pl.BlockSpec((1, inner), lambda g: (0, g)),
            pl.BlockSpec((rows, 2 * NS), lambda g: (0, 0)),
            pl.BlockSpec((1, rows, heads), lambda g: (g, 0, 0)),
        ],
        out_specs=[
            pl.BlockSpec((ext, inner), lambda g: (0, g)),
            pl.BlockSpec((rows, inner), lambda g: (0, g)),
            pl.BlockSpec((NS, inner), lambda g: (0, g)),
        ],
        out_shape=(
            jax.ShapeDtypeStruct((ext, groups * inner), BF16),
            jax.ShapeDtypeStruct((rows, groups * inner), BF16),
            jax.ShapeDtypeStruct((NS, groups * inner), F32),
        ),
        scratch_shapes=[pltpu.VMEM((rows, inner), BF16)],
        compiler_params=pltpu.CompilerParams(vmem_limit_bytes=VMEM),
        name="project",
    )(normed, weight, conv_w, conv_b, bc, wf)


def scan_kernel(x_ref, bc_ref, c2_ref, cd_ref, cdt_ref, s0_ref, skip_ref, y_ref, sin_ref, state, ya_s, xw_s):
    rows, inner = x_ref.shape
    heads = inner // HEAD
    causal = iota((CHUNK, CHUNK), 0) >= iota((CHUNK, CHUNK), 1)
    state[...] = s0_ref[...]

    def chunk(k, carry):
        start = pl.multiple_of(k * CHUNK, CHUNK)
        here = pl.ds(start, CHUNK)
        in_map, out_map = bc_ref[here, :NS], bc_ref[here, NS:]
        c2, cd = c2_ref[0, here], cd_ref[0, here]
        cd_t = cdt_ref[0, :, here]
        last = c2[CHUNK - 1 : CHUNK]
        from_start, to_end, whole = jnp.exp2(c2), jnp.exp2(last - cd), jnp.exp2(last)
        held = state[...].astype(BF16)
        sin_ref[k] = held
        ya_s[...] = dot(out_map, held)
        scores = dot(out_map, in_map, NT)
        for q in range(heads // 2):
            lanes = slice(q * LANES, (q + 1) * LANES)
            x = x_ref[here, lanes]
            x32 = x.astype(F32)
            weights = []
            for head in (2 * q, 2 * q + 1):
                spread = c2[:, head : head + 1] - cd_t[head : head + 1]
                weights.append((scores * jnp.exp2(jnp.where(causal, spread, NEG))).astype(BF16))
            within = dot(jnp.concatenate(weights, axis=1), jnp.concatenate(halves(x), axis=0))
            y = within + mix(from_start, 2 * q) * ya_s[:, lanes] + skip_ref[:, lanes] * x32
            y_ref[here, lanes] = y.astype(BF16)
            xw_s[:, lanes] = (x32 * mix(to_end, 2 * q)).astype(BF16)
            state[:, lanes] = state[:, lanes] * mix_row(whole, 2 * q)
        state[...] += dot(in_map, xw_s[...], TN)
        return carry

    lax.fori_loop(0, rows // CHUNK, chunk, 0)


def scan(x, bc, c2, cd, cdt, state, skip):
    rows = x.shape[0]
    groups, _, heads = c2.shape
    inner = heads * HEAD
    count = rows // CHUNK
    return pl.pallas_call(
        scan_kernel,
        grid=(groups,),
        in_specs=[
            pl.BlockSpec((rows, inner), lambda g: (0, g)),
            pl.BlockSpec((rows, 2 * NS), lambda g: (0, 0)),
            pl.BlockSpec((1, rows, heads), lambda g: (g, 0, 0)),
            pl.BlockSpec((1, rows, heads), lambda g: (g, 0, 0)),
            pl.BlockSpec((1, heads, rows), lambda g: (g, 0, 0)),
            pl.BlockSpec((NS, inner), lambda g: (0, g)),
            pl.BlockSpec((1, inner), lambda g: (0, g)),
        ],
        out_specs=[
            pl.BlockSpec((rows, inner), lambda g: (0, g)),
            pl.BlockSpec((count, NS, inner), lambda g: (0, 0, g)),
        ],
        out_shape=(
            jax.ShapeDtypeStruct((rows, groups * inner), BF16),
            jax.ShapeDtypeStruct((count, NS, groups * inner), BF16),
        ),
        scratch_shapes=[
            pltpu.VMEM((NS, inner), F32),
            pltpu.VMEM((CHUNK, inner), F32),
            pltpu.VMEM((CHUNK, inner), BF16),
        ],
        compiler_params=pltpu.CompilerParams(vmem_limit_bytes=VMEM),
        name="scan",
    )(x, bc, c2, cd, cdt, state, skip)


def gate_kernel(y_ref, z_ref, cot_ref, hid_ref, w_ref, gain_ref, bc_ref, ei_ref, sc_ref, out_ref, dy_ref, dz_ref, gg_ref, u_ref, gs_s, ga_s, de_s):
    rows = y_ref.shape[0]
    groups, _, inner = w_ref.shape
    tiles = groups * inner // LANES

    @pl.when(pl.program_id(0) == 0)
    def _():
        gg_ref[...] = jnp.zeros_like(gg_ref)
        u_ref[...] = jnp.zeros_like(u_ref)

    for g in range(groups):
        gs_s[:, g * inner : (g + 1) * inner] = dot(cot_ref[...], w_ref[g])
    for part in range(0, rows, CHUNK):
        here = slice(part, part + CHUNK)

        def measure(c, sums):
            lanes = pl.ds(pl.multiple_of(c * LANES, LANES), LANES)
            z = z_ref[here, lanes].astype(F32)
            gated = y_ref[here, lanes].astype(F32) * (z * jax.nn.sigmoid(z))
            ga_s[here, lanes] = gated
            return sums[0] + gated * gated, sums[1] + gs_s[here, lanes] * gain_ref[:, lanes] * gated

        zero = jnp.zeros((CHUNK, LANES), F32)
        squares, dots = lax.fori_loop(0, tiles, measure, (zero, zero))
        inverse = lax.rsqrt(jnp.sum(squares, axis=1, keepdims=True) / DI + EPSILON)
        pull = inverse * inverse * inverse * (jnp.sum(dots, axis=1, keepdims=True) / DI)
        inverse = jnp.broadcast_to(inverse, (CHUNK, LANES))
        pull = jnp.broadcast_to(pull, (CHUNK, LANES))
        for c in range(tiles):
            lanes = slice(c * LANES, (c + 1) * LANES)
            z = z_ref[here, lanes].astype(F32)
            sig = jax.nn.sigmoid(z)
            gated = ga_s[here, lanes]
            weighted = gs_s[here, lanes]
            unit = gated * inverse
            gain = gain_ref[:, lanes]
            sc_ref[here, lanes] = (unit * gain).astype(BF16)
            gg_ref[:, lanes] += fold(weighted * unit)
            grad = inverse * weighted * gain - gated * pull
            dy = (grad * (z * sig)).astype(BF16)
            dy_ref[here, lanes] = dy
            slope = sig * (1.0 + z * (1.0 - sig))
            dz_ref[here, lanes] = (grad * y_ref[here, lanes].astype(F32) * slope).astype(BF16)
            head = c * (LANES // HEAD)
            decay = mix(ei_ref[head * HEAD // inner, here], head % (inner // HEAD))
            de_s[here, lanes] = (dy.astype(F32) * decay).astype(BF16)
    total = hid_ref[...].astype(F32)
    for g in range(groups):
        cols = slice(g * inner, (g + 1) * inner)
        total = total + dot(sc_ref[:, cols], w_ref[g], NT)
        u_ref[:, cols] += dot(bc_ref[:, NS:], de_s[:, cols], TN)
    out_ref[...] = total.astype(BF16)


def gate(y, z, cot, hidden, weight, gain, bc, ei):
    rows = y.shape[0]
    groups, _, inner = weight.shape
    heads = inner // HEAD
    tile = 256
    wide = groups * inner
    row = lambda i: (i, 0)
    fixed = lambda i: (0, 0)
    return pl.pallas_call(
        gate_kernel,
        grid=(rows // tile,),
        in_specs=[
            pl.BlockSpec((tile, wide), row),
            pl.BlockSpec((tile, wide), row),
            pl.BlockSpec((tile, D), row),
            pl.BlockSpec((tile, D), row),
            pl.BlockSpec((groups, D, inner), lambda i: (0, 0, 0), pipeline_mode=pl.Buffered(1)),
            pl.BlockSpec((1, wide), fixed),
            pl.BlockSpec((tile, 2 * NS), row),
            pl.BlockSpec((groups, tile, heads), lambda i: (0, i, 0)),
        ],
        out_specs=[
            pl.BlockSpec((tile, wide), row),
            pl.BlockSpec((tile, D), row),
            pl.BlockSpec((tile, wide), row),
            pl.BlockSpec((tile, wide), row),
            pl.BlockSpec((8, wide), fixed),
            pl.BlockSpec((NS, wide), fixed),
        ],
        out_shape=(
            jax.ShapeDtypeStruct((rows, wide), BF16),
            jax.ShapeDtypeStruct((rows, D), BF16),
            jax.ShapeDtypeStruct((rows, wide), BF16),
            jax.ShapeDtypeStruct((rows, wide), BF16),
            jax.ShapeDtypeStruct((8, wide), F32),
            jax.ShapeDtypeStruct((NS, wide), F32),
        ),
        scratch_shapes=[
            pltpu.VMEM((tile, wide), F32),
            pltpu.VMEM((tile, wide), F32),
            pltpu.VMEM((tile, wide), BF16),
        ],
        compiler_params=pltpu.CompilerParams(vmem_limit_bytes=VMEM),
        name="gate",
    )(y, z, cot, hidden, weight, gain, bc, ei)


def back_kernel(pre_ref, dy_ref, bc_ref, c2_ref, cd_ref, c2t_ref, sin_ref, u_ref, skip_ref, cw_ref, cb_ref, dpre_ref, dbc_ref, acc_ref, q_ref, da_ref, state, next_s, x_s, slope_s, de_s, xw_s, ya_s, bs_s):
    rows, inner = dy_ref.shape
    heads = inner // HEAD
    count = rows // CHUNK
    square = (CHUNK, CHUNK)
    flipped = iota(square, 1) >= iota(square, 0)
    later = (iota(square, 0) >= iota(square, 1)).astype(F32)
    earlier = (iota(square, 0) < iota(square, 1)).astype(F32)
    state[...] = u_ref[...]
    next_s[...] = jnp.zeros_like(next_s)
    acc_ref[...] = jnp.zeros_like(acc_ref)

    @pl.when(pl.program_id(0) == 0)
    def _():
        dbc_ref[...] = jnp.zeros_like(dbc_ref)

    def chunk(step, carry):
        k = count - 1 - step
        start = pl.multiple_of(k * CHUNK, CHUNK)
        here = pl.ds(start, CHUNK)
        in_map, out_map = bc_ref[here, :NS], bc_ref[here, NS:]
        c2, cd = c2_ref[0, here], cd_ref[0, here]
        c2_t = c2t_ref[0, :, here]
        last = c2[CHUNK - 1 : CHUNK]
        from_start, to_end, whole = jnp.exp2(c2), jnp.exp2(last - cd), jnp.exp2(last)
        for q in range(heads // 2):
            lanes = slice(q * LANES, (q + 1) * LANES)
            block = pre_ref[pl.ds(start, CHUNK + HALO), lanes].astype(F32)
            total = conv_total(shifted(block), cw_ref[:, lanes], cb_ref[:, lanes])
            sig = jax.nn.sigmoid(total)
            x = (total * sig).astype(BF16)
            x_s[:, lanes] = x
            slope_s[:, lanes] = sig * (1.0 + total * (1.0 - sig))
            de_s[:, lanes] = (dy_ref[here, lanes].astype(F32) * mix(from_start, 2 * q)).astype(BF16)
            xw_s[:, lanes] = (x.astype(F32) * mix(to_end, 2 * q)).astype(BF16)
        held = sin_ref[k]
        after = state[...]
        after_low = after.astype(BF16)
        ya_s[...] = dot(out_map, held)
        bs_s[...] = dot(in_map, after_low)
        grad_out = dot(de_s[...], held, NT)
        grad_in = dot(xw_s[...], after_low, NT)
        through = col_sum(after * held.astype(F32))
        state[...] = dot(out_map, de_s[...], TN)
        scores = dot(in_map, out_map, NT)
        grad_scores = jnp.zeros(square, F32)
        rc_rows, st_rows, q_rows, tails = [], [], [], []
        for q in range(heads // 2):
            lanes = slice(q * LANES, (q + 1) * LANES)
            x, dy = x_s[:, lanes], dy_ref[here, lanes]
            x_parts, dy_parts = halves(x), halves(dy)
            weights, row_sums = [], []
            for side, head in enumerate((2 * q, 2 * q + 1)):
                spread = c2_t[head : head + 1] - cd[:, head : head + 1]
                decay = jnp.exp2(jnp.where(flipped, spread, NEG))
                weight = (scores * decay).astype(BF16)
                weights.append(weight)
                grad_weight = dot(x_parts[side], dy, NT)
                grad_scores = grad_scores + grad_weight * decay
                row_sums.append(col_sum(weight.astype(F32) * grad_weight))
            dx_in = dot(jnp.concatenate(weights, axis=1), jnp.concatenate(dy_parts, axis=0))
            dx_out = bs_s[:, lanes] * mix(to_end, 2 * q)
            x32, dy32 = x.astype(F32), dy.astype(F32)
            inside = x32 * dx_in
            outside = x32 * dx_out
            crossed = (de_s[:, lanes].astype(F32) * ya_s[:, lanes] - inside).T
            outside_t = outside.T
            both_t = (inside + outside).T
            through_q = through[:, lanes] * mix_row(whole, 2 * q)
            for side in range(2):
                part = slice(side * HEAD, (side + 1) * HEAD)
                rc_rows.append(row_sums[side] + col_sum(crossed[part]))
                st_rows.append(col_sum(outside_t[part]))
                q_rows.append(col_sum(both_t[part]))
                own = first_half((1, LANES)) if side == 0 else ~first_half((1, LANES))
                tails.append(jnp.sum(jnp.where(own, through_q, 0.0), axis=1, keepdims=True))
            state[:, lanes] += after[:, lanes] * mix_row(whole, 2 * q)
            grad = (dx_in + dx_out + skip_ref[:, lanes] * dy32) * slope_s[:, lanes]
            taps = shifted(pre_ref[pl.ds(start, CHUNK + HALO), lanes].astype(F32))
            for tap in range(KW):
                acc_ref[tap * 8 : tap * 8 + 8, lanes] += fold(grad * taps[tap])
            acc_ref[32:40, lanes] += fold(grad)
            acc_ref[40:48, lanes] += fold(dy32 * x32)
            dpre = conv_pull(grad, next_s[:, lanes], cw_ref[:, lanes])
            dpre_ref[pl.ds(pl.multiple_of(start + HALO, HALO), CHUNK), lanes] = dpre.astype(BF16)
            next_s[:, lanes] = grad[0:8]
        low_scores = grad_scores.astype(BF16)
        dbc_ref[here, :NS] += grad_in + dot(low_scores, out_map)
        dbc_ref[here, NS:] += grad_out + dot(low_scores, in_map, TN)
        da = dot(jnp.concatenate(rc_rows, axis=0), later, precision=PRECISE)
        da = da + dot(jnp.concatenate(st_rows, axis=0), earlier, precision=PRECISE)
        da_ref[0, :, here] = da + jnp.concatenate(tails, axis=0)
        q_ref[0, :, here] = jnp.concatenate(q_rows, axis=0)
        return carry

    lax.fori_loop(0, count, chunk, 0)
    for q in range(heads // 2):
        lanes = slice(q * LANES, (q + 1) * LANES)
        empty = jnp.zeros((HALO, LANES), F32)
        dpre_ref[0:HALO, lanes] = conv_pull(empty, next_s[:, lanes], cw_ref[:, lanes]).astype(BF16)


def back(pre, dy, bc, c2, cd, c2t, states, pull, skip, conv_w, conv_b):
    ext = pre.shape[0]
    rows = ext - HALO
    groups, _, heads = c2.shape
    inner = heads * HEAD
    wide = groups * inner
    count = rows // CHUNK
    return pl.pallas_call(
        back_kernel,
        grid=(groups,),
        in_specs=[
            pl.BlockSpec((ext, inner), lambda g: (0, g)),
            pl.BlockSpec((rows, inner), lambda g: (0, g)),
            pl.BlockSpec((rows, 2 * NS), lambda g: (0, 0)),
            pl.BlockSpec((1, rows, heads), lambda g: (g, 0, 0)),
            pl.BlockSpec((1, rows, heads), lambda g: (g, 0, 0)),
            pl.BlockSpec((1, heads, rows), lambda g: (g, 0, 0)),
            pl.BlockSpec((count, NS, inner), lambda g: (0, 0, g)),
            pl.BlockSpec((NS, inner), lambda g: (0, g)),
            pl.BlockSpec((1, inner), lambda g: (0, g)),
            pl.BlockSpec((KW, inner), lambda g: (0, g)),
            pl.BlockSpec((1, inner), lambda g: (0, g)),
        ],
        out_specs=[
            pl.BlockSpec((ext, inner), lambda g: (0, g)),
            pl.BlockSpec((rows, 2 * NS), lambda g: (0, 0)),
            pl.BlockSpec((48, inner), lambda g: (0, g)),
            pl.BlockSpec((1, heads, rows), lambda g: (g, 0, 0)),
            pl.BlockSpec((1, heads, rows), lambda g: (g, 0, 0)),
        ],
        out_shape=(
            jax.ShapeDtypeStruct((ext, wide), BF16),
            jax.ShapeDtypeStruct((rows, 2 * NS), F32),
            jax.ShapeDtypeStruct((48, wide), F32),
            jax.ShapeDtypeStruct((groups, heads, rows), F32),
            jax.ShapeDtypeStruct((groups, heads, rows), F32),
        ),
        scratch_shapes=[
            pltpu.VMEM((NS, inner), F32),
            pltpu.VMEM((8, inner), F32),
            pltpu.VMEM((CHUNK, inner), BF16),
            pltpu.VMEM((CHUNK, inner), F32),
            pltpu.VMEM((CHUNK, inner), BF16),
            pltpu.VMEM((CHUNK, inner), BF16),
            pltpu.VMEM((CHUNK, inner), F32),
            pltpu.VMEM((CHUNK, inner), F32),
        ],
        compiler_params=pltpu.CompilerParams(vmem_limit_bytes=VMEM),
        name="back",
    )(pre, dy, bc, c2, cd, c2t, states, pull, skip, conv_w, conv_b)


def map_back_kernel(pre_ref, grad_ref, cw_ref, cb_ref, dpre_ref, acc_ref, next_s):
    rows, wide = grad_ref.shape
    count = rows // CHUNK
    next_s[...] = jnp.zeros_like(next_s)
    acc_ref[...] = jnp.zeros_like(acc_ref)
    for k in range(count - 1, -1, -1):
        start = k * CHUNK
        for q in range(wide // LANES):
            lanes = slice(q * LANES, (q + 1) * LANES)
            taps = shifted(pre_ref[start : start + CHUNK + HALO, lanes].astype(F32))
            total = conv_total(taps, cw_ref[:, lanes], cb_ref[:, lanes])
            sig = jax.nn.sigmoid(total)
            grad = grad_ref[start : start + CHUNK, lanes] * (sig * (1.0 + total * (1.0 - sig)))
            for tap in range(KW):
                acc_ref[tap * 8 : tap * 8 + 8, lanes] += fold(grad * taps[tap])
            acc_ref[32:40, lanes] += fold(grad)
            dpre = conv_pull(grad, next_s[:, lanes], cw_ref[:, lanes])
            dpre_ref[start + HALO : start + HALO + CHUNK, lanes] = dpre.astype(BF16)
            next_s[:, lanes] = grad[0:8]
    for q in range(wide // LANES):
        lanes = slice(q * LANES, (q + 1) * LANES)
        empty = jnp.zeros((HALO, LANES), F32)
        dpre_ref[0:HALO, lanes] = conv_pull(empty, next_s[:, lanes], cw_ref[:, lanes]).astype(BF16)


def map_back(pre, grad, conv_w, conv_b):
    return pl.pallas_call(
        map_back_kernel,
        out_shape=(jax.ShapeDtypeStruct(pre.shape, BF16), jax.ShapeDtypeStruct((40, pre.shape[1]), F32)),
        scratch_shapes=[pltpu.VMEM((8, pre.shape[1]), F32)],
        compiler_params=pltpu.CompilerParams(vmem_limit_bytes=VMEM),
        name="map_back",
    )(pre, grad, conv_w, conv_b)


def shards(
    tp,
    hidden,
    norm_gain,
    head_weight,
    step_weight,
    map_weight,
    conv_weight,
    conv_bias,
    step_bias,
    decay_log,
    skip_gain,
    gate_gain,
    out_weight,
    cotangent,
):
    rows = hidden.shape[0]
    inner = head_weight.shape[2]
    heads = step_weight.shape[1]
    span = LEN // rows
    forward = [(i, i + 1) for i in range(tp - 1) if (i + 1) % span]
    backward = [(j, i) for i, j in forward]

    halo = lax.ppermute(hidden[rows - HALO :], "tensor", forward)
    everything = ("tensor", "dp")
    gather = lambda part: lax.all_gather(part, everything, axis=0, tiled=True)
    map_full = lax.all_gather(map_weight, ("dp", "tensor"), axis=0, tiled=True)
    step_full = gather(step_weight).reshape(tp, D, heads)
    x_full = gather(head_weight[:, 1]).reshape(tp, D, inner)
    z_full = gather(head_weight[:, 0]).reshape(tp, D, inner)
    out_full = gather(out_weight).reshape(tp, D, inner)

    tokens = jnp.concatenate([halo, hidden], axis=0).astype(F32)
    inverse_ext = lax.rsqrt(jnp.mean(tokens * tokens, axis=-1, keepdims=True) + EPSILON)
    normed_ext = (tokens * inverse_ext * norm_gain).astype(BF16)
    normed = normed_ext[HALO:]

    lane_pad = lambda a: jnp.pad(a, ((0, 0), (0, LANES - H)))
    step_flat = jnp.moveaxis(step_full, 0, 1).reshape(D, H)
    conv_x, bias_x = conv_weight[:, :DI], conv_bias[None, :DI]
    conv_m, bias_m = conv_weight[:, DI:], conv_bias[None, DI:]
    pre_m, bc, v, c2, cd, c2t, cdt, wf, ei, total = prep(
        normed_ext, map_full, lane_pad(step_flat), conv_m, bias_m, lane_pad(step_bias[None]), lane_pad(decay_log[None]), tp, heads
    )
    skip = jnp.repeat(skip_gain, HEAD)[None]
    device_decay = jnp.repeat(jnp.exp2(total[0, :H]), HEAD)[None]

    pre, x, local_state = project(normed_ext, x_full, conv_x, bias_x, bc, wf)
    state = jnp.zeros_like(local_state)
    for _ in range(span - 1):
        state = lax.ppermute(local_state + device_decay * state, "tensor", forward)
    y, states = scan(x, bc, c2, cd, cdt, state, skip)
    z = jnp.einsum("rd,gdi->rgi", normed, z_full, preferred_element_type=F32).astype(BF16).reshape(rows, DI)

    scaled, block_out, dy, dz, gain_sums, local_pull = gate(y, z, cotangent, hidden, out_full, gate_gain[None], bc, ei)
    pull = jnp.zeros_like(local_pull)
    for _ in range(span - 1):
        pull = lax.ppermute(local_pull + device_decay * pull, "tensor", backward)

    def weight_grad(left, right):
        whole = jnp.einsum("rd,rgi->gdi", left, right.reshape(right.shape[0], tp, inner), preferred_element_type=F32)
        whole = whole.astype(BF16).reshape(tp * D, inner)
        return lax.psum_scatter(whole, everything, scatter_dimension=0, tiled=True).astype(F32)

    grad_out = weight_grad(cotangent, scaled)
    grad_z = weight_grad(normed, dz)
    dpre, dbc, sums, q, da = back(pre, dy, bc, c2, cd, c2t, states, pull, skip, conv_x, bias_x)
    dpre_m, sums_m = map_back(pre_m, dbc, conv_m, bias_m)
    grad_x = weight_grad(normed_ext, dpre)

    v, q, da = (a.reshape(H, rows) for a in (v, q, da))
    delta, sig = jax.nn.softplus(v), jax.nn.sigmoid(v)
    rate = -jnp.exp(decay_log)[:, None]
    ratio = jnp.where(v < -15.0, 1.0, sig / jnp.maximum(delta, 1e-30))
    dstep = q * ratio + da * rate * sig
    dstep_low = dstep.astype(BF16)
    grad_step_bias = jnp.sum(dstep, axis=1)
    grad_decay = jnp.sum(da * delta, axis=1) * rate[:, 0]
    grad_skip = jnp.sum(sums[40:48].reshape(8, H, HEAD), axis=(0, 2))
    grad_gain = jnp.sum(gain_sums, axis=0)
    taps = jnp.concatenate([sums[:32], sums_m[:32]], axis=1).reshape(KW, 8, -1).sum(1)
    taps_bias = jnp.concatenate([sums[32:40], sums_m[32:40]], axis=1).sum(0)

    grad_map = dot(normed_ext, dpre_m, TN)
    grad_step = lax.dot_general(normed, dstep_low, (((0,), (1,)), ((), ())), preferred_element_type=F32)
    map_shard = lax.psum_scatter(grad_map, ("dp", "tensor"), scatter_dimension=0, tiled=True)
    grad_step = jnp.moveaxis(grad_step.reshape(D, tp, heads), 1, 0).reshape(tp * D, heads)
    step_shard = lax.psum_scatter(grad_step, everything, scatter_dimension=0, tiled=True)

    dn = jnp.einsum("rgi,gdi->rd", dpre.reshape(-1, tp, inner), x_full, preferred_element_type=F32)
    dn = dn + dot(dpre_m, map_full, NT)
    dn_halo, dn = dn[:HALO], dn[HALO:]
    dn = dn + jnp.einsum("rgi,gdi->rd", dz.reshape(-1, tp, inner), z_full, preferred_element_type=F32)
    dn = dn + lax.dot_general(dstep_low, step_flat, (((0,), (1,)), ((), ())), preferred_element_type=F32)
    dn_next = lax.ppermute(dn_halo, "tensor", backward)
    dn = dn + jnp.pad(dn_next, ((rows - HALO, 0), (0, 0)))

    tokens, inverse = tokens[HALO:], inverse_ext[HALO:]
    scaled_in = dn * norm_gain
    grad_hidden = (
        cotangent.astype(F32)
        + inverse * scaled_in
        - tokens * inverse**3 * jnp.mean(scaled_in * tokens, axis=-1, keepdims=True)
    )
    grad_norm = jnp.sum(dn * tokens * inverse, axis=0)
    flat = jnp.concatenate([grad_norm, taps.reshape(-1), taps_bias, grad_step_bias, grad_decay, grad_skip, grad_gain])
    flat = lax.psum(flat, ("dp", "tensor"))
    wide = DI + 2 * NS
    cuts = [D, KW * wide, wide, H, H, H, DI]
    parts, at = [], 0
    for size in cuts:
        parts.append(flat[at : at + size])
        at += size
    grad_head = jnp.stack([grad_z, grad_x], axis=1)
    return (
        block_out,
        grad_hidden,
        parts[0],
        grad_head,
        step_shard,
        map_shard,
        parts[1].reshape(KW, wide),
        parts[2],
        parts[3],
        parts[4],
        parts[5],
        parts[6],
        grad_out,
    )


def solution(mesh):
    both = ("dp", "tensor")
    placed = (
        P(both, None),
        P(),
        P("dp", None, "tensor"),
        P("dp", "tensor"),
        P(both, None),
        P(),
        P(),
        P(),
        P(),
        P(),
        P(),
        P("dp", "tensor"),
        P(both, None),
    )
    outs = (
        P(both, None),
        P(both, None),
        P(),
        P("dp", None, "tensor"),
        P("dp", "tensor"),
        P(both, None),
        P(),
        P(),
        P(),
        P(),
        P(),
        P(),
        P("dp", "tensor"),
    )
    return jax.shard_map(
        functools.partial(shards, mesh.shape["tensor"]), mesh=mesh, in_specs=placed, out_specs=outs, check_vma=False
    )
```

```python
import functools
import math

import jax
import jax.numpy as jnp
from jax import lax
from jax.experimental import pallas as pl
from jax.experimental.pallas import tpu as pltpu
from jax.sharding import Mesh
from jax.sharding import PartitionSpec as P

D = 1536
H = 48
HEAD = 64
NS = 128
KW = 4
LEN = 2048
DI = 3072
EPSILON = 1e-05

CHUNK = 128
HALO = 16
TAIL = 112
LANES = 128
LOG2E = math.log2(math.e)
NEG = -1e30
VMEM = 58 * 2**20
F32 = jnp.float32
BF16 = jnp.bfloat16
PRECISE = lax.Precision.HIGHEST
NT = (((1,), (1,)), ((), ()))
TN = (((0,), (0,)), ((), ()))


def dot(a, b, dims=(((1,), (0,)), ((), ())), precision=None):
    return lax.dot_general(a, b, dims, precision=precision, preferred_element_type=F32)


def iota(shape, axis):
    return lax.broadcasted_iota(jnp.int32, shape, axis)


def first_half(shape):
    return iota(shape, len(shape) - 1) < HEAD


def mix(columns, head, rows=CHUNK):
    shape = (rows, LANES)
    left = jnp.broadcast_to(columns[:, head : head + 1], shape)
    right = jnp.broadcast_to(columns[:, head + 1 : head + 2], shape)
    return jnp.where(first_half(shape), left, right)


def mix_row(row, head):
    shape = (1, LANES)
    left = jnp.broadcast_to(row[:, head : head + 1], shape)
    right = jnp.broadcast_to(row[:, head + 1 : head + 2], shape)
    return jnp.where(first_half(shape), left, right)


def halves(block):
    left = first_half(block.shape)
    zero = jnp.zeros_like(block)
    return jnp.where(left, block, zero), jnp.where(left, zero, block)


def shifted(block):
    return [pltpu.roll(block, KW - 1 - tap, 0)[HALO:] if tap < KW - 1 else block[HALO:] for tap in range(KW)]


def conv_total(taps, weight, bias):
    total = bias + weight[KW - 1 : KW] * taps[KW - 1]
    for tap in range(KW - 1):
        total = total + weight[tap : tap + 1] * taps[tap]
    return total


def conv_pull(grad, after, weight):
    rows = grad.shape[0]
    ext = jnp.concatenate([grad, after], axis=0)
    out = weight[KW - 1 : KW] * grad
    for ahead in range(1, KW):
        out = out + weight[KW - 1 - ahead : KW - ahead] * pltpu.roll(ext, rows + 8 - ahead, 0)[:rows]
    return out


def fold(block):
    total = block[0:8]
    for at in range(8, block.shape[0], 8):
        total = total + block[at : at + 8]
    return total


def col_sum(block):
    return jnp.sum(block, axis=0, keepdims=True)


def cost(us):
    return pl.CostEstimate(flops=0, bytes_accessed=int(us), transcendentals=0)


def times(left_ref, blocks):
    total, at = None, 0
    for block in blocks:
        term = dot(left_ref[:, at : at + block.shape[0]], block[...])
        total = term if total is None else total + term
        at += block.shape[0]
    return total


def split(refs, counts):
    out, at = [], 0
    for count in counts:
        out.append(refs[at : at + count])
        at += count
    return out


def place_spec(place):
    array, index = place
    return pl.BlockSpec((D // 2, array.shape[1]), lambda *_: (index, 0), pipeline_mode=pl.Buffered(1))


def whole_spec(array):
    return pl.BlockSpec(array.shape, lambda *_: (0,) * array.ndim, pipeline_mode=pl.Buffered(1))


def prep_kernel(heads, pitch, n_ref, wm_ref, ws_ref, cw_ref, cb_ref, sb_ref, dl_ref, pre_ref, bc_ref, v_ref, c2_ref, cd_ref, c2t_ref, cdt_ref, wf_ref, ei_ref, tot_ref, c2_s, cd_s):
    rows = bc_ref.shape[0]
    groups = c2_ref.shape[0]
    count = rows // CHUNK
    pre_ref[...] = dot(n_ref[...], wm_ref[...]).astype(BF16)
    for at in range(count):
        for pair in range(2):
            cols = slice(pair * LANES, (pair + 1) * LANES)
            block = pre_ref[at * CHUNK : at * CHUNK + CHUNK + HALO, cols].astype(F32)
            total = conv_total(shifted(block), cw_ref[:, cols], cb_ref[:, cols])
            bc_ref[at * CHUNK : (at + 1) * CHUNK, cols] = (total * jax.nn.sigmoid(total)).astype(BF16)
    rate = -jnp.exp(dl_ref[...]) * LOG2E
    lower = (iota((CHUNK, CHUNK), 0) >= iota((CHUNK, CHUNK), 1)).astype(F32)
    raw = dot(n_ref[HALO:], ws_ref[...], NT)
    totals = []
    for at in range(count):
        here = slice(at * CHUNK, (at + 1) * CHUNK)
        v = raw[here] + sb_ref[...]
        delta = jnp.maximum(v, 0.0) + jnp.log1p(jnp.exp(-jnp.abs(v)))
        log_delta = jnp.where(v < -15.0, v, jnp.log(jnp.maximum(delta, 1e-30)))
        c2 = dot(lower, delta * rate, precision=PRECISE)
        cd = c2 - log_delta * LOG2E
        c2_s[here] = c2
        cd_s[here] = cd
        totals.append(c2[CHUNK - 1 : CHUNK])
        v_t, c2_t, cd_t = v.T, c2.T, cd.T
        for g in range(groups):
            own = slice(g * pitch, g * pitch + heads)
            c2_ref[g, here] = c2[:, own]
            cd_ref[g, here] = cd[:, own]
            v_ref[g, :, here] = v_t[own]
            c2t_ref[g, :, here] = c2_t[own]
            cdt_ref[g, :, here] = cd_t[own]
    before = jnp.zeros_like(totals[0])
    for at in range(count):
        here = slice(at * CHUNK, (at + 1) * CHUNK)
        to_here = jnp.exp2(before + c2_s[here])
        before = before + totals[at]
        for g in range(groups):
            ei_ref[g, here] = to_here[:, g * pitch : g * pitch + heads]
    tot_ref[...] = before
    after = jnp.zeros_like(totals[0])
    for at in range(count - 1, -1, -1):
        here = slice(at * CHUNK, (at + 1) * CHUNK)
        after = after + totals[at]
        to_end = jnp.exp2(after - cd_s[here])
        for g in range(groups):
            wf_ref[g, here] = to_end[:, g * pitch : g * pitch + heads]


def prep(normed, map_w, step_w, conv_w, conv_b, step_b, decay_log, groups, heads, pitch):
    rows = normed.shape[0] - HALO - TAIL
    cols = jax.ShapeDtypeStruct((groups, rows, heads), F32)
    flat = jax.ShapeDtypeStruct((groups, heads, rows), F32)
    return pl.pallas_call(
        functools.partial(prep_kernel, heads, pitch),
        out_shape=(
            jax.ShapeDtypeStruct((rows + HALO, 2 * NS), BF16),
            jax.ShapeDtypeStruct((rows, 2 * NS), BF16),
            flat,
            cols,
            cols,
            flat,
            flat,
            cols,
            cols,
            jax.ShapeDtypeStruct((1, LANES), F32),
        ),
        grid=(1,),
        in_specs=[pl.BlockSpec((rows + HALO, D), lambda i: (0, 0))]
        + [whole_spec(a) for a in (map_w, step_w, conv_w, conv_b, step_b, decay_log)],
        scratch_shapes=[pltpu.VMEM((rows, LANES), F32), pltpu.VMEM((rows, LANES), F32)],
        compiler_params=pltpu.CompilerParams(vmem_limit_bytes=VMEM),
        cost_estimate=cost(11),
        name="prep",
    )(normed, map_w, step_w, conv_w, conv_b, step_b, decay_log)


def proj_kernel(tile, count, n_ref, *refs):
    blocks = refs[:count]
    cw_ref, cb_ref, bc_ref, wf_ref, pre_ref, x_ref, s_ref, xw_s = refs[count:]
    rows, inner = x_ref.shape
    for at in range(0, inner, tile):
        cols = slice(at, at + tile)
        pre_ref[:, cols] = times(n_ref, [block.at[:, cols] for block in blocks]).astype(BF16)

        def chunk(k, carry, at=at):
            start = pl.multiple_of(k * CHUNK, CHUNK)
            weights = wf_ref[0, pl.ds(start, CHUNK)]
            for q in range(at // LANES, (at + tile) // LANES):
                lanes = slice(q * LANES, (q + 1) * LANES)
                block = pre_ref[pl.ds(start, CHUNK + HALO), lanes].astype(F32)
                total = conv_total(shifted(block), cw_ref[:, lanes], cb_ref[:, lanes])
                x = (total * jax.nn.sigmoid(total)).astype(BF16)
                x_ref[pl.ds(start, CHUNK), lanes] = x
                xw_s[pl.ds(start, CHUNK), lanes] = (x.astype(F32) * mix(weights, 2 * q)).astype(BF16)
            return carry

        lax.fori_loop(0, rows // CHUNK, chunk, 0)
    s_ref[...] = dot(bc_ref[:, :NS], xw_s[...], TN).astype(BF16)


def project(g, normed, blocks, conv_w, conv_b, bc, wf):
    rows = normed.shape[0] - HALO - TAIL
    ext = rows + HALO
    inner = blocks[0][0].shape[1]
    heads = inner // HEAD
    tile = 256 if inner % 256 == 0 else LANES
    return pl.pallas_call(
        functools.partial(proj_kernel, tile, len(blocks)),
        grid=(1,),
        in_specs=[
            pl.BlockSpec((ext, D), lambda i: (0, 0)),
            *map(place_spec, blocks),
            pl.BlockSpec((KW, inner), lambda i: (0, g)),
            pl.BlockSpec((1, inner), lambda i: (0, g)),
            whole_spec(bc),
            pl.BlockSpec((1, rows, heads), lambda i: (g, 0, 0)),
        ],
        out_specs=[
            pl.BlockSpec((ext, inner), lambda i: (0, 0)),
            pl.BlockSpec((rows, inner), lambda i: (0, 0)),
            pl.BlockSpec((NS, inner), lambda i: (0, 0)),
        ],
        out_shape=(
            jax.ShapeDtypeStruct((ext, inner), BF16),
            jax.ShapeDtypeStruct((rows, inner), BF16),
            jax.ShapeDtypeStruct((NS, inner), BF16),
        ),
        scratch_shapes=[pltpu.VMEM((rows, inner), BF16)],
        compiler_params=pltpu.CompilerParams(vmem_limit_bytes=VMEM),
        cost_estimate=cost(10),
        name="project",
    )(normed, *(array for array, _ in blocks), conv_w, conv_b, bc, wf)


def product_kernel(count, n_ref, *refs):
    refs[count][...] = times(n_ref, refs[:count]).astype(BF16)


def product(left, blocks):
    rows = left.shape[0]
    inner = blocks[0][0].shape[1]
    tile = 256 if inner % 256 == 0 else LANES
    return pl.pallas_call(
        functools.partial(product_kernel, len(blocks)),
        grid=(inner // tile,),
        in_specs=[whole_spec(left), *(pl.BlockSpec((D // 2, tile), functools.partial(lambda index, j: (index, j), index)) for _, index in blocks)],
        out_specs=pl.BlockSpec((rows, tile), lambda j: (0, j)),
        out_shape=jax.ShapeDtypeStruct((rows, inner), BF16),
        compiler_params=pltpu.CompilerParams(vmem_limit_bytes=VMEM),
        cost_estimate=cost(4),
        name="product",
    )(left, *(array for array, _ in blocks))


def scan_kernel(x_ref, bc_ref, c2_ref, cd_ref, cdt_ref, s0_ref, skip_ref, y_ref, sin_ref, state, ya_s, xw_s):
    rows, inner = x_ref.shape
    heads = inner // HEAD
    causal = iota((CHUNK, CHUNK), 0) >= iota((CHUNK, CHUNK), 1)
    state[...] = s0_ref[...].astype(F32)

    def chunk(k, carry):
        start = pl.multiple_of(k * CHUNK, CHUNK)
        here = pl.ds(start, CHUNK)
        in_map, out_map = bc_ref[here, :NS], bc_ref[here, NS:]
        c2, cd = c2_ref[0, here], cd_ref[0, here]
        cd_t = cdt_ref[0, :, here]
        last = c2[CHUNK - 1 : CHUNK]
        from_start, to_end, whole = jnp.exp2(c2), jnp.exp2(last - cd), jnp.exp2(last)
        held = state[...].astype(BF16)
        sin_ref[k] = held
        ya_s[...] = dot(out_map, held)
        scores = dot(out_map, in_map, NT)
        for q in range(heads // 2):
            lanes = slice(q * LANES, (q + 1) * LANES)
            x = x_ref[here, lanes]
            x32 = x.astype(F32)
            weights = []
            for head in (2 * q, 2 * q + 1):
                spread = c2[:, head : head + 1] - cd_t[head : head + 1]
                weights.append((scores * jnp.exp2(jnp.where(causal, spread, NEG))).astype(BF16))
            within = dot(jnp.concatenate(weights, axis=1), jnp.concatenate(halves(x), axis=0))
            y = within + mix(from_start, 2 * q) * ya_s[:, lanes] + skip_ref[:, lanes] * x32
            y_ref[here, lanes] = y.astype(BF16)
            xw_s[:, lanes] = (x32 * mix(to_end, 2 * q)).astype(BF16)
            state[:, lanes] = state[:, lanes] * mix_row(whole, 2 * q)
        state[...] += dot(in_map, xw_s[...], TN)
        return carry

    lax.fori_loop(0, rows // CHUNK, chunk, 0)


def scan(g, x, bc, c2, cd, cdt, state, skip):
    rows = x.shape[0]
    heads = c2.shape[2]
    inner = heads * HEAD
    count = rows // CHUNK
    return pl.pallas_call(
        scan_kernel,
        grid=(1,),
        in_specs=[
            whole_spec(x),
            whole_spec(bc),
            pl.BlockSpec((1, rows, heads), lambda i: (g, 0, 0)),
            pl.BlockSpec((1, rows, heads), lambda i: (g, 0, 0)),
            pl.BlockSpec((1, heads, rows), lambda i: (g, 0, 0)),
            whole_spec(state),
            pl.BlockSpec((1, inner), lambda i: (0, g)),
        ],
        out_specs=[
            pl.BlockSpec((rows, inner), lambda i: (0, 0)),
            pl.BlockSpec((count, NS, inner), lambda i: (0, 0, 0)),
        ],
        out_shape=(
            jax.ShapeDtypeStruct((rows, inner), BF16),
            jax.ShapeDtypeStruct((count, NS, inner), BF16),
        ),
        scratch_shapes=[
            pltpu.VMEM((NS, inner), F32),
            pltpu.VMEM((CHUNK, inner), F32),
            pltpu.VMEM((CHUNK, inner), BF16),
        ],
        compiler_params=pltpu.CompilerParams(vmem_limit_bytes=VMEM),
        cost_estimate=cost(9),
        name="scan",
    )(x, bc, c2, cd, cdt, state, skip)


def gate_kernel(groups, width, out_counts, z_counts, *refs):
    ys, zs, outs_w, zs_w, rest, scs, dys, dzs, us, tail = split(
        refs, (groups, groups, sum(out_counts), sum(z_counts), 6, groups, groups, groups, groups, 8)
    )
    outs_w, zs_w = split(outs_w, out_counts), split(zs_w, z_counts)
    cot_ref, hid_ref, gain_ref, bc_ref, ei_ref, flag_ref = rest
    out_ref, dn_ref, gg_ref, gs_s, ga_s, de_s, sum_s, u_s = tail
    rows, inner = ys[0].shape
    tiles = inner // LANES

    @pl.when(pl.program_id(0) == 0)
    def _():
        gg_ref[...] = jnp.zeros_like(gg_ref)
        u_s[...] = jnp.zeros_like(u_s)

    for g in range(groups):
        gs_s[:, g * inner : (g + 1) * inner] = times(cot_ref, outs_w[g])
    for part in range(0, rows, CHUNK):
        here = slice(part, part + CHUNK)
        squares = jnp.zeros((CHUNK, LANES), F32)
        dots = jnp.zeros((CHUNK, LANES), F32)
        for g in range(groups):

            def measure(c, sums, g=g):
                lanes = pl.ds(pl.multiple_of(c * LANES, LANES), LANES)
                wide = pl.ds(pl.multiple_of(g * inner + c * LANES, LANES), LANES)
                z = zs[g][here, lanes].astype(F32)
                gated = ys[g][here, lanes].astype(F32) * (z * jax.nn.sigmoid(z))
                ga_s[here, wide] = gated
                return sums[0] + gated * gated, sums[1] + gs_s[here, wide] * gain_ref[:, wide] * gated

            squares, dots = lax.fori_loop(0, tiles, measure, (squares, dots))
        inverse = lax.rsqrt(jnp.sum(squares, axis=1, keepdims=True) / DI + EPSILON)
        pull = inverse * inverse * inverse * (jnp.sum(dots, axis=1, keepdims=True) / DI)
        inverse = jnp.broadcast_to(inverse, (CHUNK, LANES))
        pull = jnp.broadcast_to(pull, (CHUNK, LANES))
        for g in range(groups):
            for c in range(tiles):
                lanes = slice(c * LANES, (c + 1) * LANES)
                wide = slice(g * inner + c * LANES, g * inner + (c + 1) * LANES)
                z = zs[g][here, lanes].astype(F32)
                sig = jax.nn.sigmoid(z)
                gated = ga_s[here, wide]
                weighted = gs_s[here, wide]
                unit = gated * inverse
                gain = gain_ref[:, wide]
                scs[g][here, lanes] = (unit * gain).astype(BF16)
                gg_ref[:, wide] += fold(weighted * unit)
                grad = inverse * weighted * gain - gated * pull
                dy = (grad * (z * sig)).astype(BF16)
                dys[g][here, lanes] = dy
                slope = sig * (1.0 + z * (1.0 - sig))
                dzs[g][here, lanes] = (grad * ys[g][here, lanes].astype(F32) * slope).astype(BF16)
                de_s[here, wide] = (dy.astype(F32) * mix(ei_ref[g, here], 2 * c)).astype(BF16)
    for g in range(groups):
        cols = slice(g * inner, (g + 1) * inner)
        u_s[:, cols] += dot(bc_ref[:, NS:], de_s[:, cols], TN)
        us[g][...] = u_s[:, cols].astype(BF16)
    back_times(sum_s, scs, outs_w, hid_ref)
    natural(out_ref, sum_s, flag_ref, width)
    back_times(dn_ref, dzs, zs_w, None)


def natural(out_ref, source_ref, flag_ref, width):
    first = flag_ref[0:1, 0:1] == 0.0
    half = source_ref.shape[1] // 2
    for z in range(half // width):
        own = source_ref[:, z * width : (z + 1) * width]
        other = source_ref[:, half + z * width : half + (z + 1) * width]
        pair = jnp.concatenate([jnp.where(first, own, other), jnp.where(first, other, own)], axis=1)
        out_ref[:, 2 * z * width : 2 * (z + 1) * width] = pair.astype(out_ref.dtype)


def back_times(out_ref, lefts, weights, base_ref):
    cuts = sorted({0} | {sum(b.shape[0] for b in blocks[: i + 1]) for blocks in weights for i in range(len(blocks))})
    for low, high in zip(cuts[:-1], cuts[1:]):
        total = None if base_ref is None else base_ref[:, low:high].astype(F32)
        for left, blocks in zip(lefts, weights):
            at = 0
            for block in blocks:
                if at <= low < at + block.shape[0]:
                    term = dot(left[...], block[low - at : high - at], NT)
                    total = term if total is None else total + term
                at += block.shape[0]
        out_ref[:, low:high] = total.astype(out_ref.dtype)


def arrays(places):
    return [array for array, _ in flat(places)]


def flat(lists):
    return [item for items in lists for item in items]


def gate(ys, zs, outs_w, zs_w, cot, hidden, gain, bc, ei, flag, width):
    groups = len(ys)
    rows, inner = ys[0].shape
    heads = inner // HEAD
    tile = 256
    wide = groups * inner
    row = lambda i: (i, 0)
    fixed = lambda i: (0, 0)
    group = [pl.BlockSpec((tile, inner), row)] * groups
    group_shape = [jax.ShapeDtypeStruct((rows, inner), BF16)] * groups
    out = pl.pallas_call(
        functools.partial(gate_kernel, groups, width, tuple(map(len, outs_w)), tuple(map(len, zs_w))),
        grid=(rows // tile,),
        in_specs=[
            *group,
            *group,
            *map(place_spec, flat(outs_w)),
            *map(place_spec, flat(zs_w)),
            pl.BlockSpec((tile, D), row),
            pl.BlockSpec((tile, D), row),
            pl.BlockSpec((1, wide), fixed),
            pl.BlockSpec((tile, 2 * NS), row),
            pl.BlockSpec((groups, tile, heads), lambda i: (0, i, 0)),
            whole_spec(flag),
        ],
        out_specs=[
            *group,
            *group,
            *group,
            *[pl.BlockSpec((NS, inner), fixed)] * groups,
            pl.BlockSpec((tile, D), row),
            pl.BlockSpec((tile, D), row),
            pl.BlockSpec((8, wide), fixed),
        ],
        out_shape=(
            *group_shape,
            *group_shape,
            *group_shape,
            *[jax.ShapeDtypeStruct((NS, inner), BF16)] * groups,
            jax.ShapeDtypeStruct((rows, D), BF16),
            jax.ShapeDtypeStruct((rows, D), F32),
            jax.ShapeDtypeStruct((8, wide), F32),
        ),
        scratch_shapes=[
            pltpu.VMEM((tile, wide), F32),
            pltpu.VMEM((tile, wide), F32),
            pltpu.VMEM((tile, wide), BF16),
            pltpu.VMEM((tile, D), F32),
            pltpu.VMEM((NS, wide), F32),
        ],
        compiler_params=pltpu.CompilerParams(vmem_limit_bytes=VMEM),
        cost_estimate=cost(55),
        name="gate",
    )(*ys, *zs, *arrays(outs_w), *arrays(zs_w), cot, hidden, gain, bc, ei, flag)
    return split(out, (groups, groups, groups, groups)) + list(out[4 * groups :])


def back_kernel(pre_ref, dy_ref, bc_ref, c2_ref, cd_ref, c2t_ref, sin_ref, u_ref, skip_ref, cw_ref, cb_ref, dpre_ref, dbc_ref, acc_ref, q_ref, da_ref, state, next_s, x_s, slope_s, de_s, xw_s, ya_s, bs_s):
    rows, inner = dy_ref.shape
    heads = inner // HEAD
    count = rows // CHUNK
    square = (CHUNK, CHUNK)
    flipped = iota(square, 1) >= iota(square, 0)
    later = (iota(square, 0) >= iota(square, 1)).astype(F32)
    earlier = (iota(square, 0) < iota(square, 1)).astype(F32)
    state[...] = u_ref[...].astype(F32)
    next_s[...] = jnp.zeros_like(next_s)
    acc_ref[...] = jnp.zeros_like(acc_ref)

    def chunk(step, carry):
        k = count - 1 - step
        start = pl.multiple_of(k * CHUNK, CHUNK)
        here = pl.ds(start, CHUNK)
        in_map, out_map = bc_ref[here, :NS], bc_ref[here, NS:]
        c2, cd = c2_ref[0, here], cd_ref[0, here]
        c2_t = c2t_ref[0, :, here]
        last = c2[CHUNK - 1 : CHUNK]
        from_start, to_end, whole = jnp.exp2(c2), jnp.exp2(last - cd), jnp.exp2(last)
        for q in range(heads // 2):
            lanes = slice(q * LANES, (q + 1) * LANES)
            block = pre_ref[pl.ds(start, CHUNK + HALO), lanes].astype(F32)
            total = conv_total(shifted(block), cw_ref[:, lanes], cb_ref[:, lanes])
            sig = jax.nn.sigmoid(total)
            x = (total * sig).astype(BF16)
            x_s[:, lanes] = x
            slope_s[:, lanes] = sig * (1.0 + total * (1.0 - sig))
            de_s[:, lanes] = (dy_ref[here, lanes].astype(F32) * mix(from_start, 2 * q)).astype(BF16)
            xw_s[:, lanes] = (x.astype(F32) * mix(to_end, 2 * q)).astype(BF16)
        held = sin_ref[k]
        after = state[...]
        after_low = after.astype(BF16)
        ya_s[...] = dot(out_map, held)
        bs_s[...] = dot(in_map, after_low)
        grad_out = dot(de_s[...], held, NT)
        grad_in = dot(xw_s[...], after_low, NT)
        through = col_sum(after * held.astype(F32))
        state[...] = dot(out_map, de_s[...], TN)
        scores = dot(in_map, out_map, NT)
        grad_scores = jnp.zeros(square, F32)
        rc_rows, st_rows, q_rows, tails = [], [], [], []
        for q in range(heads // 2):
            lanes = slice(q * LANES, (q + 1) * LANES)
            x, dy = x_s[:, lanes], dy_ref[here, lanes]
            x_parts, dy_parts = halves(x), halves(dy)
            weights, row_sums = [], []
            for side, head in enumerate((2 * q, 2 * q + 1)):
                spread = c2_t[head : head + 1] - cd[:, head : head + 1]
                decay = jnp.exp2(jnp.where(flipped, spread, NEG))
                weight = (scores * decay).astype(BF16)
                weights.append(weight)
                grad_weight = dot(x_parts[side], dy, NT)
                grad_scores = grad_scores + grad_weight * decay
                row_sums.append(col_sum(weight.astype(F32) * grad_weight))
            dx_in = dot(jnp.concatenate(weights, axis=1), jnp.concatenate(dy_parts, axis=0))
            dx_out = bs_s[:, lanes] * mix(to_end, 2 * q)
            x32, dy32 = x.astype(F32), dy.astype(F32)
            inside = x32 * dx_in
            outside = x32 * dx_out
            crossed = (de_s[:, lanes].astype(F32) * ya_s[:, lanes] - inside).T
            outside_t = outside.T
            both_t = (inside + outside).T
            through_q = through[:, lanes] * mix_row(whole, 2 * q)
            for side in range(2):
                part = slice(side * HEAD, (side + 1) * HEAD)
                rc_rows.append(row_sums[side] + col_sum(crossed[part]))
                st_rows.append(col_sum(outside_t[part]))
                q_rows.append(col_sum(both_t[part]))
                own = first_half((1, LANES)) if side == 0 else ~first_half((1, LANES))
                tails.append(jnp.sum(jnp.where(own, through_q, 0.0), axis=1, keepdims=True))
            state[:, lanes] += after[:, lanes] * mix_row(whole, 2 * q)
            grad = (dx_in + dx_out + skip_ref[:, lanes] * dy32) * slope_s[:, lanes]
            taps = shifted(pre_ref[pl.ds(start, CHUNK + HALO), lanes].astype(F32))
            for tap in range(KW):
                acc_ref[tap * 8 : tap * 8 + 8, lanes] += fold(grad * taps[tap])
            acc_ref[32:40, lanes] += fold(grad)
            acc_ref[40:48, lanes] += fold(dy32 * x32)
            dpre = conv_pull(grad, next_s[:, lanes], cw_ref[:, lanes])
            dpre_ref[pl.ds(pl.multiple_of(start + HALO, HALO), CHUNK), lanes] = dpre.astype(BF16)
            next_s[:, lanes] = grad[0:8]
        low_scores = grad_scores.astype(BF16)
        dbc_ref[here, :NS] = grad_in + dot(low_scores, out_map)
        dbc_ref[here, NS:] = grad_out + dot(low_scores, in_map, TN)
        da = dot(jnp.concatenate(rc_rows, axis=0), later, precision=PRECISE)
        da = da + dot(jnp.concatenate(st_rows, axis=0), earlier, precision=PRECISE)
        da_ref[0, :, here] = da + jnp.concatenate(tails, axis=0)
        q_ref[0, :, here] = jnp.concatenate(q_rows, axis=0)
        return carry

    lax.fori_loop(0, count, chunk, 0)
    for q in range(heads // 2):
        lanes = slice(q * LANES, (q + 1) * LANES)
        empty = jnp.zeros((HALO, LANES), F32)
        dpre_ref[0:HALO, lanes] = conv_pull(empty, next_s[:, lanes], cw_ref[:, lanes]).astype(BF16)
    dpre_ref[HALO + rows :] = jnp.zeros((TAIL, inner), BF16)


def back(g, pre, dy, bc, c2, cd, c2t, states, pull, skip, conv_w, conv_b):
    ext = pre.shape[0]
    rows = ext - HALO
    heads = c2.shape[2]
    inner = heads * HEAD
    count = rows // CHUNK
    return pl.pallas_call(
        back_kernel,
        grid=(1,),
        in_specs=[
            whole_spec(pre),
            whole_spec(dy),
            whole_spec(bc),
            pl.BlockSpec((1, rows, heads), lambda i: (g, 0, 0)),
            pl.BlockSpec((1, rows, heads), lambda i: (g, 0, 0)),
            pl.BlockSpec((1, heads, rows), lambda i: (g, 0, 0)),
            whole_spec(states),
            whole_spec(pull),
            pl.BlockSpec((1, inner), lambda i: (0, g)),
            pl.BlockSpec((KW, inner), lambda i: (0, g)),
            pl.BlockSpec((1, inner), lambda i: (0, g)),
        ],
        out_specs=[
            pl.BlockSpec((ext + TAIL, inner), lambda i: (0, 0)),
            pl.BlockSpec((rows, 2 * NS), lambda i: (0, 0)),
            pl.BlockSpec((48, inner), lambda i: (0, 0)),
            pl.BlockSpec((1, heads, rows), lambda i: (0, 0, 0)),
            pl.BlockSpec((1, heads, rows), lambda i: (0, 0, 0)),
        ],
        out_shape=(
            jax.ShapeDtypeStruct((ext + TAIL, inner), BF16),
            jax.ShapeDtypeStruct((rows, 2 * NS), F32),
            jax.ShapeDtypeStruct((48, inner), F32),
            jax.ShapeDtypeStruct((1, heads, rows), F32),
            jax.ShapeDtypeStruct((1, heads, rows), F32),
        ),
        scratch_shapes=[
            pltpu.VMEM((NS, inner), F32),
            pltpu.VMEM((8, inner), F32),
            pltpu.VMEM((CHUNK, inner), BF16),
            pltpu.VMEM((CHUNK, inner), F32),
            pltpu.VMEM((CHUNK, inner), BF16),
            pltpu.VMEM((CHUNK, inner), BF16),
            pltpu.VMEM((CHUNK, inner), F32),
            pltpu.VMEM((CHUNK, inner), F32),
        ],
        compiler_params=pltpu.CompilerParams(vmem_limit_bytes=VMEM),
        cost_estimate=cost(18),
        name="back",
    )(pre, dy, bc, c2, cd, c2t, states, pull, skip, conv_w, conv_b)


def map_back_kernel(pre_ref, grad_ref, cw_ref, cb_ref, dpre_ref, acc_ref, next_s):
    rows, wide = grad_ref.shape
    count = rows // CHUNK
    next_s[...] = jnp.zeros_like(next_s)
    acc_ref[...] = jnp.zeros_like(acc_ref)
    for k in range(count - 1, -1, -1):
        start = k * CHUNK
        for q in range(wide // LANES):
            lanes = slice(q * LANES, (q + 1) * LANES)
            taps = shifted(pre_ref[start : start + CHUNK + HALO, lanes].astype(F32))
            total = conv_total(taps, cw_ref[:, lanes], cb_ref[:, lanes])
            sig = jax.nn.sigmoid(total)
            grad = grad_ref[start : start + CHUNK, lanes] * (sig * (1.0 + total * (1.0 - sig)))
            for tap in range(KW):
                acc_ref[tap * 8 : tap * 8 + 8, lanes] += fold(grad * taps[tap])
            acc_ref[32:40, lanes] += fold(grad)
            dpre = conv_pull(grad, next_s[:, lanes], cw_ref[:, lanes])
            dpre_ref[start + HALO : start + HALO + CHUNK, lanes] = dpre.astype(BF16)
            next_s[:, lanes] = grad[0:8]
    for q in range(wide // LANES):
        lanes = slice(q * LANES, (q + 1) * LANES)
        empty = jnp.zeros((HALO, LANES), F32)
        dpre_ref[0:HALO, lanes] = conv_pull(empty, next_s[:, lanes], cw_ref[:, lanes]).astype(BF16)
    dpre_ref[HALO + rows :] = jnp.zeros((TAIL, wide), BF16)


def map_back(pre, grad, conv_w, conv_b):
    return pl.pallas_call(
        map_back_kernel,
        out_shape=(jax.ShapeDtypeStruct((pre.shape[0] + TAIL, pre.shape[1]), BF16), jax.ShapeDtypeStruct((40, pre.shape[1]), F32)),
        scratch_shapes=[pltpu.VMEM((8, pre.shape[1]), F32)],
        compiler_params=pltpu.CompilerParams(vmem_limit_bytes=VMEM),
        cost_estimate=cost(4),
        name="map_back",
    )(pre, grad, conv_w, conv_b)


def final_kernel(groups, width, counts, *refs):
    ds, ws, rest = split(refs, (groups, sum(counts), 15))
    ws = split(ws, counts)
    dm_ref, wm_ref, dt_ref, wt_ref, halo_ref, dn_ref, hid_ref, cot_ref, gain_ref, flag_ref, gh_ref, gn_ref, left_s, total_s, grad_s = rest
    rows, wide = hid_ref.shape
    inner = ds[0].shape[1]
    start = pl.multiple_of(pl.program_id(0) * rows, HALO)

    @pl.when(pl.program_id(0) == 0)
    def _():
        gn_ref[...] = jnp.zeros_like(gn_ref)

    own = pl.ds(pl.multiple_of(start + HALO, HALO), rows)
    for g in range(groups):
        left_s[:, g * inner : (g + 1) * inner] = ds[g][own]
    left_s[:, groups * inner :] = dm_ref[own]

    @pl.when(pl.program_id(0) == pl.num_programs(0) - 1)
    def _():
        last = slice(rows - HALO, rows)
        left_s[last] = (left_s[last].astype(F32) + halo_ref[...].astype(F32)).astype(BF16)

    lefts = [left_s.at[:, g * inner : (g + 1) * inner] for g in range(groups)]
    lefts += [left_s.at[:, groups * inner :]]
    back_times(total_s, lefts, ws + [[wm_ref]], dn_ref)
    total_s[...] += dot(dt_ref[...], wt_ref[...])
    squares = jnp.zeros((rows, 1), F32)
    for c in range(wide // LANES):
        lanes = slice(c * LANES, (c + 1) * LANES)
        tokens = hid_ref[:, lanes].astype(F32)
        squares = squares + jnp.sum(tokens * tokens, axis=1, keepdims=True)
    inverse = lax.rsqrt(squares / wide + EPSILON)
    dots = jnp.zeros((rows, 1), F32)
    for c in range(wide // LANES):
        lanes = slice(c * LANES, (c + 1) * LANES)
        tokens = hid_ref[:, lanes].astype(F32)
        dots = dots + jnp.sum(total_s[:, lanes] * gain_ref[:, lanes] * tokens, axis=1, keepdims=True)
    pull = inverse * inverse * inverse * (dots / wide)
    for c in range(wide // LANES):
        lanes = slice(c * LANES, (c + 1) * LANES)
        tokens = hid_ref[:, lanes].astype(F32)
        grad = total_s[:, lanes]
        grad_s[:, lanes] = cot_ref[:, lanes].astype(F32) + inverse * (grad * gain_ref[:, lanes]) - tokens * pull
        gn_ref[:, lanes] += fold(grad * tokens * inverse)
    natural(gh_ref, grad_s, flag_ref, width)


def final(ds, ws, dm, wm, dt, wt, halo, dn, hidden, cot, gain, flag, width):
    groups = len(ds)
    rows = hidden.shape[0]
    inner = ds[0].shape[1]
    tile = 256
    row = lambda i: (i, 0)
    fixed = lambda i: (0, 0)
    return pl.pallas_call(
        functools.partial(final_kernel, groups, width, tuple(map(len, ws))),
        grid=(rows // tile,),
        in_specs=[
            *map(whole_spec, ds),
            *map(place_spec, flat(ws)),
            whole_spec(dm),
            whole_spec(wm),
            pl.BlockSpec((tile, LANES), row),
            whole_spec(wt),
            whole_spec(halo),
            pl.BlockSpec((tile, D), row),
            pl.BlockSpec((tile, D), row),
            pl.BlockSpec((tile, D), row),
            pl.BlockSpec((1, D), fixed),
            whole_spec(flag),
        ],
        out_specs=[pl.BlockSpec((tile, D), row), pl.BlockSpec((8, D), fixed)],
        out_shape=(jax.ShapeDtypeStruct((rows, D), F32), jax.ShapeDtypeStruct((8, D), F32)),
        scratch_shapes=[pltpu.VMEM((tile, groups * inner + 2 * NS), BF16), pltpu.VMEM((tile, D), F32), pltpu.VMEM((tile, D), F32)],
        compiler_params=pltpu.CompilerParams(vmem_limit_bytes=VMEM),
        cost_estimate=cost(20),
        name="final",
    )(*ds, *arrays(ws), dm, wm, dt, wt, halo, dn, hidden, cot, gain, flag)


def across(value, axis, size, bit):
    return lax.ppermute(value, axis, [(i, i ^ bit) for i in range(size)])


def bits(size):
    return [1 << i for i in range(size.bit_length() - 1)]


def after(value, *others):
    return lax.optimization_barrier((value, others))[0]


def shards(
    zn,
    tp,
    hidden,
    norm_gain,
    head_weight,
    step_weight,
    map_weight,
    conv_weight,
    conv_bias,
    step_bias,
    decay_log,
    skip_gain,
    gate_gain,
    out_weight,
    cotangent,
):
    rows = hidden.shape[0]
    width, _, inner = head_weight.shape
    heads = step_weight.shape[1]
    span = LEN // rows
    forward = [(i, i + 1) for i in range(tp - 1) if (i + 1) % span]
    backward = [(j, i) for i, j in forward]
    core, z_me, t_me = (lax.axis_index(name) for name in ("core", "z", "tensor"))
    swap = lambda value: across(value, "core", 2, 1)
    near = lambda value, bit: across(value, "tensor", tp, bit)
    steps = [("z", zn, b) for b in bits(zn)] + [("tensor", tp, b) for b in bits(tp)] + [("core", 2, 1)]
    half = zn * width // 2

    def to_own(array):
        parts = array.reshape(array.shape[:-1] + (zn, 2, width))
        first, second = parts[..., 0, :], parts[..., 1, :]
        both = [jnp.where(core == 0, first, second), jnp.where(core == 0, second, first)]
        return jnp.concatenate([a.reshape(array.shape[:-1] + (zn * width,)) for a in both], axis=-1)

    def from_own(array):
        lead = array.shape[:-1]
        own, other = (array[..., i * zn * width : (i + 1) * zn * width].reshape(lead + (zn, 1, width)) for i in (0, 1))
        both = [jnp.where(core == 0, own, other), jnp.where(core == 0, other, own)]
        return jnp.concatenate(both, axis=-2).reshape(lead + (D,))

    groups_now = jnp.arange(tp) ^ t_me
    z_now = jnp.arange(zn) ^ z_me
    core_now = jnp.arange(2)[:, None, None] * (zn * tp)
    by_place = (core_now + groups_now[None, None] * zn + z_now[None, :, None]).reshape(-1)
    by_group = (core_now + jnp.arange(tp)[None, None] * zn + z_now[None, :, None]).reshape(-1)

    def regroup(array):
        lead, last = array.shape[:-1], array.shape[-1]
        return jnp.take(array.reshape(lead + (tp, last // tp)), groups_now, axis=-2).reshape(array.shape)

    def send_own(mine):
        return [near(mine, 1), near(mine, 2)] if tp == 4 else [near(mine, g) for g in range(1, tp)]

    def send_far(got):
        if tp != 4:
            return [], []
        halves_now = [got[0][:half], got[1][half:]]
        return halves_now, [near(halves_now[0], 2), near(halves_now[1], 1)]

    def places(mine, mine_other, rest):
        other = swap(rest)
        return [[(mine, 0), (mine_other, 0)]] + [[(rest, g), (other, g)] for g in range(tp - 1)]

    coming = []

    class Scatter:
        def __init__(self, left, via):
            self.left, self.via, self.others = left, via, [None] * tp
            self.add = [[] for _ in range(tp)]

        def away(self, right):
            return dot(self.left[:, zn * width :], right, TN).astype(BF16)

        def swap(self, g, right):
            self.others[g] = swap(self.away(right))
            return self.others[g]

        def partial(self, g, right):
            total = dot(self.left[:, : zn * width], right, TN) + self.others[g].astype(F32)
            for term in self.add[g]:
                total = total + term.astype(F32)
            return total.astype(BF16)

        def send(self, g, right):
            part = self.partial(g, right)
            if tp == 4 and g == 3 and self.via is None:
                self.add[1].append(jnp.pad(near(part[:half], 2), ((0, half), (0, 0))))
                self.add[2].append(jnp.pad(near(part[half:], 1), ((half, 0), (0, 0))))
                coming.extend([self.add[1][-1], self.add[2][-1]])
                return part
            if tp == 4 and g == 3:
                got, at = near(part, 3 - self.via), self.via
            else:
                got, at = near(part, g), 0
            self.add[at].append(got)
            coming.append(got)
            return part

        def halves(self, g):
            return (1, 2) if tp == 4 and g == 3 and self.via is None else (0,)

        def finish(self, right):
            return self.partial(0, right)

    def scatter(total):
        return lax.psum_scatter(total, "z", scatter_dimension=0, tiled=True).astype(F32)

    def everywhere(vector):
        for axis, size, bit in steps:
            vector = vector + across(vector, axis, size, bit)
        return vector

    flag = jnp.full((8, LANES), core, F32)
    shard_x, shard_z = head_weight[:, 1], head_weight[:, 0]
    x_mine = lax.all_gather(shard_x, "z", axis=0, tiled=True)
    z_mine = lax.all_gather(after(shard_z, shard_x), "z", axis=0, tiled=True)
    out_mine = lax.all_gather(after(out_weight, shard_z), "z", axis=0, tiled=True)

    map_rows = map_weight.shape[0]
    pitch = -(-heads // 16) * 16
    strips = -(-width // LANES)
    pad_step = lambda a: jnp.pad(a, ((0, 0),) * (a.ndim - 2) + ((0, pitch - heads), (0, strips * LANES - width)))
    strip = lambda a: jnp.concatenate([a[..., i * LANES : (i + 1) * LANES] for i in range(a.shape[-1] // LANES)], axis=-2)
    small = jnp.concatenate([strip(map_weight), strip(pad_step(step_weight.T))], axis=0)[None]
    depth = small.shape[1]
    for axis, count, bit in steps:
        small = jnp.concatenate([small, across(small, axis, count, bit)], axis=0)
    pick = lambda a, index, axis: jnp.take(a, index, axis=axis, mode="clip")
    maps = pick(small[:, : 2 * map_rows], by_place, 0)
    map_w = jnp.concatenate([maps[:, i * map_rows : (i + 1) * map_rows].reshape(D, LANES) for i in (0, 1)], axis=1)
    steps_w = pick(small[:, 2 * map_rows :], by_group, 0).reshape(2, zn, tp, strips, pitch, LANES)
    steps_w = jnp.transpose(steps_w, (2, 4, 0, 1, 3, 5)).reshape(tp * pitch, 2 * zn, strips * LANES)
    step_w = steps_w[..., :width].reshape(tp * pitch, D)
    step_w = jnp.pad(step_w, ((0, LANES - tp * pitch), (0, 0)))

    x_mine = after(x_mine, map_w, step_w)
    x_own_other, x_near = swap(x_mine), send_own(x_mine)
    hidden, cotangent, norm_gain, conv_weight, conv_bias, step_bias, decay_log, skip_gain, gate_gain = after(
        (hidden, cotangent, norm_gain, conv_weight, conv_bias, step_bias, decay_log, skip_gain, gate_gain), map_w, step_w
    )
    hidden, norm_gain = to_own(hidden), to_own(norm_gain)
    halo = lax.ppermute(hidden[rows - HALO :], "tensor", forward)
    tokens = jnp.concatenate([halo, hidden], axis=0).astype(F32)
    inverse = lax.rsqrt(jnp.mean(tokens * tokens, axis=-1, keepdims=True) + EPSILON)
    normed_ext = jnp.pad((tokens * inverse * norm_gain).astype(BF16), ((0, TAIL), (0, 0)))
    normed = normed_ext[HALO : HALO + rows]

    def per_pitch(a):
        a = jnp.pad(a.reshape(tp, heads), ((0, 0), (0, pitch - heads))).reshape(1, tp * pitch)
        return jnp.pad(a, ((0, 0), (0, LANES - tp * pitch)))

    x_near, z_mine = after((x_near, z_mine), normed_ext)
    x_cut, x_far = send_far(x_near)
    z_mine = after(z_mine, *x_near)
    z_own_other, z_near = swap(z_mine), send_own(z_mine)
    cotangent, conv_weight, conv_bias, step_bias, decay_log, skip_gain, gate_gain = after(
        (cotangent, conv_weight, conv_bias, step_bias, decay_log, skip_gain, gate_gain), *x_cut
    )
    cotangent = to_own(cotangent)
    conv_x, bias_x = regroup(conv_weight[:, :DI]), regroup(conv_bias[None, :DI])
    conv_m, bias_m = conv_weight[:, DI:], conv_bias[None, DI:]
    step_bias, decay_log, skip_gain, gate_gain = (regroup(a[None]) for a in (step_bias, decay_log, skip_gain, gate_gain))
    skip = jnp.repeat(skip_gain, HEAD, axis=1)
    pre_m, bc, v, c2, cd, c2t, cdt, wf, ei, total = prep(
        normed_ext, after(map_w, *x_cut, x_own_other, out_mine, cotangent, conv_x, bias_x, skip, gate_gain), step_w, conv_m, bias_m, per_pitch(step_bias), per_pitch(decay_log), tp, heads, pitch
    )
    total = total[:, : tp * pitch].reshape(tp, pitch)[:, :heads].reshape(1, H)
    device_decay = jnp.repeat(jnp.exp2(total), HEAD, axis=1)
    groups = range(tp)
    span_of = lambda g: slice(g * inner, (g + 1) * inner)

    def pass_on(value, pairs, g):
        received = {}
        for gap in sorted({i ^ j for i, j in pairs}):
            received[g ^ gap] = lax.ppermute(value, "tensor", [(i, j) for i, j in pairs if i ^ j == gap])
        return received

    def chain(local, first, pairs):
        passed = gathered(first)
        for _ in range(span - 2):
            sums = [local[g].astype(F32) + device_decay[:, span_of(g)] * passed[g].astype(F32) for g in groups]
            passed = gathered([pass_on(total.astype(BF16), pairs, g) for g, total in enumerate(sums)])
        return passed

    def gathered(parts):
        out = [None] * tp
        for part in parts:
            for g, value in part.items():
                out[g] = value if out[g] is None else out[g] + value
        return [jnp.zeros((NS, inner), BF16) if value is None else value for value in out]

    pre, x, states, y, local = ([None] * tp for _ in range(5))

    first = []

    def run_project(g, *others):
        pre[g], x[g], local[g] = project(g, after(normed_ext, *others), x_w[g], conv_x, bias_x, bc, wf)
        first.append(pass_on(local[g], forward, g))

    def run_scan(g, *others):
        y[g], states[g] = scan(g, after(x[g], *others), bc, c2, cd, cdt, start[g], skip)

    x_w = [[(x_mine, 0), (x_own_other, 0)]]
    run_project(0)
    x_rest = jnp.concatenate(after(x_near + x_far, x[0]), axis=0)
    x_w = places(x_mine, x_own_other, x_rest)
    z = [product(after(normed, x_rest, z_own_other), [(z_mine, 0), (z_own_other, 0)])]
    run_project(1, z[0], x_w[1][1][0])
    z_near = after(z_near, x[1], *first[0].values())
    z_cut, z_far = send_far(z_near)
    if tp > 2:
        run_project(2, *z_cut)
    z_rest = jnp.concatenate(after(z_near + z_far, x[min(2, tp - 1)], *first[1].values()), axis=0)
    z_w = places(z_mine, z_own_other, z_rest)
    for g in range(3, tp):
        run_project(g, z_rest, x[g - 1])
    z.append(product(after(normed, x[tp - 1], z_w[1][1][0], *first[-2].values()), z_w[1]))
    start = after(chain(local, first, forward), z[1])
    out_mine = after(out_mine, *start)
    out_own_other, out_near = swap(out_mine), send_own(out_mine)
    run_scan(0)
    run_scan(1, y[0], out_own_other)
    out_near = after(out_near, y[1])
    out_cut, out_far = send_far(out_near)
    if tp > 2:
        run_scan(2, *out_cut)
    out_rest = jnp.concatenate(after(out_near + out_far, y[min(2, tp - 1)]), axis=0)
    out_w = places(out_mine, out_own_other, out_rest)
    for g in range(3, tp):
        run_scan(g, out_rest, y[g - 1])
    normed_late = after(normed, y[tp - 1], out_rest, out_w[1][1][0])
    z += [product(normed_late, z_w[g]) for g in range(2, tp)]

    scaled, dy, dz, local_pull, block_out, dn_z, gain_sums = gate(
        y, z, out_w, z_w, cotangent, hidden, gate_gain, bc, ei, flag, width
    )
    pulls = chain(local_pull, [pass_on(local_pull[g ^ 1], backward, g ^ 1) for g in reversed(groups)], backward)
    out_grad, z_grad, x_grad = Scatter(cotangent, 1), Scatter(normed, 2), Scatter(normed_ext, None)
    dpre, dbc, sums, q, da = ([None] * tp for _ in range(5))
    last = tp - 1
    order = list(reversed(groups))
    swapped = [out_grad.swap(last, scaled[last]), z_grad.swap(last, dz[last])]
    swapped += [out_grad.swap(g, after(scaled[g], *swapped)) for g in order[1:]]
    ready = swapped + pulls
    waiting = ready + [out_grad.send(last, after(scaled[last], *ready)), z_grad.send(last, after(dz[last], *ready))]
    later = []
    for at, g in enumerate(order):
        dpre[g], dbc[g], sums[g], q[g], da[g] = back(
            g, pre[g], after(dy[g], *waiting), bc, c2, cd, c2t, states[g], pulls[g], skip, conv_x, bias_x
        )
        arrivals = [dpre[g]] + coming
        coming.clear()
        now = lambda value: after(value, *arrivals)
        waiting = []
        if at < last:
            waiting.append(x_grad.swap(g, now(dpre[g])))
        if at == 0:
            waiting += [out_grad.send(i, now(scaled[i])) for i in order[1:-1]]
            waiting.append(x_grad.send(g, now(dpre[g])))
            later, coming[:] = coming[-len(x_grad.halves(g)) :], coming[: -len(x_grad.halves(g))]
            waiting += [z_grad.swap(i, now(dz[i])) for i in order[1:]]
        if at == 1:
            coming += later
            total = out_grad.finish(now(scaled[0]))
            waiting, total = lax.optimization_barrier((waiting, total))
            grad_out = scatter(total)
            waiting += [z_grad.send(i, now(dz[i])) for i in order[1:-1]]
        if at == last - 1:
            waiting += [x_grad.send(i, now(dpre[i])) for i in order[1:-1]]
        if at == min(2, last):
            total = z_grad.finish(now(dz[0]))
            waiting, total = lax.optimization_barrier((waiting, total))
            grad_z = scatter(total)
            waiting.append(grad_out)
    x_grad.swap(0, now(dpre[0]))
    total = x_grad.finish(now(dpre[0]))
    q, da, sums = after((q, da, sums), total)
    dbc_all, total = lax.optimization_barrier((after(functools.reduce(jnp.add, dbc), *waiting), total))
    grad_x = scatter(total)
    dpre_m, sums_m = map_back(pre_m, dbc_all, conv_m, bias_m)
    dn_z = after(dn_z, grad_z)

    v = v.reshape(H, rows)
    q, da = (jnp.concatenate(a, axis=0).reshape(H, rows) for a in (q, da))
    delta, sig = jax.nn.softplus(v), jax.nn.sigmoid(v)
    rate = -jnp.exp(decay_log).reshape(H, 1)
    ratio = jnp.where(v < -15.0, 1.0, sig / jnp.maximum(delta, 1e-30))
    dstep = q * ratio + da * rate * sig
    dstep_low = dstep.astype(BF16)
    dstep_t = jnp.pad(dstep_low.reshape(tp, heads, rows), ((0, 0), (0, pitch - heads), (0, 0))).reshape(tp * pitch, rows)
    dstep_t = jnp.pad(dstep_t, ((0, LANES - tp * pitch), (0, 0)))
    dstep_rows = dstep_t.T

    place_order = (core_now + z_now[None, None] * tp + groups_now[None, :, None]).reshape(-1)
    group_order = (core_now + z_now[None, None] * tp + jnp.arange(tp)[None, :, None]).reshape(-1)
    grad_map = dot(normed_ext, dpre_m, TN).reshape(2 * zn * tp, map_rows, 2 * NS)
    grad_map = pick(strip(grad_map), place_order, 0)
    grad_step = dot(dstep_t[: tp * pitch], normed).reshape(tp, pitch, 2, zn, width)[:, :heads]
    grad_step = strip(pad_step(jnp.transpose(grad_step, (2, 3, 0, 1, 4)).reshape(-1, heads, width)))
    grad_small = jnp.concatenate([grad_map, pick(grad_step, group_order, 0)], axis=-2)
    for axis, count, bit in reversed(steps):
        keep = grad_small.shape[0] // 2
        grad_small = grad_small[:keep] + across(grad_small[keep:], axis, count, bit)
    grad_small = grad_small[0]
    map_shard = jnp.concatenate([grad_small[:map_rows], grad_small[map_rows : 2 * map_rows]], axis=1)
    step_shard = grad_small[2 * map_rows :].reshape(strips, pitch, LANES)
    step_shard = jnp.concatenate([step_shard[i] for i in range(strips)], axis=1)[:heads, :width].T

    halo = jnp.zeros((HALO, DI + 2 * NS), BF16)
    edge = jnp.concatenate([a[:HALO] for a in dpre + [dpre_m]], axis=1)
    for gap in sorted({i ^ j for i, j in backward}):
        part = lax.ppermute(edge, "tensor", [(i, j) for i, j in backward if i ^ j == gap])
        halo = halo + jnp.concatenate([part[:, span_of(g ^ gap)] for g in groups] + [part[:, DI:]], axis=1)
    grad_hidden, norm_sums = final(
        dpre, x_w, dpre_m, map_w, dstep_rows, step_w, halo, dn_z, hidden, cotangent, norm_gain[None], flag, width
    )
    fold8 = lambda a: a.reshape(-1, 8, a.shape[-1]).sum(1)
    sums = jnp.concatenate([fold8(part) for part in sums], axis=1)
    taps = jnp.concatenate([regroup(sums[:5]), fold8(sums_m)], axis=1)
    per_head = jnp.stack(
        [
            jnp.sum(dstep, axis=1),
            jnp.sum(da * delta, axis=1) * rate[:, 0],
            jnp.sum(sums[5].reshape(H, HEAD), axis=1),
        ]
    )
    vector = [taps.reshape(-1), regroup(per_head).reshape(-1), regroup(fold8(gain_sums))[0]]
    vector = everywhere(after(jnp.concatenate(vector + [from_own(jnp.sum(norm_sums, axis=0))]), grad_x))
    wide = DI + 2 * NS
    cuts = [KW * wide, wide, H, H, H, DI, D]
    parts, at = [], 0
    for count in cuts:
        parts.append(vector[at : at + count])
        at += count
    return (
        block_out,
        grad_hidden,
        parts[6],
        jnp.stack([grad_z, grad_x], axis=1),
        step_shard,
        map_shard,
        parts[0].reshape(KW, wide),
        parts[1],
        parts[2],
        parts[3],
        parts[4],
        parts[5],
        grad_out,
    )


def solution(mesh):
    dp, tp = mesh.shape["dp"], mesh.shape["tensor"]
    inner = Mesh(mesh.devices.reshape(dp // 2, 2, tp), ("z", "core", "tensor"))
    rows = P(("z", "core", "tensor"), None)
    split_dp = ("z", "core")
    head, step, out = P(split_dp, None, "tensor"), P(split_dp, "tensor"), P(split_dp, "tensor")
    whole = P()
    return jax.shard_map(
        functools.partial(shards, dp // 2, tp),
        mesh=inner,
        in_specs=(rows, whole, head, step, rows, whole, whole, whole, whole, whole, whole, out, rows),
        out_specs=(rows, rows, whole, head, step, rows, whole, whole, whole, whole, whole, whole, out),
        check_vma=False,
    )
```

```python
import functools
import math

import jax
import jax.numpy as jnp
from jax import lax
from jax.experimental import pallas as pl
from jax.experimental.pallas import tpu as pltpu
from jax.sharding import Mesh
from jax.sharding import PartitionSpec as P

D = 1536
H = 48
HEAD = 64
NS = 128
KW = 4
LEN = 2048
DI = 3072
EPSILON = 1e-05

CHUNK = 128
HALO = 16
TAIL = 112
LANES = 128
LOG2E = math.log2(math.e)
NEG = -1e30
VMEM = 58 * 2**20
F32 = jnp.float32
BF16 = jnp.bfloat16
PRECISE = lax.Precision.HIGHEST
NT = (((1,), (1,)), ((), ()))
TN = (((0,), (0,)), ((), ()))


def dot(a, b, dims=(((1,), (0,)), ((), ())), precision=None):
    return lax.dot_general(a, b, dims, precision=precision, preferred_element_type=F32)


def iota(shape, axis):
    return lax.broadcasted_iota(jnp.int32, shape, axis)


def first_half(shape):
    return iota(shape, len(shape) - 1) < HEAD


def mix(columns, head, rows=CHUNK):
    shape = (rows, LANES)
    left = jnp.broadcast_to(columns[:, head : head + 1], shape)
    right = jnp.broadcast_to(columns[:, head + 1 : head + 2], shape)
    return jnp.where(first_half(shape), left, right)


def mix_row(row, head):
    shape = (1, LANES)
    left = jnp.broadcast_to(row[:, head : head + 1], shape)
    right = jnp.broadcast_to(row[:, head + 1 : head + 2], shape)
    return jnp.where(first_half(shape), left, right)


def halves(block):
    left = first_half(block.shape)
    zero = jnp.zeros_like(block)
    return jnp.where(left, block, zero), jnp.where(left, zero, block)


def shifted(block):
    return [pltpu.roll(block, KW - 1 - tap, 0)[HALO:] if tap < KW - 1 else block[HALO:] for tap in range(KW)]


def conv_total(taps, weight, bias):
    total = bias + weight[KW - 1 : KW] * taps[KW - 1]
    for tap in range(KW - 1):
        total = total + weight[tap : tap + 1] * taps[tap]
    return total


def conv_pull(grad, after, weight):
    rows = grad.shape[0]
    ext = jnp.concatenate([grad, after], axis=0)
    out = weight[KW - 1 : KW] * grad
    for ahead in range(1, KW):
        out = out + weight[KW - 1 - ahead : KW - ahead] * pltpu.roll(ext, rows + 8 - ahead, 0)[:rows]
    return out


def fold(block):
    total = block[0:8]
    for at in range(8, block.shape[0], 8):
        total = total + block[at : at + 8]
    return total


def col_sum(block):
    return jnp.sum(block, axis=0, keepdims=True)


def cost(us):
    return pl.CostEstimate(flops=0, bytes_accessed=int(us), transcendentals=0)


def times(left_ref, blocks):
    total, at = None, 0
    for block in blocks:
        term = dot(left_ref[:, at : at + block.shape[0]], block[...])
        total = term if total is None else total + term
        at += block.shape[0]
    return total


def launch(kernel, args, wait, in_specs, **options):
    inputs = len(args)

    def body(*refs):
        kernel(*refs[:inputs], *refs[inputs + len(wait) :])

    in_specs = [*in_specs, *[pl.BlockSpec(memory_space=pl.ANY)] * len(wait)]
    return pl.pallas_call(body, in_specs=in_specs, **options)(*args, *wait)


def split(refs, counts):
    out, at = [], 0
    for count in counts:
        out.append(refs[at : at + count])
        at += count
    return out


def place_spec(place):
    array, index = place
    return pl.BlockSpec((D // 2, array.shape[1]), lambda *_: (index, 0), pipeline_mode=pl.Buffered(1))


def whole_spec(array):
    return pl.BlockSpec(array.shape, lambda *_: (0,) * array.ndim, pipeline_mode=pl.Buffered(1))


def prep_kernel(heads, pitch, n_ref, wm_ref, ws_ref, cw_ref, cb_ref, sb_ref, dl_ref, pre_ref, bc_ref, v_ref, c2_ref, cd_ref, c2t_ref, cdt_ref, wf_ref, ei_ref, tot_ref, c2_s, cd_s):
    rows = bc_ref.shape[0]
    groups = c2_ref.shape[0]
    count = rows // CHUNK
    pre_ref[...] = dot(n_ref[...], wm_ref[...]).astype(BF16)
    for at in range(count):
        for pair in range(2):
            cols = slice(pair * LANES, (pair + 1) * LANES)
            block = pre_ref[at * CHUNK : at * CHUNK + CHUNK + HALO, cols].astype(F32)
            total = conv_total(shifted(block), cw_ref[:, cols], cb_ref[:, cols])
            bc_ref[at * CHUNK : (at + 1) * CHUNK, cols] = (total * jax.nn.sigmoid(total)).astype(BF16)
    rate = -jnp.exp(dl_ref[...]) * LOG2E
    lower = (iota((CHUNK, CHUNK), 0) >= iota((CHUNK, CHUNK), 1)).astype(F32)
    raw = dot(n_ref[HALO:], ws_ref[...], NT)
    totals = []
    for at in range(count):
        here = slice(at * CHUNK, (at + 1) * CHUNK)
        v = raw[here] + sb_ref[...]
        delta = jnp.maximum(v, 0.0) + jnp.log1p(jnp.exp(-jnp.abs(v)))
        log_delta = jnp.where(v < -15.0, v, jnp.log(jnp.maximum(delta, 1e-30)))
        c2 = dot(lower, delta * rate, precision=PRECISE)
        cd = c2 - log_delta * LOG2E
        c2_s[here] = c2
        cd_s[here] = cd
        totals.append(c2[CHUNK - 1 : CHUNK])
        v_t, c2_t, cd_t = v.T, c2.T, cd.T
        for g in range(groups):
            own = slice(g * pitch, g * pitch + heads)
            c2_ref[g, here] = c2[:, own]
            cd_ref[g, here] = cd[:, own]
            v_ref[g, :, here] = v_t[own]
            c2t_ref[g, :, here] = c2_t[own]
            cdt_ref[g, :, here] = cd_t[own]
    before = jnp.zeros_like(totals[0])
    for at in range(count):
        here = slice(at * CHUNK, (at + 1) * CHUNK)
        to_here = jnp.exp2(before + c2_s[here])
        before = before + totals[at]
        for g in range(groups):
            ei_ref[g, here] = to_here[:, g * pitch : g * pitch + heads]
    tot_ref[...] = before
    after = jnp.zeros_like(totals[0])
    for at in range(count - 1, -1, -1):
        here = slice(at * CHUNK, (at + 1) * CHUNK)
        after = after + totals[at]
        to_end = jnp.exp2(after - cd_s[here])
        for g in range(groups):
            wf_ref[g, here] = to_end[:, g * pitch : g * pitch + heads]


def prep(normed, map_w, step_w, conv_w, conv_b, step_b, decay_log, groups, heads, pitch):
    rows = normed.shape[0] - HALO - TAIL
    cols = jax.ShapeDtypeStruct((groups, rows, heads), F32)
    flat = jax.ShapeDtypeStruct((groups, heads, rows), F32)
    return pl.pallas_call(
        functools.partial(prep_kernel, heads, pitch),
        out_shape=(
            jax.ShapeDtypeStruct((rows + HALO, 2 * NS), BF16),
            jax.ShapeDtypeStruct((rows, 2 * NS), BF16),
            flat,
            cols,
            cols,
            flat,
            flat,
            cols,
            cols,
            jax.ShapeDtypeStruct((1, LANES), F32),
        ),
        grid=(1,),
        in_specs=[pl.BlockSpec((rows + HALO, D), lambda i: (0, 0))]
        + [whole_spec(a) for a in (map_w, step_w, conv_w, conv_b, step_b, decay_log)],
        scratch_shapes=[pltpu.VMEM((rows, LANES), F32), pltpu.VMEM((rows, LANES), F32)],
        compiler_params=pltpu.CompilerParams(vmem_limit_bytes=VMEM),
        cost_estimate=cost(11),
        name="prep",
    )(normed, map_w, step_w, conv_w, conv_b, step_b, decay_log)


def proj_kernel(tile, count, n_ref, *refs):
    blocks = refs[:count]
    cw_ref, cb_ref, bc_ref, wf_ref, pre_ref, x_ref, s_ref, xw_s = refs[count:]
    rows, inner = x_ref.shape
    for at in range(0, inner, tile):
        cols = slice(at, at + tile)
        pre_ref[:, cols] = times(n_ref, [block.at[:, cols] for block in blocks]).astype(BF16)

        def chunk(k, carry, at=at):
            start = pl.multiple_of(k * CHUNK, CHUNK)
            weights = wf_ref[0, pl.ds(start, CHUNK)]
            for q in range(at // LANES, (at + tile) // LANES):
                lanes = slice(q * LANES, (q + 1) * LANES)
                block = pre_ref[pl.ds(start, CHUNK + HALO), lanes].astype(F32)
                total = conv_total(shifted(block), cw_ref[:, lanes], cb_ref[:, lanes])
                x = (total * jax.nn.sigmoid(total)).astype(BF16)
                x_ref[pl.ds(start, CHUNK), lanes] = x
                xw_s[pl.ds(start, CHUNK), lanes] = (x.astype(F32) * mix(weights, 2 * q)).astype(BF16)
            return carry

        lax.fori_loop(0, rows // CHUNK, chunk, 0)
    s_ref[...] = dot(bc_ref[:, :NS], xw_s[...], TN).astype(BF16)


def project(g, normed, blocks, conv_w, conv_b, bc, wf, wait=()):
    rows = normed.shape[0] - HALO - TAIL
    ext = rows + HALO
    inner = blocks[0][0].shape[1]
    heads = inner // HEAD
    tile = inner
    return launch(
        functools.partial(proj_kernel, tile, len(blocks)),
        (normed, *(array for array, _ in blocks), conv_w, conv_b, bc, wf,),
        wait,
        grid=(1,),
        in_specs=[
            pl.BlockSpec((ext, D), lambda i: (0, 0)),
            *map(place_spec, blocks),
            pl.BlockSpec((KW, inner), lambda i: (0, g)),
            pl.BlockSpec((1, inner), lambda i: (0, g)),
            whole_spec(bc),
            pl.BlockSpec((1, rows, heads), lambda i: (g, 0, 0)),
        ],
        out_specs=[
            pl.BlockSpec((ext, inner), lambda i: (0, 0)),
            pl.BlockSpec((rows, inner), lambda i: (0, 0)),
            pl.BlockSpec((NS, inner), lambda i: (0, 0)),
        ],
        out_shape=(
            jax.ShapeDtypeStruct((ext, inner), BF16),
            jax.ShapeDtypeStruct((rows, inner), BF16),
            jax.ShapeDtypeStruct((NS, inner), BF16),
        ),
        scratch_shapes=[pltpu.VMEM((rows, inner), BF16)],
        compiler_params=pltpu.CompilerParams(vmem_limit_bytes=VMEM),
        cost_estimate=cost(10),
        name="project",
    )


def product_kernel(count, n_ref, *refs):
    refs[count][...] = times(n_ref, refs[:count]).astype(BF16)


def product(left, blocks, wait=()):
    rows = left.shape[0]
    inner = blocks[0][0].shape[1]
    tile = 256 if inner % 256 == 0 else LANES
    return launch(
        functools.partial(product_kernel, len(blocks)),
        (left, *(array for array, _ in blocks),),
        wait,
        grid=(inner // tile,),
        in_specs=[whole_spec(left), *(pl.BlockSpec((D // 2, tile), functools.partial(lambda index, j: (index, j), index)) for _, index in blocks)],
        out_specs=pl.BlockSpec((rows, tile), lambda j: (0, j)),
        out_shape=jax.ShapeDtypeStruct((rows, inner), BF16),
        compiler_params=pltpu.CompilerParams(vmem_limit_bytes=VMEM),
        cost_estimate=cost(4),
        name="product",
    )


def scan_kernel(x_ref, bc_ref, c2_ref, cd_ref, cdt_ref, s0_ref, skip_ref, y_ref, sin_ref, state, ya_s, xw_s):
    rows, inner = x_ref.shape
    heads = inner // HEAD
    causal = iota((CHUNK, CHUNK), 0) >= iota((CHUNK, CHUNK), 1)
    state[...] = s0_ref[...].astype(F32)

    def chunk(k, carry):
        start = pl.multiple_of(k * CHUNK, CHUNK)
        here = pl.ds(start, CHUNK)
        in_map, out_map = bc_ref[here, :NS], bc_ref[here, NS:]
        c2, cd = c2_ref[0, here], cd_ref[0, here]
        cd_t = cdt_ref[0, :, here]
        last = c2[CHUNK - 1 : CHUNK]
        from_start, to_end, whole = jnp.exp2(c2), jnp.exp2(last - cd), jnp.exp2(last)
        held = state[...].astype(BF16)
        sin_ref[k] = held
        ya_s[...] = dot(out_map, held)
        scores = dot(out_map, in_map, NT)
        for q in range(heads // 2):
            lanes = slice(q * LANES, (q + 1) * LANES)
            x = x_ref[here, lanes]
            x32 = x.astype(F32)
            weights = []
            for head in (2 * q, 2 * q + 1):
                spread = c2[:, head : head + 1] - cd_t[head : head + 1]
                weights.append((scores * jnp.exp2(jnp.where(causal, spread, NEG))).astype(BF16))
            within = dot(jnp.concatenate(weights, axis=1), jnp.concatenate(halves(x), axis=0))
            y = within + mix(from_start, 2 * q) * ya_s[:, lanes] + skip_ref[:, lanes] * x32
            y_ref[here, lanes] = y.astype(BF16)
            xw_s[:, lanes] = (x32 * mix(to_end, 2 * q)).astype(BF16)
            state[:, lanes] = state[:, lanes] * mix_row(whole, 2 * q)
        state[...] += dot(in_map, xw_s[...], TN)
        return carry

    lax.fori_loop(0, rows // CHUNK, chunk, 0, unroll=2)


def scan(g, x, bc, c2, cd, cdt, state, skip, wait=()):
    rows = x.shape[0]
    heads = c2.shape[2]
    inner = heads * HEAD
    count = rows // CHUNK
    return launch(
        scan_kernel,
        (x, bc, c2, cd, cdt, state, skip,),
        wait,
        grid=(1,),
        in_specs=[
            whole_spec(x),
            whole_spec(bc),
            pl.BlockSpec((1, rows, heads), lambda i: (g, 0, 0)),
            pl.BlockSpec((1, rows, heads), lambda i: (g, 0, 0)),
            pl.BlockSpec((1, heads, rows), lambda i: (g, 0, 0)),
            whole_spec(state),
            pl.BlockSpec((1, inner), lambda i: (0, g)),
        ],
        out_specs=[
            pl.BlockSpec((rows, inner), lambda i: (0, 0)),
            pl.BlockSpec((count, NS, inner), lambda i: (0, 0, 0)),
        ],
        out_shape=(
            jax.ShapeDtypeStruct((rows, inner), BF16),
            jax.ShapeDtypeStruct((count, NS, inner), BF16),
        ),
        scratch_shapes=[
            pltpu.VMEM((NS, inner), F32),
            pltpu.VMEM((CHUNK, inner), F32),
            pltpu.VMEM((CHUNK, inner), BF16),
        ],
        compiler_params=pltpu.CompilerParams(vmem_limit_bytes=VMEM),
        cost_estimate=cost(9),
        name="scan",
    )


def gate_kernel(groups, width, out_counts, z_counts, *refs):
    ys, zs, outs_w, zs_w, rest, scs, dys, dzs, us, tail = split(
        refs, (groups, groups, sum(out_counts), sum(z_counts), 6, groups, groups, groups, groups, 8)
    )
    outs_w, zs_w = split(outs_w, out_counts), split(zs_w, z_counts)
    cot_ref, hid_ref, gain_ref, bc_ref, ei_ref, flag_ref = rest
    out_ref, dn_ref, gg_ref, gs_s, ga_s, de_s, sum_s, u_s = tail
    rows, inner = ys[0].shape
    tiles = inner // LANES

    @pl.when(pl.program_id(0) == 0)
    def _():
        gg_ref[...] = jnp.zeros_like(gg_ref)
        u_s[...] = jnp.zeros_like(u_s)

    for g in range(groups):
        gs_s[:, g * inner : (g + 1) * inner] = times(cot_ref, outs_w[g])
    for part in range(0, rows, CHUNK):
        here = slice(part, part + CHUNK)
        squares = jnp.zeros((CHUNK, LANES), F32)
        dots = jnp.zeros((CHUNK, LANES), F32)
        for g in range(groups):

            def measure(c, sums, g=g):
                lanes = pl.ds(pl.multiple_of(c * LANES, LANES), LANES)
                wide = pl.ds(pl.multiple_of(g * inner + c * LANES, LANES), LANES)
                z = zs[g][here, lanes].astype(F32)
                gated = ys[g][here, lanes].astype(F32) * (z * jax.nn.sigmoid(z))
                ga_s[here, wide] = gated
                return sums[0] + gated * gated, sums[1] + gs_s[here, wide] * gain_ref[:, wide] * gated

            squares, dots = lax.fori_loop(0, tiles, measure, (squares, dots), unroll=True)
        inverse = lax.rsqrt(jnp.sum(squares, axis=1, keepdims=True) / DI + EPSILON)
        pull = inverse * inverse * inverse * (jnp.sum(dots, axis=1, keepdims=True) / DI)
        inverse = jnp.broadcast_to(inverse, (CHUNK, LANES))
        pull = jnp.broadcast_to(pull, (CHUNK, LANES))
        for g in range(groups):
            for c in range(tiles):
                lanes = slice(c * LANES, (c + 1) * LANES)
                wide = slice(g * inner + c * LANES, g * inner + (c + 1) * LANES)
                z = zs[g][here, lanes].astype(F32)
                sig = jax.nn.sigmoid(z)
                gated = ga_s[here, wide]
                weighted = gs_s[here, wide]
                unit = gated * inverse
                gain = gain_ref[:, wide]
                scs[g][here, lanes] = (unit * gain).astype(BF16)
                gg_ref[:, wide] += fold(weighted * unit)
                grad = inverse * weighted * gain - gated * pull
                dy = (grad * (z * sig)).astype(BF16)
                dys[g][here, lanes] = dy
                slope = sig * (1.0 + z * (1.0 - sig))
                dzs[g][here, lanes] = (grad * ys[g][here, lanes].astype(F32) * slope).astype(BF16)
                de_s[here, wide] = (dy.astype(F32) * mix(ei_ref[g, here], 2 * c)).astype(BF16)
    for g in range(groups):
        cols = slice(g * inner, (g + 1) * inner)
        u_s[:, cols] += dot(bc_ref[:, NS:], de_s[:, cols], TN)
        us[g][...] = u_s[:, cols].astype(BF16)
    back_times(sum_s, scs, outs_w, hid_ref)
    natural(out_ref, sum_s, flag_ref, width)
    back_times(dn_ref, dzs, zs_w, None)


def natural(out_ref, source_ref, flag_ref, width):
    first = flag_ref[0:1, 0:1] == 0.0
    half = source_ref.shape[1] // 2
    for z in range(half // width):
        own = source_ref[:, z * width : (z + 1) * width]
        other = source_ref[:, half + z * width : half + (z + 1) * width]
        pair = jnp.concatenate([jnp.where(first, own, other), jnp.where(first, other, own)], axis=1)
        out_ref[:, 2 * z * width : 2 * (z + 1) * width] = pair.astype(out_ref.dtype)


def back_times(out_ref, lefts, weights, base_ref):
    cuts = sorted({0} | {sum(b.shape[0] for b in blocks[: i + 1]) for blocks in weights for i in range(len(blocks))})
    for low, high in zip(cuts[:-1], cuts[1:]):
        total = None if base_ref is None else base_ref[:, low:high].astype(F32)
        for left, blocks in zip(lefts, weights):
            at = 0
            for block in blocks:
                if at <= low < at + block.shape[0]:
                    term = dot(left[...], block[low - at : high - at], NT)
                    total = term if total is None else total + term
                at += block.shape[0]
        out_ref[:, low:high] = total.astype(out_ref.dtype)


def arrays(places):
    return [array for array, _ in flat(places)]


def flat(lists):
    return [item for items in lists for item in items]


def gate(ys, zs, outs_w, zs_w, cot, hidden, gain, bc, ei, flag, width):
    groups = len(ys)
    rows, inner = ys[0].shape
    heads = inner // HEAD
    tile = 256
    wide = groups * inner
    row = lambda i: (i, 0)
    fixed = lambda i: (0, 0)
    group = [pl.BlockSpec((tile, inner), row)] * groups
    group_shape = [jax.ShapeDtypeStruct((rows, inner), BF16)] * groups
    out = pl.pallas_call(
        functools.partial(gate_kernel, groups, width, tuple(map(len, outs_w)), tuple(map(len, zs_w))),
        grid=(rows // tile,),
        in_specs=[
            *group,
            *group,
            *map(place_spec, flat(outs_w)),
            *map(place_spec, flat(zs_w)),
            pl.BlockSpec((tile, D), row),
            pl.BlockSpec((tile, D), row),
            pl.BlockSpec((1, wide), fixed),
            pl.BlockSpec((tile, 2 * NS), row),
            pl.BlockSpec((groups, tile, heads), lambda i: (0, i, 0)),
            whole_spec(flag),
        ],
        out_specs=[
            *group,
            *group,
            *group,
            *[pl.BlockSpec((NS, inner), fixed)] * groups,
            pl.BlockSpec((tile, D), row),
            pl.BlockSpec((tile, D), row),
            pl.BlockSpec((8, wide), fixed),
        ],
        out_shape=(
            *group_shape,
            *group_shape,
            *group_shape,
            *[jax.ShapeDtypeStruct((NS, inner), BF16)] * groups,
            jax.ShapeDtypeStruct((rows, D), BF16),
            jax.ShapeDtypeStruct((rows, D), F32),
            jax.ShapeDtypeStruct((8, wide), F32),
        ),
        scratch_shapes=[
            pltpu.VMEM((tile, wide), F32),
            pltpu.VMEM((tile, wide), F32),
            pltpu.VMEM((tile, wide), BF16),
            pltpu.VMEM((tile, D), F32),
            pltpu.VMEM((NS, wide), F32),
        ],
        compiler_params=pltpu.CompilerParams(vmem_limit_bytes=VMEM),
        cost_estimate=cost(55),
        name="gate",
    )(*ys, *zs, *arrays(outs_w), *arrays(zs_w), cot, hidden, gain, bc, ei, flag)
    return split(out, (groups, groups, groups, groups)) + list(out[4 * groups :])


def back_kernel(pre_ref, dy_ref, bc_ref, c2_ref, cd_ref, c2t_ref, sin_ref, u_ref, skip_ref, cw_ref, cb_ref, dpre_ref, dbc_ref, acc_ref, q_ref, da_ref, state, next_s, x_s, slope_s, de_s, xw_s, ya_s, bs_s):
    rows, inner = dy_ref.shape
    heads = inner // HEAD
    count = rows // CHUNK
    square = (CHUNK, CHUNK)
    flipped = iota(square, 1) >= iota(square, 0)
    later = (iota(square, 0) >= iota(square, 1)).astype(F32)
    earlier = (iota(square, 0) < iota(square, 1)).astype(F32)
    state[...] = u_ref[...].astype(F32)
    next_s[...] = jnp.zeros_like(next_s)
    acc_ref[...] = jnp.zeros_like(acc_ref)

    def chunk(step, carry):
        k = count - 1 - step
        start = pl.multiple_of(k * CHUNK, CHUNK)
        here = pl.ds(start, CHUNK)
        in_map, out_map = bc_ref[here, :NS], bc_ref[here, NS:]
        c2, cd = c2_ref[0, here], cd_ref[0, here]
        c2_t = c2t_ref[0, :, here]
        last = c2[CHUNK - 1 : CHUNK]
        from_start, to_end, whole = jnp.exp2(c2), jnp.exp2(last - cd), jnp.exp2(last)
        for q in range(heads // 2):
            lanes = slice(q * LANES, (q + 1) * LANES)
            block = pre_ref[pl.ds(start, CHUNK + HALO), lanes].astype(F32)
            total = conv_total(shifted(block), cw_ref[:, lanes], cb_ref[:, lanes])
            sig = jax.nn.sigmoid(total)
            x = (total * sig).astype(BF16)
            x_s[:, lanes] = x
            slope_s[:, lanes] = sig * (1.0 + total * (1.0 - sig))
            de_s[:, lanes] = (dy_ref[here, lanes].astype(F32) * mix(from_start, 2 * q)).astype(BF16)
            xw_s[:, lanes] = (x.astype(F32) * mix(to_end, 2 * q)).astype(BF16)
        held = sin_ref[k]
        after = state[...]
        after_low = after.astype(BF16)
        ya_s[...] = dot(out_map, held)
        bs_s[...] = dot(in_map, after_low)
        grad_out = dot(de_s[...], held, NT)
        grad_in = dot(xw_s[...], after_low, NT)
        through = col_sum(after * held.astype(F32))
        state[...] = dot(out_map, de_s[...], TN)
        scores = dot(in_map, out_map, NT)
        grad_scores = jnp.zeros(square, F32)
        rc_rows, st_rows, q_rows, tails = [], [], [], []
        for q in range(heads // 2):
            lanes = slice(q * LANES, (q + 1) * LANES)
            x, dy = x_s[:, lanes], dy_ref[here, lanes]
            x_parts, dy_parts = halves(x), halves(dy)
            weights, row_sums = [], []
            for side, head in enumerate((2 * q, 2 * q + 1)):
                spread = c2_t[head : head + 1] - cd[:, head : head + 1]
                decay = jnp.exp2(jnp.where(flipped, spread, NEG))
                weight = (scores * decay).astype(BF16)
                weights.append(weight)
                grad_weight = dot(x_parts[side], dy, NT)
                grad_scores = grad_scores + grad_weight * decay
                row_sums.append(col_sum(weight.astype(F32) * grad_weight))
            dx_in = dot(jnp.concatenate(weights, axis=1), jnp.concatenate(dy_parts, axis=0))
            dx_out = bs_s[:, lanes] * mix(to_end, 2 * q)
            x32, dy32 = x.astype(F32), dy.astype(F32)
            inside = x32 * dx_in
            outside = x32 * dx_out
            crossed = (de_s[:, lanes].astype(F32) * ya_s[:, lanes] - inside).T
            outside_t = outside.T
            both_t = (inside + outside).T
            through_q = through[:, lanes] * mix_row(whole, 2 * q)
            for side in range(2):
                part = slice(side * HEAD, (side + 1) * HEAD)
                rc_rows.append(row_sums[side] + col_sum(crossed[part]))
                st_rows.append(col_sum(outside_t[part]))
                q_rows.append(col_sum(both_t[part]))
                own = first_half((1, LANES)) if side == 0 else ~first_half((1, LANES))
                tails.append(jnp.sum(jnp.where(own, through_q, 0.0), axis=1, keepdims=True))
            state[:, lanes] += after[:, lanes] * mix_row(whole, 2 * q)
            grad = (dx_in + dx_out + skip_ref[:, lanes] * dy32) * slope_s[:, lanes]
            taps = shifted(pre_ref[pl.ds(start, CHUNK + HALO), lanes].astype(F32))
            for tap in range(KW):
                acc_ref[tap * 8 : tap * 8 + 8, lanes] += fold(grad * taps[tap])
            acc_ref[32:40, lanes] += fold(grad)
            acc_ref[40:48, lanes] += fold(dy32 * x32)
            dpre = conv_pull(grad, next_s[:, lanes], cw_ref[:, lanes])
            dpre_ref[pl.ds(pl.multiple_of(start + HALO, HALO), CHUNK), lanes] = dpre.astype(BF16)
            next_s[:, lanes] = grad[0:8]
        low_scores = grad_scores.astype(BF16)
        dbc_ref[here, :NS] = grad_in + dot(low_scores, out_map)
        dbc_ref[here, NS:] = grad_out + dot(low_scores, in_map, TN)
        da = dot(jnp.concatenate(rc_rows, axis=0), later, precision=PRECISE)
        da = da + dot(jnp.concatenate(st_rows, axis=0), earlier, precision=PRECISE)
        da_ref[0, :, here] = da + jnp.concatenate(tails, axis=0)
        q_ref[0, :, here] = jnp.concatenate(q_rows, axis=0)
        return carry

    lax.fori_loop(0, count, chunk, 0, unroll=2)
    for q in range(heads // 2):
        lanes = slice(q * LANES, (q + 1) * LANES)
        empty = jnp.zeros((HALO, LANES), F32)
        dpre_ref[0:HALO, lanes] = conv_pull(empty, next_s[:, lanes], cw_ref[:, lanes]).astype(BF16)
    dpre_ref[HALO + rows :] = jnp.zeros((TAIL, inner), BF16)


def back(g, pre, dy, bc, c2, cd, c2t, states, pull, skip, conv_w, conv_b, wait=()):
    ext = pre.shape[0]
    rows = ext - HALO
    heads = c2.shape[2]
    inner = heads * HEAD
    count = rows // CHUNK
    return launch(
        back_kernel,
        (pre, dy, bc, c2, cd, c2t, states, pull, skip, conv_w, conv_b,),
        wait,
        grid=(1,),
        in_specs=[
            whole_spec(pre),
            whole_spec(dy),
            whole_spec(bc),
            pl.BlockSpec((1, rows, heads), lambda i: (g, 0, 0)),
            pl.BlockSpec((1, rows, heads), lambda i: (g, 0, 0)),
            pl.BlockSpec((1, heads, rows), lambda i: (g, 0, 0)),
            whole_spec(states),
            whole_spec(pull),
            pl.BlockSpec((1, inner), lambda i: (0, g)),
            pl.BlockSpec((KW, inner), lambda i: (0, g)),
            pl.BlockSpec((1, inner), lambda i: (0, g)),
        ],
        out_specs=[
            pl.BlockSpec((ext + TAIL, inner), lambda i: (0, 0)),
            pl.BlockSpec((rows, 2 * NS), lambda i: (0, 0)),
            pl.BlockSpec((48, inner), lambda i: (0, 0)),
            pl.BlockSpec((1, heads, rows), lambda i: (0, 0, 0)),
            pl.BlockSpec((1, heads, rows), lambda i: (0, 0, 0)),
        ],
        out_shape=(
            jax.ShapeDtypeStruct((ext + TAIL, inner), BF16),
            jax.ShapeDtypeStruct((rows, 2 * NS), F32),
            jax.ShapeDtypeStruct((48, inner), F32),
            jax.ShapeDtypeStruct((1, heads, rows), F32),
            jax.ShapeDtypeStruct((1, heads, rows), F32),
        ),
        scratch_shapes=[
            pltpu.VMEM((NS, inner), F32),
            pltpu.VMEM((8, inner), F32),
            pltpu.VMEM((CHUNK, inner), BF16),
            pltpu.VMEM((CHUNK, inner), F32),
            pltpu.VMEM((CHUNK, inner), BF16),
            pltpu.VMEM((CHUNK, inner), BF16),
            pltpu.VMEM((CHUNK, inner), F32),
            pltpu.VMEM((CHUNK, inner), F32),
        ],
        compiler_params=pltpu.CompilerParams(vmem_limit_bytes=VMEM),
        cost_estimate=cost(18),
        name="back",
    )


def map_back_kernel(pre_ref, grad_ref, cw_ref, cb_ref, dpre_ref, acc_ref, next_s):
    rows, wide = grad_ref.shape
    count = rows // CHUNK
    next_s[...] = jnp.zeros_like(next_s)
    acc_ref[...] = jnp.zeros_like(acc_ref)
    for k in range(count - 1, -1, -1):
        start = k * CHUNK
        for q in range(wide // LANES):
            lanes = slice(q * LANES, (q + 1) * LANES)
            taps = shifted(pre_ref[start : start + CHUNK + HALO, lanes].astype(F32))
            total = conv_total(taps, cw_ref[:, lanes], cb_ref[:, lanes])
            sig = jax.nn.sigmoid(total)
            grad = grad_ref[start : start + CHUNK, lanes] * (sig * (1.0 + total * (1.0 - sig)))
            for tap in range(KW):
                acc_ref[tap * 8 : tap * 8 + 8, lanes] += fold(grad * taps[tap])
            acc_ref[32:40, lanes] += fold(grad)
            dpre = conv_pull(grad, next_s[:, lanes], cw_ref[:, lanes])
            dpre_ref[start + HALO : start + HALO + CHUNK, lanes] = dpre.astype(BF16)
            next_s[:, lanes] = grad[0:8]
    for q in range(wide // LANES):
        lanes = slice(q * LANES, (q + 1) * LANES)
        empty = jnp.zeros((HALO, LANES), F32)
        dpre_ref[0:HALO, lanes] = conv_pull(empty, next_s[:, lanes], cw_ref[:, lanes]).astype(BF16)
    dpre_ref[HALO + rows :] = jnp.zeros((TAIL, wide), BF16)


def map_back(pre, grad, conv_w, conv_b):
    return pl.pallas_call(
        map_back_kernel,
        out_shape=(jax.ShapeDtypeStruct((pre.shape[0] + TAIL, pre.shape[1]), BF16), jax.ShapeDtypeStruct((40, pre.shape[1]), F32)),
        scratch_shapes=[pltpu.VMEM((8, pre.shape[1]), F32)],
        compiler_params=pltpu.CompilerParams(vmem_limit_bytes=VMEM),
        cost_estimate=cost(4),
        name="map_back",
    )(pre, grad, conv_w, conv_b)


def final_kernel(groups, width, counts, *refs):
    ds, ws, rest = split(refs, (groups, sum(counts), 15))
    ws = split(ws, counts)
    dm_ref, wm_ref, dt_ref, wt_ref, halo_ref, dn_ref, hid_ref, cot_ref, gain_ref, flag_ref, gh_ref, gn_ref, left_s, total_s, grad_s = rest
    rows, wide = hid_ref.shape
    inner = ds[0].shape[1]
    start = pl.multiple_of(pl.program_id(0) * rows, HALO)

    @pl.when(pl.program_id(0) == 0)
    def _():
        gn_ref[...] = jnp.zeros_like(gn_ref)

    own = pl.ds(pl.multiple_of(start + HALO, HALO), rows)
    for g in range(groups):
        left_s[:, g * inner : (g + 1) * inner] = ds[g][own]
    left_s[:, groups * inner :] = dm_ref[own]

    @pl.when(pl.program_id(0) == pl.num_programs(0) - 1)
    def _():
        last = slice(rows - HALO, rows)
        left_s[last] = (left_s[last].astype(F32) + halo_ref[...].astype(F32)).astype(BF16)

    lefts = [left_s.at[:, g * inner : (g + 1) * inner] for g in range(groups)]
    lefts += [left_s.at[:, groups * inner :]]
    back_times(total_s, lefts, ws + [[wm_ref]], dn_ref)
    total_s[...] += dot(dt_ref[...], wt_ref[...])
    squares = jnp.zeros((rows, 1), F32)
    for c in range(wide // LANES):
        lanes = slice(c * LANES, (c + 1) * LANES)
        tokens = hid_ref[:, lanes].astype(F32)
        squares = squares + jnp.sum(tokens * tokens, axis=1, keepdims=True)
    inverse = lax.rsqrt(squares / wide + EPSILON)
    dots = jnp.zeros((rows, 1), F32)
    for c in range(wide // LANES):
        lanes = slice(c * LANES, (c + 1) * LANES)
        tokens = hid_ref[:, lanes].astype(F32)
        dots = dots + jnp.sum(total_s[:, lanes] * gain_ref[:, lanes] * tokens, axis=1, keepdims=True)
    pull = inverse * inverse * inverse * (dots / wide)
    for c in range(wide // LANES):
        lanes = slice(c * LANES, (c + 1) * LANES)
        tokens = hid_ref[:, lanes].astype(F32)
        grad = total_s[:, lanes]
        grad_s[:, lanes] = cot_ref[:, lanes].astype(F32) + inverse * (grad * gain_ref[:, lanes]) - tokens * pull
        gn_ref[:, lanes] += fold(grad * tokens * inverse)
    natural(gh_ref, grad_s, flag_ref, width)


def final(ds, ws, dm, wm, dt, wt, halo, dn, hidden, cot, gain, flag, width, wait=()):
    groups = len(ds)
    rows = hidden.shape[0]
    inner = ds[0].shape[1]
    tile = 256
    row = lambda i: (i, 0)
    fixed = lambda i: (0, 0)
    return launch(
        functools.partial(final_kernel, groups, width, tuple(map(len, ws))),
        (*ds, *arrays(ws), dm, wm, dt, wt, halo, dn, hidden, cot, gain, flag,),
        wait,
        grid=(rows // tile,),
        in_specs=[
            *map(whole_spec, ds),
            *map(place_spec, flat(ws)),
            whole_spec(dm),
            whole_spec(wm),
            pl.BlockSpec((tile, LANES), row),
            whole_spec(wt),
            whole_spec(halo),
            pl.BlockSpec((tile, D), row),
            pl.BlockSpec((tile, D), row),
            pl.BlockSpec((tile, D), row),
            pl.BlockSpec((1, D), fixed),
            whole_spec(flag),
        ],
        out_specs=[pl.BlockSpec((tile, D), row), pl.BlockSpec((8, D), fixed)],
        out_shape=(jax.ShapeDtypeStruct((rows, D), F32), jax.ShapeDtypeStruct((8, D), F32)),
        scratch_shapes=[pltpu.VMEM((tile, groups * inner + 2 * NS), BF16), pltpu.VMEM((tile, D), F32), pltpu.VMEM((tile, D), F32)],
        compiler_params=pltpu.CompilerParams(vmem_limit_bytes=VMEM),
        cost_estimate=cost(20),
        name="final",
    )


def across(value, axis, size, bit):
    return lax.ppermute(value, axis, [(i, i ^ bit) for i in range(size)])


def bits(size):
    return [1 << i for i in range(size.bit_length() - 1)]


def after(value, *others):
    return lax.optimization_barrier((value, others))[0]


def shards(
    zn,
    tp,
    hidden,
    norm_gain,
    head_weight,
    step_weight,
    map_weight,
    conv_weight,
    conv_bias,
    step_bias,
    decay_log,
    skip_gain,
    gate_gain,
    out_weight,
    cotangent,
):
    rows = hidden.shape[0]
    width, _, inner = head_weight.shape
    heads = step_weight.shape[1]
    span = LEN // rows
    forward = [(i, i + 1) for i in range(tp - 1) if (i + 1) % span]
    backward = [(j, i) for i, j in forward]
    core, z_me, t_me = (lax.axis_index(name) for name in ("core", "z", "tensor"))
    swap = lambda value: across(value, "core", 2, 1)
    near = lambda value, bit: across(value, "tensor", tp, bit)
    steps = [("z", zn, b) for b in bits(zn)] + [("tensor", tp, b) for b in bits(tp)] + [("core", 2, 1)]
    half = zn * width // 2

    def to_own(array):
        parts = array.reshape(array.shape[:-1] + (zn, 2, width))
        first, second = parts[..., 0, :], parts[..., 1, :]
        both = [jnp.where(core == 0, first, second), jnp.where(core == 0, second, first)]
        return jnp.concatenate([a.reshape(array.shape[:-1] + (zn * width,)) for a in both], axis=-1)

    def from_own(array):
        lead = array.shape[:-1]
        own, other = (array[..., i * zn * width : (i + 1) * zn * width].reshape(lead + (zn, 1, width)) for i in (0, 1))
        both = [jnp.where(core == 0, own, other), jnp.where(core == 0, other, own)]
        return jnp.concatenate(both, axis=-2).reshape(lead + (D,))

    groups_now = jnp.arange(tp) ^ t_me
    z_now = jnp.arange(zn) ^ z_me
    core_now = jnp.arange(2)[:, None, None] * (zn * tp)
    by_place = (core_now + groups_now[None, None] * zn + z_now[None, :, None]).reshape(-1)
    by_group = (core_now + jnp.arange(tp)[None, None] * zn + z_now[None, :, None]).reshape(-1)

    def regroup(array):
        lead, last = array.shape[:-1], array.shape[-1]
        return jnp.take(array.reshape(lead + (tp, last // tp)), groups_now, axis=-2).reshape(array.shape)

    def send_own(mine):
        return [near(mine, 1), near(mine, 2)] if tp == 4 else [near(mine, g) for g in range(1, tp)]

    def send_far(got):
        if tp != 4:
            return [], []
        halves_now = [got[0][:half], got[1][half:]]
        return halves_now, [near(halves_now[0], 2), near(halves_now[1], 1)]

    def places(mine, mine_other, rest):
        other = swap(rest)
        return [[(mine, 0), (mine_other, 0)]] + [[(rest, g), (other, g)] for g in range(tp - 1)]

    coming = []

    class Scatter:
        def __init__(self, left, via):
            self.left, self.via, self.others = left, via, [None] * tp
            self.add = [[] for _ in range(tp)]

        def away(self, right):
            return dot(self.left[:, zn * width :], right, TN).astype(BF16)

        def swap(self, g, right):
            self.others[g] = swap(self.away(right))
            return self.others[g]

        def partial(self, g, right):
            total = dot(self.left[:, : zn * width], right, TN) + self.others[g].astype(F32)
            for term in self.add[g]:
                total = total + term.astype(F32)
            return total.astype(BF16)

        def send(self, g, right):
            part = self.partial(g, right)
            if tp == 4 and g == 3:
                got, at = near(part, 3 - self.via), self.via
            else:
                got, at = near(part, g), 0
            self.add[at].append(got)
            coming.append(got)
            return part

        def finish(self, right):
            return self.partial(0, right)

    def scatter(total):
        return lax.psum_scatter(total, "z", scatter_dimension=0, tiled=True)

    def everywhere(vector):
        for axis, size in (("z", zn), ("tensor", tp), ("core", 2)):
            if size == 4:
                one, two, three = (across(vector, axis, size, gap) for gap in (1, 2, 3))
                vector = (vector + one) + (two + three)
            else:
                for bit in bits(size):
                    vector = vector + across(vector, axis, size, bit)
        return vector

    flag = jnp.full((8, LANES), core, F32)
    shard_x, shard_z = head_weight[:, 1], head_weight[:, 0]
    x_mine = lax.all_gather(shard_x, "z", axis=0, tiled=True)
    z_mine = lax.all_gather(after(shard_z, shard_x), "z", axis=0, tiled=True)
    out_mine = lax.all_gather(after(out_weight, shard_z), "z", axis=0, tiled=True)

    map_rows = map_weight.shape[0]
    pitch = -(-heads // 16) * 16
    strips = -(-width // LANES)
    pad_step = lambda a: jnp.pad(a, ((0, 0),) * (a.ndim - 2) + ((0, pitch - heads), (0, strips * LANES - width)))
    strip = lambda a: jnp.concatenate([a[..., i * LANES : (i + 1) * LANES] for i in range(a.shape[-1] // LANES)], axis=-2)
    small = jnp.concatenate([strip(map_weight), strip(pad_step(step_weight.T))], axis=0)[None]
    depth = small.shape[1]
    for axis, count, bit in steps:
        small = jnp.concatenate([small, across(small, axis, count, bit)], axis=0)
    pick = lambda a, index, axis: jnp.take(a, index, axis=axis, mode="clip")
    maps = pick(small[:, : 2 * map_rows], by_place, 0)
    map_w = jnp.concatenate([maps[:, i * map_rows : (i + 1) * map_rows].reshape(D, LANES) for i in (0, 1)], axis=1)
    steps_w = pick(small[:, 2 * map_rows :], by_group, 0).reshape(2, zn, tp, strips, pitch, LANES)
    steps_w = jnp.transpose(steps_w, (2, 4, 0, 1, 3, 5)).reshape(tp * pitch, 2 * zn, strips * LANES)
    step_w = steps_w[..., :width].reshape(tp * pitch, D)
    step_w = jnp.pad(step_w, ((0, LANES - tp * pitch), (0, 0)))

    x_mine = after(x_mine, map_w, step_w)
    x_own_other, x_near = swap(x_mine), send_own(x_mine)
    hidden, cotangent, norm_gain, conv_weight, conv_bias, step_bias, decay_log, skip_gain, gate_gain = after(
        (hidden, cotangent, norm_gain, conv_weight, conv_bias, step_bias, decay_log, skip_gain, gate_gain), map_w, step_w
    )
    hidden, norm_gain = to_own(hidden), to_own(norm_gain)
    halo = lax.ppermute(hidden[rows - HALO :], "tensor", forward)
    tokens = jnp.concatenate([halo, hidden], axis=0).astype(F32)
    inverse = lax.rsqrt(jnp.mean(tokens * tokens, axis=-1, keepdims=True) + EPSILON)
    normed_ext = jnp.pad((tokens * inverse * norm_gain).astype(BF16), ((0, TAIL), (0, 0)))
    normed = normed_ext[HALO : HALO + rows]

    def per_pitch(a):
        a = jnp.pad(a.reshape(tp, heads), ((0, 0), (0, pitch - heads))).reshape(1, tp * pitch)
        return jnp.pad(a, ((0, 0), (0, LANES - tp * pitch)))

    skip_gain, gate_gain, cotangent_late = after((skip_gain, gate_gain, cotangent), normed_ext)
    conv_x, bias_x = regroup(conv_weight[:, :DI]), regroup(conv_bias[None, :DI])
    conv_m, bias_m = conv_weight[:, DI:], conv_bias[None, DI:]
    step_bias, decay_log = (regroup(a[None]) for a in (step_bias, decay_log))
    pre_m, bc, v, c2, cd, c2t, cdt, wf, ei, total = prep(
        normed_ext, after(map_w, x_own_other, conv_x, bias_x), step_w, conv_m, bias_m, per_pitch(step_bias), per_pitch(decay_log), tp, heads, pitch
    )
    total = total[:, : tp * pitch].reshape(tp, pitch)[:, :heads].reshape(1, H)
    device_decay = jnp.repeat(jnp.exp2(total), HEAD, axis=1)
    groups = range(tp)
    span_of = lambda g: slice(g * inner, (g + 1) * inner)

    def pass_on(value, pairs, g):
        received = {}
        for gap in sorted({i ^ j for i, j in pairs}):
            received[g ^ gap] = lax.ppermute(value, "tensor", [(i, j) for i, j in pairs if i ^ j == gap])
        return received

    def chain(local, first, pairs):
        passed = gathered(first)
        for _ in range(span - 2):
            sums = [local[g].astype(F32) + device_decay[:, span_of(g)] * passed[g].astype(F32) for g in groups]
            passed = gathered([pass_on(total.astype(BF16), pairs, g) for g, total in enumerate(sums)])
        return passed

    def gathered(parts):
        out = [None] * tp
        for part in parts:
            for g, value in part.items():
                out[g] = value if out[g] is None else out[g] + value
        return [jnp.zeros((NS, inner), BF16) if value is None else value for value in out]

    pre, x, states, y, local = ([None] * tp for _ in range(5))

    first = []

    def run_project(g, *others):
        pre[g], x[g], local[g] = project(g, normed_ext, x_w[g], conv_x, bias_x, bc, wf, others)
        first.append(pass_on(local[g], forward, g))

    def run_scan(g, *others):
        y[g], states[g] = scan(g, x[g], bc, c2, cd, cdt, start[g], skip, others)

    cotangent, skip_gain, gate_gain = after((cotangent_late, skip_gain, gate_gain), bc)
    cotangent, skip_gain, gate_gain = to_own(cotangent), regroup(skip_gain[None]), regroup(gate_gain[None])
    skip = jnp.repeat(skip_gain, HEAD, axis=1)
    x_near, z_mine = after((x_near, z_mine), bc, cotangent)
    x_cut, x_far = send_far(x_near)
    z_mine = after(z_mine, *x_cut)
    z_own_other, z_near = swap(z_mine), send_own(z_mine)
    x_w = [[(x_mine, 0), (x_own_other, 0)]]
    run_project(0, *x_cut)
    x_rest = jnp.concatenate(after(x_near + x_far, x[0]), axis=0)
    x_w = places(x_mine, x_own_other, x_rest)
    run_project(1, x_w[1][1][0], skip, gate_gain, z_own_other)
    z_near = after(z_near, x[1], *first[0].values())
    z_cut, z_far = send_far(z_near)
    if tp > 2:
        run_project(2, x[1], out_mine, *z_cut)
    z_rest = jnp.concatenate(after(z_near + z_far, x[min(2, tp - 1)], *first[1].values()), axis=0)
    z_w = places(z_mine, z_own_other, z_rest)
    for g in range(3, tp):
        run_project(g, z_rest, x[g - 1])
    z = [product(normed, z_w[0], (x[tp - 1], *first[-2].values()))]
    start = chain(local, first, forward)
    out_mine = after(out_mine, *start)
    out_own_other, out_near = swap(out_mine), send_own(out_mine)
    run_scan(0, z[0])
    run_scan(1, y[0], out_own_other, z_w[1][1][0])
    out_near = after(out_near, y[1])
    out_cut, out_far = send_far(out_near)
    if tp > 2:
        run_scan(2, y[1], *out_cut)
    out_rest = jnp.concatenate(after(out_near + out_far, y[min(2, tp - 1)]), axis=0)
    out_w = places(out_mine, out_own_other, out_rest)
    for g in range(3, tp):
        run_scan(g, out_rest, y[g - 1])
    z += [product(normed, z_w[g], (y[tp - 1], out_w[1][1][0])) for g in range(1, tp)]

    scaled, dy, dz, local_pull, block_out, dn_z, gain_sums = gate(
        y, z, out_w, z_w, cotangent, hidden, gate_gain, bc, ei, flag, width
    )
    pulls = chain(local_pull, [pass_on(local_pull[g ^ 1], backward, g ^ 1) for g in reversed(groups)], backward)
    out_grad, z_grad, x_grad = Scatter(cotangent, 1), Scatter(normed, 2), Scatter(normed_ext, 1)
    dpre, dbc, sums, q, da = ([None] * tp for _ in range(5))
    last = tp - 1
    order = list(reversed(groups))
    swapped = [out_grad.swap(last, scaled[last]), z_grad.swap(last, dz[last])]
    far_out = out_grad.send(last, after(scaled[last], *swapped))
    ready = [out_grad.swap(g, after(scaled[g], far_out)) for g in order[1:]]
    far_z = z_grad.send(last, after(dz[last], *ready, *pulls))
    waiting = ready + [far_out, far_z] + pulls
    finished = []
    for at, g in enumerate(order):
        dpre[g], dbc[g], sums[g], q[g], da[g] = back(
            g, pre[g], dy[g], bc, c2, cd, c2t, states[g], pulls[g], skip, conv_x, bias_x, waiting
        )
        arrivals = [dpre[g]] + coming + finished
        coming.clear()
        waiting = []
        now = lambda value: after(value, *arrivals, *waiting)
        if at == 0:
            waiting += [out_grad.send(i, now(scaled[i])) for i in order[1:-1]]
        if at == 1:
            waiting.append(x_grad.send(order[0], now(dpre[order[0]])))
        if at == last - 1 and at > 0:
            waiting += [x_grad.send(i, now(dpre[i])) for i in order[1:-2]]
        if at < last:
            waiting.append(x_grad.swap(g, now(dpre[g])))
        if at == 0:
            waiting += [z_grad.swap(i, now(dz[i])) for i in order[1:]]
            waiting += [z_grad.send(i, now(dz[i])) for i in order[1:-1]]
            del coming[-len(order[1:-1]) :]
        if at == last - 1 and at > 0:
            waiting.append(x_grad.send(g, now(dpre[g])))
        if at == 1:
            total = out_grad.finish(now(scaled[0]))
            waiting.append(total)
            grad_out = scatter(total)
            total = z_grad.finish(now(dz[0]))
            waiting.append(total)
            grad_z = scatter(total)
            finished = [grad_out]
        if at == min(2, last):
            finished = [grad_z]
    x_grad.swap(0, now(dpre[0]))
    total = x_grad.finish(now(dpre[0]))
    grad_x = scatter(total)
    q, da, sums = after((q, da, sums), total)
    dbc_all = after(functools.reduce(jnp.add, dbc), total)
    dpre_m, sums_m = map_back(pre_m, dbc_all, conv_m, bias_m)

    v = v.reshape(H, rows)
    q, da = (jnp.concatenate(a, axis=0).reshape(H, rows) for a in (q, da))
    delta, sig = jax.nn.softplus(v), jax.nn.sigmoid(v)
    rate = -jnp.exp(decay_log).reshape(H, 1)
    ratio = jnp.where(v < -15.0, 1.0, sig / jnp.maximum(delta, 1e-30))
    dstep = q * ratio + da * rate * sig
    dstep_low = dstep.astype(BF16)
    dstep_t = jnp.pad(dstep_low.reshape(tp, heads, rows), ((0, 0), (0, pitch - heads), (0, 0))).reshape(tp * pitch, rows)
    dstep_t = jnp.pad(dstep_t, ((0, LANES - tp * pitch), (0, 0)))
    dstep_rows = dstep_t.T

    place_order = (core_now + z_now[None, None] * tp + groups_now[None, :, None]).reshape(-1)
    group_order = (core_now + z_now[None, None] * tp + jnp.arange(tp)[None, :, None]).reshape(-1)
    grad_map = dot(normed_ext, dpre_m, TN).reshape(2 * zn * tp, map_rows, 2 * NS)
    grad_map = pick(strip(grad_map), place_order, 0)
    grad_step = dot(dstep_t[: tp * pitch], normed).reshape(tp, pitch, 2, zn, width)[:, :heads]
    grad_step = strip(pad_step(jnp.transpose(grad_step, (2, 3, 0, 1, 4)).reshape(-1, heads, width)))
    grad_small = jnp.concatenate([grad_map, pick(grad_step, group_order, 0)], axis=-2)
    def to_owners(parts, axis, count):
        parts = parts.reshape((count, -1) + parts.shape[1:])
        total = parts[0]
        for gap in range(1, count):
            total = total + across(parts[gap], axis, count, gap)
        return total

    grad_small = to_owners(grad_small, "core", 2)
    halo = jnp.zeros((HALO, DI + 2 * NS), BF16)
    edge = jnp.concatenate([a[:HALO] for a in dpre + [dpre_m]], axis=1)
    for gap in sorted({i ^ j for i, j in backward}):
        part = lax.ppermute(edge, "tensor", [(i, j) for i, j in backward if i ^ j == gap])
        halo = halo + jnp.concatenate([part[:, span_of(g ^ gap)] for g in groups] + [part[:, DI:]], axis=1)
    grad_hidden, norm_sums = final(
        dpre, x_w, dpre_m, map_w, dstep_rows, step_w, halo, dn_z, hidden, cotangent, norm_gain[None], flag, width, (grad_x,)
    )
    grad_small = to_owners(to_owners(after(grad_small, norm_sums), "tensor", tp), "z", zn)[0]
    map_shard = jnp.concatenate([grad_small[:map_rows], grad_small[map_rows : 2 * map_rows]], axis=1)
    step_shard = grad_small[2 * map_rows :].reshape(strips, pitch, LANES)
    step_shard = jnp.concatenate([step_shard[i] for i in range(strips)], axis=1)[:heads, :width].T

    fold8 = lambda a: a.reshape(-1, 8, a.shape[-1]).sum(1)
    sums = jnp.concatenate([fold8(part) for part in sums], axis=1)
    taps = jnp.concatenate([regroup(sums[:5]), fold8(sums_m)], axis=1)
    per_head = jnp.stack(
        [
            jnp.sum(dstep, axis=1),
            jnp.sum(da * delta, axis=1) * rate[:, 0],
            jnp.sum(sums[5].reshape(H, HEAD), axis=1),
        ]
    )
    vector = [taps.reshape(-1), regroup(per_head).reshape(-1), regroup(fold8(gain_sums))[0]]
    vector = everywhere(jnp.concatenate(vector + [from_own(jnp.sum(norm_sums, axis=0))]))
    wide = DI + 2 * NS
    cuts = [KW * wide, wide, H, H, H, DI, D]
    parts, at = [], 0
    for count in cuts:
        parts.append(vector[at : at + count])
        at += count
    return (
        block_out,
        grad_hidden,
        parts[6],
        jnp.stack([grad_z, grad_x], axis=1).astype(F32),
        step_shard,
        map_shard,
        parts[0].reshape(KW, wide),
        parts[1],
        parts[2],
        parts[3],
        parts[4],
        parts[5],
        grad_out.astype(F32),
    )


def solution(mesh):
    dp, tp = mesh.shape["dp"], mesh.shape["tensor"]
    inner = Mesh(mesh.devices.reshape(dp // 2, 2, tp), ("z", "core", "tensor"))
    rows = P(("z", "core", "tensor"), None)
    split_dp = ("z", "core")
    head, step, out = P(split_dp, None, "tensor"), P(split_dp, "tensor"), P(split_dp, "tensor")
    whole = P()
    return jax.shard_map(
        functools.partial(shards, dp // 2, tp),
        mesh=inner,
        in_specs=(rows, whole, head, step, rows, whole, whole, whole, whole, whole, whole, out, rows),
        out_specs=(rows, rows, whole, head, step, rows, whole, whole, whole, whole, whole, whole, out),
        check_vma=False,
    )
```

```python
import functools
import math

import jax
import jax.numpy as jnp
from jax import lax
from jax.experimental import pallas as pl
from jax.experimental.pallas import tpu as pltpu
from jax.sharding import Mesh
from jax.sharding import PartitionSpec as P

D = 1536
H = 48
HEAD = 64
NS = 128
KW = 4
LEN = 2048
DI = 3072
EPSILON = 1e-05

CHUNK = 128
HALO = 16
TAIL = 112
LANES = 128
LOG2E = math.log2(math.e)
NEG = -1e30
VMEM = 58 * 2**20
F32 = jnp.float32
BF16 = jnp.bfloat16
PRECISE = lax.Precision.HIGHEST
NT = (((1,), (1,)), ((), ()))
TN = (((0,), (0,)), ((), ()))


def dot(a, b, dims=(((1,), (0,)), ((), ())), precision=None):
    return lax.dot_general(a, b, dims, precision=precision, preferred_element_type=F32)


def iota(shape, axis):
    return lax.broadcasted_iota(jnp.int32, shape, axis)


def first_half(shape):
    return iota(shape, len(shape) - 1) < HEAD


def mix(columns, head, rows=CHUNK):
    shape = (rows, LANES)
    left = jnp.broadcast_to(columns[:, head : head + 1], shape)
    right = jnp.broadcast_to(columns[:, head + 1 : head + 2], shape)
    return jnp.where(first_half(shape), left, right)


def mix_row(row, head):
    shape = (1, LANES)
    left = jnp.broadcast_to(row[:, head : head + 1], shape)
    right = jnp.broadcast_to(row[:, head + 1 : head + 2], shape)
    return jnp.where(first_half(shape), left, right)


def halves(block):
    left = first_half(block.shape)
    zero = jnp.zeros_like(block)
    return jnp.where(left, block, zero), jnp.where(left, zero, block)


def shifted(block):
    return [pltpu.roll(block, KW - 1 - tap, 0)[HALO:] if tap < KW - 1 else block[HALO:] for tap in range(KW)]


def conv_total(taps, weight, bias):
    total = bias + weight[KW - 1 : KW] * taps[KW - 1]
    for tap in range(KW - 1):
        total = total + weight[tap : tap + 1] * taps[tap]
    return total


def conv_pull(grad, after, weight):
    rows = grad.shape[0]
    ext = jnp.concatenate([grad, after], axis=0)
    out = weight[KW - 1 : KW] * grad
    for ahead in range(1, KW):
        out = out + weight[KW - 1 - ahead : KW - ahead] * pltpu.roll(ext, rows + 8 - ahead, 0)[:rows]
    return out


def fold(block):
    total = block[0:8]
    for at in range(8, block.shape[0], 8):
        total = total + block[at : at + 8]
    return total


def col_sum(block):
    return jnp.sum(block, axis=0, keepdims=True)


def cost(us):
    return pl.CostEstimate(flops=0, bytes_accessed=int(us), transcendentals=0)


def times(left_ref, blocks):
    total, at = None, 0
    for block in blocks:
        term = dot(left_ref[:, at : at + block.shape[0]], block[...])
        total = term if total is None else total + term
        at += block.shape[0]
    return total


def launch(kernel, args, wait, in_specs, **options):
    inputs = len(args)

    def body(*refs):
        kernel(*refs[:inputs], *refs[inputs + len(wait) :])

    in_specs = [*in_specs, *[pl.BlockSpec(memory_space=pl.ANY)] * len(wait)]
    return pl.pallas_call(body, in_specs=in_specs, **options)(*args, *wait)


def split(refs, counts):
    out, at = [], 0
    for count in counts:
        out.append(refs[at : at + count])
        at += count
    return out


def place_spec(place):
    array, index = place
    return pl.BlockSpec((D // 2, array.shape[1]), lambda *_: (index, 0), pipeline_mode=pl.Buffered(1))


def whole_spec(array):
    return pl.BlockSpec(array.shape, lambda *_: (0,) * array.ndim, pipeline_mode=pl.Buffered(1))


def prep_kernel(heads, pitch, n_ref, wm_ref, ws_ref, cw_ref, cb_ref, sb_ref, dl_ref, pre_ref, bc_ref, v_ref, c2_ref, cd_ref, c2t_ref, cdt_ref, wf_ref, ei_ref, tot_ref, c2_s, cd_s):
    rows = bc_ref.shape[0]
    groups = c2_ref.shape[0]
    count = rows // CHUNK
    pre_ref[...] = dot(n_ref[...], wm_ref[...]).astype(BF16)
    for at in range(count):
        for pair in range(2):
            cols = slice(pair * LANES, (pair + 1) * LANES)
            block = pre_ref[at * CHUNK : at * CHUNK + CHUNK + HALO, cols].astype(F32)
            total = conv_total(shifted(block), cw_ref[:, cols], cb_ref[:, cols])
            bc_ref[at * CHUNK : (at + 1) * CHUNK, cols] = (total * jax.nn.sigmoid(total)).astype(BF16)
    rate = -jnp.exp(dl_ref[...]) * LOG2E
    lower = (iota((CHUNK, CHUNK), 0) >= iota((CHUNK, CHUNK), 1)).astype(F32)
    raw = dot(n_ref[HALO:], ws_ref[...], NT)
    totals = []
    for at in range(count):
        here = slice(at * CHUNK, (at + 1) * CHUNK)
        v = raw[here] + sb_ref[...]
        delta = jnp.maximum(v, 0.0) + jnp.log1p(jnp.exp(-jnp.abs(v)))
        log_delta = jnp.where(v < -15.0, v, jnp.log(jnp.maximum(delta, 1e-30)))
        c2 = dot(lower, delta * rate, precision=PRECISE)
        cd = c2 - log_delta * LOG2E
        c2_s[here] = c2
        cd_s[here] = cd
        totals.append(c2[CHUNK - 1 : CHUNK])
        v_t, c2_t, cd_t = v.T, c2.T, cd.T
        for g in range(groups):
            own = slice(g * pitch, g * pitch + heads)
            c2_ref[g, here] = c2[:, own]
            cd_ref[g, here] = cd[:, own]
            v_ref[g, :, here] = v_t[own]
            c2t_ref[g, :, here] = c2_t[own]
            cdt_ref[g, :, here] = cd_t[own]
    before = jnp.zeros_like(totals[0])
    for at in range(count):
        here = slice(at * CHUNK, (at + 1) * CHUNK)
        to_here = jnp.exp2(before + c2_s[here])
        before = before + totals[at]
        for g in range(groups):
            ei_ref[g, here] = to_here[:, g * pitch : g * pitch + heads]
    tot_ref[...] = before
    after = jnp.zeros_like(totals[0])
    for at in range(count - 1, -1, -1):
        here = slice(at * CHUNK, (at + 1) * CHUNK)
        after = after + totals[at]
        to_end = jnp.exp2(after - cd_s[here])
        for g in range(groups):
            wf_ref[g, here] = to_end[:, g * pitch : g * pitch + heads]


def prep(normed, map_w, step_w, conv_w, conv_b, step_b, decay_log, groups, heads, pitch):
    rows = normed.shape[0] - HALO - TAIL
    cols = jax.ShapeDtypeStruct((groups, rows, heads), F32)
    flat = jax.ShapeDtypeStruct((groups, heads, rows), F32)
    return pl.pallas_call(
        functools.partial(prep_kernel, heads, pitch),
        out_shape=(
            jax.ShapeDtypeStruct((rows + HALO, 2 * NS), BF16),
            jax.ShapeDtypeStruct((rows, 2 * NS), BF16),
            flat,
            cols,
            cols,
            flat,
            flat,
            cols,
            cols,
            jax.ShapeDtypeStruct((1, LANES), F32),
        ),
        grid=(1,),
        in_specs=[pl.BlockSpec((rows + HALO, D), lambda i: (0, 0))]
        + [whole_spec(a) for a in (map_w, step_w, conv_w, conv_b, step_b, decay_log)],
        scratch_shapes=[pltpu.VMEM((rows, LANES), F32), pltpu.VMEM((rows, LANES), F32)],
        compiler_params=pltpu.CompilerParams(vmem_limit_bytes=VMEM),
        cost_estimate=cost(11),
        name="prep",
    )(normed, map_w, step_w, conv_w, conv_b, step_b, decay_log)


def proj_kernel(tile, count, n_ref, *refs):
    blocks = refs[:count]
    cw_ref, cb_ref, bc_ref, wf_ref, pre_ref, x_ref, s_ref, xw_s = refs[count:]
    rows, inner = x_ref.shape
    for at in range(0, inner, tile):
        cols = slice(at, at + tile)
        pre_ref[:, cols] = times(n_ref, [block.at[:, cols] for block in blocks]).astype(BF16)

        def chunk(k, carry, at=at):
            start = pl.multiple_of(k * CHUNK, CHUNK)
            weights = wf_ref[0, pl.ds(start, CHUNK)]
            for q in range(at // LANES, (at + tile) // LANES):
                lanes = slice(q * LANES, (q + 1) * LANES)
                block = pre_ref[pl.ds(start, CHUNK + HALO), lanes].astype(F32)
                total = conv_total(shifted(block), cw_ref[:, lanes], cb_ref[:, lanes])
                x = (total * jax.nn.sigmoid(total)).astype(BF16)
                x_ref[pl.ds(start, CHUNK), lanes] = x
                xw_s[pl.ds(start, CHUNK), lanes] = (x.astype(F32) * mix(weights, 2 * q)).astype(BF16)
            return carry

        lax.fori_loop(0, rows // CHUNK, chunk, 0)
    s_ref[...] = dot(bc_ref[:, :NS], xw_s[...], TN).astype(BF16)


def project(g, normed, blocks, conv_w, conv_b, bc, wf, wait=()):
    rows = normed.shape[0] - HALO - TAIL
    ext = rows + HALO
    inner = blocks[0][0].shape[1]
    heads = inner // HEAD
    tile = inner
    return launch(
        functools.partial(proj_kernel, tile, len(blocks)),
        (normed, *(array for array, _ in blocks), conv_w, conv_b, bc, wf,),
        wait,
        grid=(1,),
        in_specs=[
            pl.BlockSpec((ext, D), lambda i: (0, 0)),
            *map(place_spec, blocks),
            pl.BlockSpec((KW, inner), lambda i: (0, g)),
            pl.BlockSpec((1, inner), lambda i: (0, g)),
            whole_spec(bc),
            pl.BlockSpec((1, rows, heads), lambda i: (g, 0, 0)),
        ],
        out_specs=[
            pl.BlockSpec((ext, inner), lambda i: (0, 0)),
            pl.BlockSpec((rows, inner), lambda i: (0, 0)),
            pl.BlockSpec((NS, inner), lambda i: (0, 0)),
        ],
        out_shape=(
            jax.ShapeDtypeStruct((ext, inner), BF16),
            jax.ShapeDtypeStruct((rows, inner), BF16),
            jax.ShapeDtypeStruct((NS, inner), BF16),
        ),
        scratch_shapes=[pltpu.VMEM((rows, inner), BF16)],
        compiler_params=pltpu.CompilerParams(vmem_limit_bytes=VMEM),
        cost_estimate=cost(10),
        name="project",
    )


def product_kernel(count, n_ref, *refs):
    refs[count][...] = times(n_ref, refs[:count]).astype(BF16)


def product(left, blocks, wait=()):
    rows = left.shape[0]
    inner = blocks[0][0].shape[1]
    tile = 256 if inner % 256 == 0 else LANES
    return launch(
        functools.partial(product_kernel, len(blocks)),
        (left, *(array for array, _ in blocks),),
        wait,
        grid=(inner // tile,),
        in_specs=[whole_spec(left), *(pl.BlockSpec((D // 2, tile), functools.partial(lambda index, j: (index, j), index)) for _, index in blocks)],
        out_specs=pl.BlockSpec((rows, tile), lambda j: (0, j)),
        out_shape=jax.ShapeDtypeStruct((rows, inner), BF16),
        compiler_params=pltpu.CompilerParams(vmem_limit_bytes=VMEM),
        cost_estimate=cost(4),
        name="product",
    )


def scan_kernel(x_ref, bc_ref, c2_ref, cd_ref, cdt_ref, s0_ref, skip_ref, y_ref, sin_ref, state, ya_s, xw_s):
    rows, inner = x_ref.shape
    heads = inner // HEAD
    causal = iota((CHUNK, CHUNK), 0) >= iota((CHUNK, CHUNK), 1)
    state[...] = s0_ref[...].astype(F32)

    def chunk(k, carry):
        start = pl.multiple_of(k * CHUNK, CHUNK)
        here = pl.ds(start, CHUNK)
        in_map, out_map = bc_ref[here, :NS], bc_ref[here, NS:]
        c2, cd = c2_ref[0, here], cd_ref[0, here]
        cd_t = cdt_ref[0, :, here]
        last = c2[CHUNK - 1 : CHUNK]
        from_start, to_end, whole = jnp.exp2(c2), jnp.exp2(last - cd), jnp.exp2(last)
        held = state[...].astype(BF16)
        sin_ref[k] = held
        ya_s[...] = dot(out_map, held)
        scores = dot(out_map, in_map, NT)
        for q in range(heads // 2):
            lanes = slice(q * LANES, (q + 1) * LANES)
            x = x_ref[here, lanes]
            x32 = x.astype(F32)
            weights = []
            for head in (2 * q, 2 * q + 1):
                spread = c2[:, head : head + 1] - cd_t[head : head + 1]
                weights.append((scores * jnp.exp2(jnp.where(causal, spread, NEG))).astype(BF16))
            within = dot(jnp.concatenate(weights, axis=1), jnp.concatenate(halves(x), axis=0))
            y = within + mix(from_start, 2 * q) * ya_s[:, lanes] + skip_ref[:, lanes] * x32
            y_ref[here, lanes] = y.astype(BF16)
            xw_s[:, lanes] = (x32 * mix(to_end, 2 * q)).astype(BF16)
            state[:, lanes] = state[:, lanes] * mix_row(whole, 2 * q)
        state[...] += dot(in_map, xw_s[...], TN)
        return carry

    lax.fori_loop(0, rows // CHUNK, chunk, 0, unroll=2)


def scan(g, x, bc, c2, cd, cdt, state, skip, wait=()):
    rows = x.shape[0]
    heads = c2.shape[2]
    inner = heads * HEAD
    count = rows // CHUNK
    return launch(
        scan_kernel,
        (x, bc, c2, cd, cdt, state, skip,),
        wait,
        grid=(1,),
        in_specs=[
            whole_spec(x),
            whole_spec(bc),
            pl.BlockSpec((1, rows, heads), lambda i: (g, 0, 0)),
            pl.BlockSpec((1, rows, heads), lambda i: (g, 0, 0)),
            pl.BlockSpec((1, heads, rows), lambda i: (g, 0, 0)),
            whole_spec(state),
            pl.BlockSpec((1, inner), lambda i: (0, g)),
        ],
        out_specs=[
            pl.BlockSpec((rows, inner), lambda i: (0, 0)),
            pl.BlockSpec((count, NS, inner), lambda i: (0, 0, 0)),
        ],
        out_shape=(
            jax.ShapeDtypeStruct((rows, inner), BF16),
            jax.ShapeDtypeStruct((count, NS, inner), BF16),
        ),
        scratch_shapes=[
            pltpu.VMEM((NS, inner), F32),
            pltpu.VMEM((CHUNK, inner), F32),
            pltpu.VMEM((CHUNK, inner), BF16),
        ],
        compiler_params=pltpu.CompilerParams(vmem_limit_bytes=VMEM),
        cost_estimate=cost(9),
        name="scan",
    )


def gate_kernel(groups, width, out_counts, z_counts, *refs):
    ys, zs, outs_w, zs_w, rest, scs, dys, dzs, us, tail = split(
        refs, (groups, groups, sum(out_counts), sum(z_counts), 6, groups, groups, groups, groups, 8)
    )
    outs_w, zs_w = split(outs_w, out_counts), split(zs_w, z_counts)
    cot_ref, hid_ref, gain_ref, bc_ref, ei_ref, flag_ref = rest
    out_ref, dn_ref, gg_ref, gs_s, ga_s, de_s, sum_s, u_s = tail
    rows, inner = ys[0].shape
    tiles = inner // LANES

    @pl.when(pl.program_id(0) == 0)
    def _():
        gg_ref[...] = jnp.zeros_like(gg_ref)
        u_s[...] = jnp.zeros_like(u_s)

    for g in range(groups):
        gs_s[:, g * inner : (g + 1) * inner] = times(cot_ref, outs_w[g])
    for part in range(0, rows, CHUNK):
        here = slice(part, part + CHUNK)
        squares = jnp.zeros((CHUNK, LANES), F32)
        dots = jnp.zeros((CHUNK, LANES), F32)
        for g in range(groups):

            def measure(c, sums, g=g):
                lanes = pl.ds(pl.multiple_of(c * LANES, LANES), LANES)
                wide = pl.ds(pl.multiple_of(g * inner + c * LANES, LANES), LANES)
                z = zs[g][here, lanes].astype(F32)
                gated = ys[g][here, lanes].astype(F32) * (z * jax.nn.sigmoid(z))
                ga_s[here, wide] = gated
                return sums[0] + gated * gated, sums[1] + gs_s[here, wide] * gain_ref[:, wide] * gated

            squares, dots = lax.fori_loop(0, tiles, measure, (squares, dots), unroll=True)
        inverse = lax.rsqrt(jnp.sum(squares, axis=1, keepdims=True) / DI + EPSILON)
        pull = inverse * inverse * inverse * (jnp.sum(dots, axis=1, keepdims=True) / DI)
        inverse = jnp.broadcast_to(inverse, (CHUNK, LANES))
        pull = jnp.broadcast_to(pull, (CHUNK, LANES))
        for g in range(groups):
            for c in range(tiles):
                lanes = slice(c * LANES, (c + 1) * LANES)
                wide = slice(g * inner + c * LANES, g * inner + (c + 1) * LANES)
                z = zs[g][here, lanes].astype(F32)
                sig = jax.nn.sigmoid(z)
                gated = ga_s[here, wide]
                weighted = gs_s[here, wide]
                unit = gated * inverse
                gain = gain_ref[:, wide]
                scs[g][here, lanes] = (unit * gain).astype(BF16)
                gg_ref[:, wide] += fold(weighted * unit)
                grad = inverse * weighted * gain - gated * pull
                dy = (grad * (z * sig)).astype(BF16)
                dys[g][here, lanes] = dy
                slope = sig * (1.0 + z * (1.0 - sig))
                dzs[g][here, lanes] = (grad * ys[g][here, lanes].astype(F32) * slope).astype(BF16)
                de_s[here, wide] = (dy.astype(F32) * mix(ei_ref[g, here], 2 * c)).astype(BF16)
    for g in range(groups):
        cols = slice(g * inner, (g + 1) * inner)
        u_s[:, cols] += dot(bc_ref[:, NS:], de_s[:, cols], TN)
        us[g][...] = u_s[:, cols].astype(BF16)
    back_times(sum_s, scs, outs_w, hid_ref)
    natural(out_ref, sum_s, flag_ref, width)
    back_times(dn_ref, dzs, zs_w, None)


def natural(out_ref, source_ref, flag_ref, width):
    first = flag_ref[0:1, 0:1] == 0.0
    half = source_ref.shape[1] // 2
    for z in range(half // width):
        own = source_ref[:, z * width : (z + 1) * width]
        other = source_ref[:, half + z * width : half + (z + 1) * width]
        pair = jnp.concatenate([jnp.where(first, own, other), jnp.where(first, other, own)], axis=1)
        out_ref[:, 2 * z * width : 2 * (z + 1) * width] = pair.astype(out_ref.dtype)


def back_times(out_ref, lefts, weights, base_ref):
    cuts = sorted({0} | {sum(b.shape[0] for b in blocks[: i + 1]) for blocks in weights for i in range(len(blocks))})
    for low, high in zip(cuts[:-1], cuts[1:]):
        total = None if base_ref is None else base_ref[:, low:high].astype(F32)
        for left, blocks in zip(lefts, weights):
            at = 0
            for block in blocks:
                if at <= low < at + block.shape[0]:
                    term = dot(left[...], block[low - at : high - at], NT)
                    total = term if total is None else total + term
                at += block.shape[0]
        out_ref[:, low:high] = total.astype(out_ref.dtype)


def arrays(places):
    return [array for array, _ in flat(places)]


def flat(lists):
    return [item for items in lists for item in items]


def gate(ys, zs, outs_w, zs_w, cot, hidden, gain, bc, ei, flag, width):
    groups = len(ys)
    rows, inner = ys[0].shape
    heads = inner // HEAD
    tile = 256
    wide = groups * inner
    row = lambda i: (i, 0)
    fixed = lambda i: (0, 0)
    group = [pl.BlockSpec((tile, inner), row)] * groups
    group_shape = [jax.ShapeDtypeStruct((rows, inner), BF16)] * groups
    out = pl.pallas_call(
        functools.partial(gate_kernel, groups, width, tuple(map(len, outs_w)), tuple(map(len, zs_w))),
        grid=(rows // tile,),
        in_specs=[
            *group,
            *group,
            *map(place_spec, flat(outs_w)),
            *map(place_spec, flat(zs_w)),
            pl.BlockSpec((tile, D), row),
            pl.BlockSpec((tile, D), row),
            pl.BlockSpec((1, wide), fixed),
            pl.BlockSpec((tile, 2 * NS), row),
            pl.BlockSpec((groups, tile, heads), lambda i: (0, i, 0)),
            whole_spec(flag),
        ],
        out_specs=[
            *group,
            *group,
            *group,
            *[pl.BlockSpec((NS, inner), fixed)] * groups,
            pl.BlockSpec((tile, D), row),
            pl.BlockSpec((tile, D), row),
            pl.BlockSpec((8, wide), fixed),
        ],
        out_shape=(
            *group_shape,
            *group_shape,
            *group_shape,
            *[jax.ShapeDtypeStruct((NS, inner), BF16)] * groups,
            jax.ShapeDtypeStruct((rows, D), BF16),
            jax.ShapeDtypeStruct((rows, D), F32),
            jax.ShapeDtypeStruct((8, wide), F32),
        ),
        scratch_shapes=[
            pltpu.VMEM((tile, wide), F32),
            pltpu.VMEM((tile, wide), F32),
            pltpu.VMEM((tile, wide), BF16),
            pltpu.VMEM((tile, D), F32),
            pltpu.VMEM((NS, wide), F32),
        ],
        compiler_params=pltpu.CompilerParams(vmem_limit_bytes=VMEM),
        cost_estimate=cost(55),
        name="gate",
    )(*ys, *zs, *arrays(outs_w), *arrays(zs_w), cot, hidden, gain, bc, ei, flag)
    return split(out, (groups, groups, groups, groups)) + list(out[4 * groups :])


def back_kernel(pre_ref, dy_ref, bc_ref, c2_ref, cd_ref, c2t_ref, sin_ref, u_ref, skip_ref, cw_ref, cb_ref, dpre_ref, dbc_ref, acc_ref, q_ref, da_ref, state, next_s, x_s, slope_s, de_s, xw_s, ya_s, bs_s):
    rows, inner = dy_ref.shape
    heads = inner // HEAD
    count = rows // CHUNK
    square = (CHUNK, CHUNK)
    flipped = iota(square, 1) >= iota(square, 0)
    later = (iota(square, 0) >= iota(square, 1)).astype(F32)
    earlier = (iota(square, 0) < iota(square, 1)).astype(F32)
    state[...] = u_ref[...].astype(F32)
    next_s[...] = jnp.zeros_like(next_s)
    acc_ref[...] = jnp.zeros_like(acc_ref)

    def chunk(step, carry):
        k = count - 1 - step
        start = pl.multiple_of(k * CHUNK, CHUNK)
        here = pl.ds(start, CHUNK)
        in_map, out_map = bc_ref[here, :NS], bc_ref[here, NS:]
        c2, cd = c2_ref[0, here], cd_ref[0, here]
        c2_t = c2t_ref[0, :, here]
        last = c2[CHUNK - 1 : CHUNK]
        from_start, to_end, whole = jnp.exp2(c2), jnp.exp2(last - cd), jnp.exp2(last)
        for q in range(heads // 2):
            lanes = slice(q * LANES, (q + 1) * LANES)
            block = pre_ref[pl.ds(start, CHUNK + HALO), lanes].astype(F32)
            total = conv_total(shifted(block), cw_ref[:, lanes], cb_ref[:, lanes])
            sig = jax.nn.sigmoid(total)
            x = (total * sig).astype(BF16)
            x_s[:, lanes] = x
            slope_s[:, lanes] = sig * (1.0 + total * (1.0 - sig))
            de_s[:, lanes] = (dy_ref[here, lanes].astype(F32) * mix(from_start, 2 * q)).astype(BF16)
            xw_s[:, lanes] = (x.astype(F32) * mix(to_end, 2 * q)).astype(BF16)
        held = sin_ref[k]
        after = state[...]
        after_low = after.astype(BF16)
        ya_s[...] = dot(out_map, held)
        bs_s[...] = dot(in_map, after_low)
        grad_out = dot(de_s[...], held, NT)
        grad_in = dot(xw_s[...], after_low, NT)
        through = col_sum(after * held.astype(F32))
        state[...] = dot(out_map, de_s[...], TN)
        scores = dot(in_map, out_map, NT)
        grad_scores = jnp.zeros(square, F32)
        rc_rows, st_rows, q_rows, tails = [], [], [], []
        for q in range(heads // 2):
            lanes = slice(q * LANES, (q + 1) * LANES)
            x, dy = x_s[:, lanes], dy_ref[here, lanes]
            x_parts, dy_parts = halves(x), halves(dy)
            weights, row_sums = [], []
            for side, head in enumerate((2 * q, 2 * q + 1)):
                spread = c2_t[head : head + 1] - cd[:, head : head + 1]
                decay = jnp.exp2(jnp.where(flipped, spread, NEG))
                weight = (scores * decay).astype(BF16)
                weights.append(weight)
                grad_weight = dot(x_parts[side], dy, NT)
                grad_scores = grad_scores + grad_weight * decay
                row_sums.append(col_sum(weight.astype(F32) * grad_weight))
            dx_in = dot(jnp.concatenate(weights, axis=1), jnp.concatenate(dy_parts, axis=0))
            dx_out = bs_s[:, lanes] * mix(to_end, 2 * q)
            x32, dy32 = x.astype(F32), dy.astype(F32)
            inside = x32 * dx_in
            outside = x32 * dx_out
            crossed = (de_s[:, lanes].astype(F32) * ya_s[:, lanes] - inside).T
            outside_t = outside.T
            both_t = (inside + outside).T
            through_q = through[:, lanes] * mix_row(whole, 2 * q)
            for side in range(2):
                part = slice(side * HEAD, (side + 1) * HEAD)
                rc_rows.append(row_sums[side] + col_sum(crossed[part]))
                st_rows.append(col_sum(outside_t[part]))
                q_rows.append(col_sum(both_t[part]))
                own = first_half((1, LANES)) if side == 0 else ~first_half((1, LANES))
                tails.append(jnp.sum(jnp.where(own, through_q, 0.0), axis=1, keepdims=True))
            state[:, lanes] += after[:, lanes] * mix_row(whole, 2 * q)
            grad = (dx_in + dx_out + skip_ref[:, lanes] * dy32) * slope_s[:, lanes]
            taps = shifted(pre_ref[pl.ds(start, CHUNK + HALO), lanes].astype(F32))
            for tap in range(KW):
                acc_ref[tap * 8 : tap * 8 + 8, lanes] += fold(grad * taps[tap])
            acc_ref[32:40, lanes] += fold(grad)
            acc_ref[40:48, lanes] += fold(dy32 * x32)
            dpre = conv_pull(grad, next_s[:, lanes], cw_ref[:, lanes])
            dpre_ref[pl.ds(pl.multiple_of(start + HALO, HALO), CHUNK), lanes] = dpre.astype(BF16)
            next_s[:, lanes] = grad[0:8]
        low_scores = grad_scores.astype(BF16)
        dbc_ref[here, :NS] = grad_in + dot(low_scores, out_map)
        dbc_ref[here, NS:] = grad_out + dot(low_scores, in_map, TN)
        da = dot(jnp.concatenate(rc_rows, axis=0), later, precision=PRECISE)
        da = da + dot(jnp.concatenate(st_rows, axis=0), earlier, precision=PRECISE)
        da_ref[0, :, here] = da + jnp.concatenate(tails, axis=0)
        q_ref[0, :, here] = jnp.concatenate(q_rows, axis=0)
        return carry

    lax.fori_loop(0, count, chunk, 0, unroll=2)
    for q in range(heads // 2):
        lanes = slice(q * LANES, (q + 1) * LANES)
        empty = jnp.zeros((HALO, LANES), F32)
        dpre_ref[0:HALO, lanes] = conv_pull(empty, next_s[:, lanes], cw_ref[:, lanes]).astype(BF16)
    dpre_ref[HALO + rows :] = jnp.zeros((TAIL, inner), BF16)


def back(g, pre, dy, bc, c2, cd, c2t, states, pull, skip, conv_w, conv_b, wait=()):
    ext = pre.shape[0]
    rows = ext - HALO
    heads = c2.shape[2]
    inner = heads * HEAD
    count = rows // CHUNK
    return launch(
        back_kernel,
        (pre, dy, bc, c2, cd, c2t, states, pull, skip, conv_w, conv_b,),
        wait,
        grid=(1,),
        in_specs=[
            whole_spec(pre),
            whole_spec(dy),
            whole_spec(bc),
            pl.BlockSpec((1, rows, heads), lambda i: (g, 0, 0)),
            pl.BlockSpec((1, rows, heads), lambda i: (g, 0, 0)),
            pl.BlockSpec((1, heads, rows), lambda i: (g, 0, 0)),
            whole_spec(states),
            whole_spec(pull),
            pl.BlockSpec((1, inner), lambda i: (0, g)),
            pl.BlockSpec((KW, inner), lambda i: (0, g)),
            pl.BlockSpec((1, inner), lambda i: (0, g)),
        ],
        out_specs=[
            pl.BlockSpec((ext + TAIL, inner), lambda i: (0, 0)),
            pl.BlockSpec((rows, 2 * NS), lambda i: (0, 0)),
            pl.BlockSpec((48, inner), lambda i: (0, 0)),
            pl.BlockSpec((1, heads, rows), lambda i: (0, 0, 0)),
            pl.BlockSpec((1, heads, rows), lambda i: (0, 0, 0)),
        ],
        out_shape=(
            jax.ShapeDtypeStruct((ext + TAIL, inner), BF16),
            jax.ShapeDtypeStruct((rows, 2 * NS), F32),
            jax.ShapeDtypeStruct((48, inner), F32),
            jax.ShapeDtypeStruct((1, heads, rows), F32),
            jax.ShapeDtypeStruct((1, heads, rows), F32),
        ),
        scratch_shapes=[
            pltpu.VMEM((NS, inner), F32),
            pltpu.VMEM((8, inner), F32),
            pltpu.VMEM((CHUNK, inner), BF16),
            pltpu.VMEM((CHUNK, inner), F32),
            pltpu.VMEM((CHUNK, inner), BF16),
            pltpu.VMEM((CHUNK, inner), BF16),
            pltpu.VMEM((CHUNK, inner), F32),
            pltpu.VMEM((CHUNK, inner), F32),
        ],
        compiler_params=pltpu.CompilerParams(vmem_limit_bytes=VMEM),
        cost_estimate=cost(18),
        name="back",
    )


def map_back_kernel(pre_ref, grad_ref, cw_ref, cb_ref, dpre_ref, acc_ref, next_s):
    rows, wide = grad_ref.shape
    count = rows // CHUNK
    next_s[...] = jnp.zeros_like(next_s)
    acc_ref[...] = jnp.zeros_like(acc_ref)
    for k in range(count - 1, -1, -1):
        start = k * CHUNK
        for q in range(wide // LANES):
            lanes = slice(q * LANES, (q + 1) * LANES)
            taps = shifted(pre_ref[start : start + CHUNK + HALO, lanes].astype(F32))
            total = conv_total(taps, cw_ref[:, lanes], cb_ref[:, lanes])
            sig = jax.nn.sigmoid(total)
            grad = grad_ref[start : start + CHUNK, lanes] * (sig * (1.0 + total * (1.0 - sig)))
            for tap in range(KW):
                acc_ref[tap * 8 : tap * 8 + 8, lanes] += fold(grad * taps[tap])
            acc_ref[32:40, lanes] += fold(grad)
            dpre = conv_pull(grad, next_s[:, lanes], cw_ref[:, lanes])
            dpre_ref[start + HALO : start + HALO + CHUNK, lanes] = dpre.astype(BF16)
            next_s[:, lanes] = grad[0:8]
    for q in range(wide // LANES):
        lanes = slice(q * LANES, (q + 1) * LANES)
        empty = jnp.zeros((HALO, LANES), F32)
        dpre_ref[0:HALO, lanes] = conv_pull(empty, next_s[:, lanes], cw_ref[:, lanes]).astype(BF16)
    dpre_ref[HALO + rows :] = jnp.zeros((TAIL, wide), BF16)


def map_back(pre, grad, conv_w, conv_b):
    return pl.pallas_call(
        map_back_kernel,
        out_shape=(jax.ShapeDtypeStruct((pre.shape[0] + TAIL, pre.shape[1]), BF16), jax.ShapeDtypeStruct((40, pre.shape[1]), F32)),
        scratch_shapes=[pltpu.VMEM((8, pre.shape[1]), F32)],
        compiler_params=pltpu.CompilerParams(vmem_limit_bytes=VMEM),
        cost_estimate=cost(4),
        name="map_back",
    )(pre, grad, conv_w, conv_b)


def final_kernel(groups, width, counts, *refs):
    ds, ws, rest = split(refs, (groups, sum(counts), 15))
    ws = split(ws, counts)
    dm_ref, wm_ref, dt_ref, wt_ref, halo_ref, dn_ref, hid_ref, cot_ref, gain_ref, flag_ref, gh_ref, gn_ref, left_s, total_s, grad_s = rest
    rows, wide = hid_ref.shape
    inner = ds[0].shape[1]
    start = pl.multiple_of(pl.program_id(0) * rows, HALO)

    @pl.when(pl.program_id(0) == 0)
    def _():
        gn_ref[...] = jnp.zeros_like(gn_ref)

    own = pl.ds(pl.multiple_of(start + HALO, HALO), rows)
    for g in range(groups):
        left_s[:, g * inner : (g + 1) * inner] = ds[g][own]
    left_s[:, groups * inner :] = dm_ref[own]

    @pl.when(pl.program_id(0) == pl.num_programs(0) - 1)
    def _():
        last = slice(rows - HALO, rows)
        left_s[last] = (left_s[last].astype(F32) + halo_ref[...].astype(F32)).astype(BF16)

    lefts = [left_s.at[:, g * inner : (g + 1) * inner] for g in range(groups)]
    lefts += [left_s.at[:, groups * inner :]]
    back_times(total_s, lefts, ws + [[wm_ref]], dn_ref)
    total_s[...] += dot(dt_ref[...], wt_ref[...])
    squares = jnp.zeros((rows, 1), F32)
    for c in range(wide // LANES):
        lanes = slice(c * LANES, (c + 1) * LANES)
        tokens = hid_ref[:, lanes].astype(F32)
        squares = squares + jnp.sum(tokens * tokens, axis=1, keepdims=True)
    inverse = lax.rsqrt(squares / wide + EPSILON)
    dots = jnp.zeros((rows, 1), F32)
    for c in range(wide // LANES):
        lanes = slice(c * LANES, (c + 1) * LANES)
        tokens = hid_ref[:, lanes].astype(F32)
        dots = dots + jnp.sum(total_s[:, lanes] * gain_ref[:, lanes] * tokens, axis=1, keepdims=True)
    pull = inverse * inverse * inverse * (dots / wide)
    for c in range(wide // LANES):
        lanes = slice(c * LANES, (c + 1) * LANES)
        tokens = hid_ref[:, lanes].astype(F32)
        grad = total_s[:, lanes]
        grad_s[:, lanes] = cot_ref[:, lanes].astype(F32) + inverse * (grad * gain_ref[:, lanes]) - tokens * pull
        gn_ref[:, lanes] += fold(grad * tokens * inverse)
    natural(gh_ref, grad_s, flag_ref, width)


def final(ds, ws, dm, wm, dt, wt, halo, dn, hidden, cot, gain, flag, width, wait=()):
    groups = len(ds)
    rows = hidden.shape[0]
    inner = ds[0].shape[1]
    tile = 256
    row = lambda i: (i, 0)
    fixed = lambda i: (0, 0)
    return launch(
        functools.partial(final_kernel, groups, width, tuple(map(len, ws))),
        (*ds, *arrays(ws), dm, wm, dt, wt, halo, dn, hidden, cot, gain, flag,),
        wait,
        grid=(rows // tile,),
        in_specs=[
            *map(whole_spec, ds),
            *map(place_spec, flat(ws)),
            whole_spec(dm),
            whole_spec(wm),
            pl.BlockSpec((tile, LANES), row),
            whole_spec(wt),
            whole_spec(halo),
            pl.BlockSpec((tile, D), row),
            pl.BlockSpec((tile, D), row),
            pl.BlockSpec((tile, D), row),
            pl.BlockSpec((1, D), fixed),
            whole_spec(flag),
        ],
        out_specs=[pl.BlockSpec((tile, D), row), pl.BlockSpec((8, D), fixed)],
        out_shape=(jax.ShapeDtypeStruct((rows, D), F32), jax.ShapeDtypeStruct((8, D), F32)),
        scratch_shapes=[pltpu.VMEM((tile, groups * inner + 2 * NS), BF16), pltpu.VMEM((tile, D), F32), pltpu.VMEM((tile, D), F32)],
        compiler_params=pltpu.CompilerParams(vmem_limit_bytes=VMEM),
        cost_estimate=cost(20),
        name="final",
    )


def across(value, axis, size, bit):
    return lax.ppermute(value, axis, [(i, i ^ bit) for i in range(size)])


def bits(size):
    return [1 << i for i in range(size.bit_length() - 1)]


def after(value, *others):
    return lax.optimization_barrier((value, others))[0]


def shards(
    zn,
    tp,
    hidden,
    norm_gain,
    head_weight,
    step_weight,
    map_weight,
    conv_weight,
    conv_bias,
    step_bias,
    decay_log,
    skip_gain,
    gate_gain,
    out_weight,
    cotangent,
):
    rows = hidden.shape[0]
    width, _, inner = head_weight.shape
    heads = step_weight.shape[1]
    span = LEN // rows
    forward = [(i, i + 1) for i in range(tp - 1) if (i + 1) % span]
    backward = [(j, i) for i, j in forward]
    core, z_me, t_me = (lax.axis_index(name) for name in ("core", "z", "tensor"))
    swap = lambda value: across(value, "core", 2, 1)
    near = lambda value, bit: across(value, "tensor", tp, bit)
    steps = [("z", zn, b) for b in bits(zn)] + [("tensor", tp, b) for b in bits(tp)] + [("core", 2, 1)]
    half = zn * width // 2

    def to_own(array):
        parts = array.reshape(array.shape[:-1] + (zn, 2, width))
        first, second = parts[..., 0, :], parts[..., 1, :]
        both = [jnp.where(core == 0, first, second), jnp.where(core == 0, second, first)]
        return jnp.concatenate([a.reshape(array.shape[:-1] + (zn * width,)) for a in both], axis=-1)

    def from_own(array):
        lead = array.shape[:-1]
        own, other = (array[..., i * zn * width : (i + 1) * zn * width].reshape(lead + (zn, 1, width)) for i in (0, 1))
        both = [jnp.where(core == 0, own, other), jnp.where(core == 0, other, own)]
        return jnp.concatenate(both, axis=-2).reshape(lead + (D,))

    groups_now = jnp.arange(tp) ^ t_me
    z_now = jnp.arange(zn) ^ z_me
    core_now = jnp.arange(2)[:, None, None] * (zn * tp)
    by_place = (core_now + groups_now[None, None] * zn + z_now[None, :, None]).reshape(-1)
    by_group = (core_now + jnp.arange(tp)[None, None] * zn + z_now[None, :, None]).reshape(-1)

    def regroup(array):
        lead, last = array.shape[:-1], array.shape[-1]
        return jnp.take(array.reshape(lead + (tp, last // tp)), groups_now, axis=-2).reshape(array.shape)

    def send_own(mine):
        return [near(mine, 1), near(mine, 2)] if tp == 4 else [near(mine, g) for g in range(1, tp)]

    def send_far(got):
        if tp != 4:
            return [], []
        halves_now = [got[0][:half], got[1][half:]]
        return halves_now, [near(halves_now[0], 2), near(halves_now[1], 1)]

    def places(mine, mine_other, rest):
        other = swap(rest)
        return [[(mine, 0), (mine_other, 0)]] + [[(rest, g), (other, g)] for g in range(tp - 1)]

    coming = []

    class Scatter:
        def __init__(self, left, via):
            self.left, self.via, self.others = left, via, [None] * tp
            self.add = [[] for _ in range(tp)]

        def away(self, right):
            return dot(self.left[:, zn * width :], right, TN).astype(BF16)

        def swap(self, g, right):
            self.others[g] = swap(self.away(right))
            return self.others[g]

        def partial(self, g, right):
            total = dot(self.left[:, : zn * width], right, TN) + self.others[g].astype(F32)
            for term in self.add[g]:
                total = total + term.astype(F32)
            return total.astype(BF16)

        def send(self, g, right):
            part = self.partial(g, right)
            if tp == 4 and g == 3:
                got, at = near(part, 3 - self.via), self.via
            else:
                got, at = near(part, g), 0
            self.add[at].append(got)
            coming.append(got)
            return part

        def finish(self, right):
            return self.partial(0, right)

    def scatter(total):
        return lax.psum_scatter(total, "z", scatter_dimension=0, tiled=True)

    def everywhere(vector):
        for axis, size in (("z", zn), ("tensor", tp), ("core", 2)):
            if size == 4:
                one, two, three = (across(vector, axis, size, gap) for gap in (1, 2, 3))
                vector = (vector + one) + (two + three)
            else:
                for bit in bits(size):
                    vector = vector + across(vector, axis, size, bit)
        return vector

    flag = jnp.full((8, LANES), core, F32)
    shard_x, shard_z = head_weight[:, 1], head_weight[:, 0]
    x_mine = lax.all_gather(shard_x, "z", axis=0, tiled=True)
    z_mine = lax.all_gather(after(shard_z, shard_x), "z", axis=0, tiled=True)
    out_mine = lax.all_gather(after(out_weight, shard_z), "z", axis=0, tiled=True)

    map_rows = map_weight.shape[0]
    pitch = -(-heads // 16) * 16
    strips = -(-width // LANES)
    pad_step = lambda a: jnp.pad(a, ((0, 0),) * (a.ndim - 2) + ((0, pitch - heads), (0, strips * LANES - width)))
    strip = lambda a: jnp.concatenate([a[..., i * LANES : (i + 1) * LANES] for i in range(a.shape[-1] // LANES)], axis=-2)
    small = jnp.concatenate([strip(map_weight), strip(pad_step(step_weight.T))], axis=0)[None]
    depth = small.shape[1]
    for axis, count, bit in steps:
        small = jnp.concatenate([small, across(small, axis, count, bit)], axis=0)
    pick = lambda a, index, axis: jnp.take(a, index, axis=axis, mode="clip")
    maps = pick(small[:, : 2 * map_rows], by_place, 0)
    map_w = jnp.concatenate([maps[:, i * map_rows : (i + 1) * map_rows].reshape(D, LANES) for i in (0, 1)], axis=1)
    steps_w = pick(small[:, 2 * map_rows :], by_group, 0).reshape(2, zn, tp, strips, pitch, LANES)
    steps_w = jnp.transpose(steps_w, (2, 4, 0, 1, 3, 5)).reshape(tp * pitch, 2 * zn, strips * LANES)
    step_w = steps_w[..., :width].reshape(tp * pitch, D)
    step_w = jnp.pad(step_w, ((0, LANES - tp * pitch), (0, 0)))

    x_mine = after(x_mine, map_w, step_w)
    x_own_other, x_near = swap(x_mine), send_own(x_mine)
    hidden, cotangent, norm_gain, conv_weight, conv_bias, step_bias, decay_log, skip_gain, gate_gain = after(
        (hidden, cotangent, norm_gain, conv_weight, conv_bias, step_bias, decay_log, skip_gain, gate_gain), map_w, step_w
    )
    hidden, norm_gain = to_own(hidden), to_own(norm_gain)
    halo = lax.ppermute(hidden[rows - HALO :], "tensor", forward)
    tokens = jnp.concatenate([halo, hidden], axis=0).astype(F32)
    inverse = lax.rsqrt(jnp.mean(tokens * tokens, axis=-1, keepdims=True) + EPSILON)
    normed_ext = jnp.pad((tokens * inverse * norm_gain).astype(BF16), ((0, TAIL), (0, 0)))
    normed = normed_ext[HALO : HALO + rows]

    def per_pitch(a):
        a = jnp.pad(a.reshape(tp, heads), ((0, 0), (0, pitch - heads))).reshape(1, tp * pitch)
        return jnp.pad(a, ((0, 0), (0, LANES - tp * pitch)))

    skip_gain, gate_gain, cotangent_late = after((skip_gain, gate_gain, cotangent), normed_ext)
    conv_x, bias_x = regroup(conv_weight[:, :DI]), regroup(conv_bias[None, :DI])
    conv_m, bias_m = conv_weight[:, DI:], conv_bias[None, DI:]
    step_bias, decay_log = (regroup(a[None]) for a in (step_bias, decay_log))
    pre_m, bc, v, c2, cd, c2t, cdt, wf, ei, total = prep(
        normed_ext, after(map_w, x_own_other, conv_x, bias_x), step_w, conv_m, bias_m, per_pitch(step_bias), per_pitch(decay_log), tp, heads, pitch
    )
    total = total[:, : tp * pitch].reshape(tp, pitch)[:, :heads].reshape(1, H)
    device_decay = jnp.repeat(jnp.exp2(total), HEAD, axis=1)
    groups = range(tp)
    span_of = lambda g: slice(g * inner, (g + 1) * inner)

    def pass_on(value, pairs, g):
        received = {}
        for gap in sorted({i ^ j for i, j in pairs}):
            received[g ^ gap] = lax.ppermute(value, "tensor", [(i, j) for i, j in pairs if i ^ j == gap])
        return received

    def chain(local, first, pairs):
        passed = gathered(first)
        for _ in range(span - 2):
            sums = [local[g].astype(F32) + device_decay[:, span_of(g)] * passed[g].astype(F32) for g in groups]
            passed = gathered([pass_on(total.astype(BF16), pairs, g) for g, total in enumerate(sums)])
        return passed

    def gathered(parts):
        out = [None] * tp
        for part in parts:
            for g, value in part.items():
                out[g] = value if out[g] is None else out[g] + value
        return [jnp.zeros((NS, inner), BF16) if value is None else value for value in out]

    pre, x, states, y, local = ([None] * tp for _ in range(5))

    first = []

    def run_project(g, *others):
        pre[g], x[g], local[g] = project(g, normed_ext, x_w[g], conv_x, bias_x, bc, wf, others)
        first.append(pass_on(local[g], forward, g))

    def run_scan(g, *others):
        y[g], states[g] = scan(g, x[g], bc, c2, cd, cdt, start[g], skip, others)

    cotangent, skip_gain, gate_gain = after((cotangent_late, skip_gain, gate_gain), bc)
    cotangent, skip_gain, gate_gain = to_own(cotangent), regroup(skip_gain[None]), regroup(gate_gain[None])
    skip = jnp.repeat(skip_gain, HEAD, axis=1)
    x_near, z_mine = after((x_near, z_mine), bc, cotangent)
    x_cut, x_far = send_far(x_near)
    z_mine = after(z_mine, *x_cut)
    z_own_other, z_near = swap(z_mine), send_own(z_mine)
    x_w = [[(x_mine, 0), (x_own_other, 0)]]
    run_project(0, *x_cut)
    x_rest = jnp.concatenate(after(x_near + x_far, x[0]), axis=0)
    x_w = places(x_mine, x_own_other, x_rest)
    run_project(1, x_w[1][1][0], skip, gate_gain, z_own_other)
    z_near = after(z_near, x[1], *first[0].values())
    z_cut, z_far = send_far(z_near)
    if tp > 2:
        run_project(2, x[1], out_mine, *z_cut)
    z_rest = jnp.concatenate(after(z_near + z_far, x[min(2, tp - 1)], *first[1].values()), axis=0)
    z_w = places(z_mine, z_own_other, z_rest)
    for g in range(3, tp):
        run_project(g, z_rest, x[g - 1])
    z = [product(normed, z_w[0], (x[tp - 1], *first[-2].values()))]
    start = chain(local, first, forward)
    out_mine = after(out_mine, *start)
    out_own_other, out_near = swap(out_mine), send_own(out_mine)
    run_scan(0, z[0])
    run_scan(1, y[0], out_own_other, z_w[1][1][0])
    out_near = after(out_near, y[1])
    out_cut, out_far = send_far(out_near)
    if tp > 2:
        run_scan(2, y[1], *out_cut)
    out_rest = jnp.concatenate(after(out_near + out_far, y[min(2, tp - 1)]), axis=0)
    out_w = places(out_mine, out_own_other, out_rest)
    for g in range(3, tp):
        run_scan(g, out_rest, y[g - 1])
    z += [product(normed, z_w[g], (y[tp - 1], out_w[1][1][0])) for g in range(1, tp)]

    scaled, dy, dz, local_pull, block_out, dn_z, gain_sums = gate(
        y, z, out_w, z_w, cotangent, hidden, gate_gain, bc, ei, flag, width
    )
    pulls = chain(local_pull, [pass_on(local_pull[g ^ 1], backward, g ^ 1) for g in reversed(groups)], backward)
    out_grad, z_grad, x_grad = Scatter(cotangent, 1), Scatter(normed, 2), Scatter(normed_ext, 1)
    dpre, dbc, sums, q, da = ([None] * tp for _ in range(5))
    last = tp - 1
    order = list(reversed(groups))
    swapped = [out_grad.swap(last, scaled[last]), z_grad.swap(last, dz[last])]
    far_out = out_grad.send(last, after(scaled[last], *swapped))
    ready = [out_grad.swap(g, after(scaled[g], far_out)) for g in order[1:]]
    far_z = z_grad.send(last, after(dz[last], *ready, *pulls))
    waiting = ready + [far_out, far_z] + pulls
    finished = []
    for at, g in enumerate(order):
        dpre[g], dbc[g], sums[g], q[g], da[g] = back(
            g, pre[g], dy[g], bc, c2, cd, c2t, states[g], pulls[g], skip, conv_x, bias_x, waiting
        )
        arrivals = [dpre[g]] + coming + finished
        coming.clear()
        waiting = []
        now = lambda value: after(value, *arrivals, *waiting)
        if at == 0:
            waiting += [out_grad.send(i, now(scaled[i])) for i in order[1:-1]]
        if at == 1:
            waiting.append(x_grad.send(order[0], now(dpre[order[0]])))
        if at == last - 1 and at > 0:
            waiting += [x_grad.send(i, now(dpre[i])) for i in order[1:-2]]
        if at < last:
            waiting.append(x_grad.swap(g, now(dpre[g])))
        if at == 0:
            waiting += [z_grad.swap(i, now(dz[i])) for i in order[1:]]
            waiting += [z_grad.send(i, now(dz[i])) for i in order[1:-1]]
            del coming[-len(order[1:-1]) :]
        if at == last - 1 and at > 0:
            waiting.append(x_grad.send(g, now(dpre[g])))
        if at == 1:
            total = out_grad.finish(now(scaled[0]))
            waiting.append(total)
            grad_out = scatter(total)
            finished = [grad_out]
        if at == min(2, last):
            total = z_grad.finish(now(dz[0]))
            waiting.append(total)
            grad_z = scatter(total)
            finished = [grad_z]
    x_grad.swap(0, now(dpre[0]))
    total = x_grad.finish(now(dpre[0]))
    grad_x = scatter(total)
    q, da, sums = after((q, da, sums), total)
    dbc_all = after(functools.reduce(jnp.add, dbc), total)
    dpre_m, sums_m = map_back(pre_m, dbc_all, conv_m, bias_m)

    v = v.reshape(H, rows)
    q, da = (jnp.concatenate(a, axis=0).reshape(H, rows) for a in (q, da))
    delta, sig = jax.nn.softplus(v), jax.nn.sigmoid(v)
    rate = -jnp.exp(decay_log).reshape(H, 1)
    ratio = jnp.where(v < -15.0, 1.0, sig / jnp.maximum(delta, 1e-30))
    dstep = q * ratio + da * rate * sig
    dstep_low = dstep.astype(BF16)
    dstep_t = jnp.pad(dstep_low.reshape(tp, heads, rows), ((0, 0), (0, pitch - heads), (0, 0))).reshape(tp * pitch, rows)
    dstep_t = jnp.pad(dstep_t, ((0, LANES - tp * pitch), (0, 0)))
    dstep_rows = dstep_t.T

    place_order = (core_now + z_now[None, None] * tp + groups_now[None, :, None]).reshape(-1)
    group_order = (core_now + z_now[None, None] * tp + jnp.arange(tp)[None, :, None]).reshape(-1)
    grad_map = dot(normed_ext, dpre_m, TN).reshape(2 * zn * tp, map_rows, 2 * NS)
    grad_map = pick(strip(grad_map), place_order, 0)
    grad_step = dot(dstep_t[: tp * pitch], normed).reshape(tp, pitch, 2, zn, width)[:, :heads]
    grad_step = strip(pad_step(jnp.transpose(grad_step, (2, 3, 0, 1, 4)).reshape(-1, heads, width)))
    grad_small = jnp.concatenate([grad_map, pick(grad_step, group_order, 0)], axis=-2)
    def to_owners(parts, axis, count):
        parts = parts.reshape((count, -1) + parts.shape[1:])
        total = parts[0]
        for gap in range(1, count):
            total = total + across(parts[gap], axis, count, gap)
        return total

    grad_small = to_owners(grad_small, "core", 2)
    halo = jnp.zeros((HALO, DI + 2 * NS), BF16)
    edge = jnp.concatenate([a[:HALO] for a in dpre + [dpre_m]], axis=1)
    for gap in sorted({i ^ j for i, j in backward}):
        part = lax.ppermute(edge, "tensor", [(i, j) for i, j in backward if i ^ j == gap])
        halo = halo + jnp.concatenate([part[:, span_of(g ^ gap)] for g in groups] + [part[:, DI:]], axis=1)
    grad_hidden, norm_sums = final(
        dpre, x_w, dpre_m, map_w, dstep_rows, step_w, halo, dn_z, hidden, cotangent, norm_gain[None], flag, width, (grad_x,)
    )
    grad_small = to_owners(to_owners(after(grad_small, norm_sums), "tensor", tp), "z", zn)[0]
    map_shard = jnp.concatenate([grad_small[:map_rows], grad_small[map_rows : 2 * map_rows]], axis=1)
    step_shard = grad_small[2 * map_rows :].reshape(strips, pitch, LANES)
    step_shard = jnp.concatenate([step_shard[i] for i in range(strips)], axis=1)[:heads, :width].T

    fold8 = lambda a: a.reshape(-1, 8, a.shape[-1]).sum(1)
    sums = jnp.concatenate([fold8(part) for part in sums], axis=1)
    taps = jnp.concatenate([regroup(sums[:5]), fold8(sums_m)], axis=1)
    per_head = jnp.stack(
        [
            jnp.sum(dstep, axis=1),
            jnp.sum(da * delta, axis=1) * rate[:, 0],
            jnp.sum(sums[5].reshape(H, HEAD), axis=1),
        ]
    )
    vector = [taps.reshape(-1), regroup(per_head).reshape(-1), regroup(fold8(gain_sums))[0]]
    vector = everywhere(jnp.concatenate(vector + [from_own(jnp.sum(norm_sums, axis=0))]))
    wide = DI + 2 * NS
    cuts = [KW * wide, wide, H, H, H, DI, D]
    parts, at = [], 0
    for count in cuts:
        parts.append(vector[at : at + count])
        at += count
    return (
        block_out,
        grad_hidden,
        parts[6],
        jnp.stack([grad_z, grad_x], axis=1).astype(F32),
        step_shard,
        map_shard,
        parts[0].reshape(KW, wide),
        parts[1],
        parts[2],
        parts[3],
        parts[4],
        parts[5],
        grad_out.astype(F32),
    )


def solution(mesh):
    dp, tp = mesh.shape["dp"], mesh.shape["tensor"]
    inner = Mesh(mesh.devices.reshape(dp // 2, 2, tp), ("z", "core", "tensor"))
    rows = P(("z", "core", "tensor"), None)
    split_dp = ("z", "core")
    head, step, out = P(split_dp, None, "tensor"), P(split_dp, "tensor"), P(split_dp, "tensor")
    whole = P()
    return jax.shard_map(
        functools.partial(shards, dp // 2, tp),
        mesh=inner,
        in_specs=(rows, whole, head, step, rows, whole, whole, whole, whole, whole, whole, out, rows),
        out_specs=(rows, rows, whole, head, step, rows, whole, whole, whole, whole, whole, whole, out),
        check_vma=False,
    )
```
